32 devices in a mesh: expert: 8 (over z, x), fsdp: 4 (over y, core).
Axes of the slice: x: 2, y: 2, z: 4, core: 2. Of those that a mesh axis runs over, the one named last changes fastest.
Arguments:
- tokens: bfloat16 [16384, 1536], P(('expert', 'fsdp')), may hold values from -6 to 6
- cotangent: bfloat16 [16384, 1536], P(('expert', 'fsdp')), may hold values from -6 to 6
- routes: int32 [16384, 4], P(('expert', 'fsdp')), may hold values from 0 to 31, all different within a row; in each aligned block of 512 rows (0 to 511, 512 to 1023, ...) at most 80 rows name the same one
- gains: float32 [2, 1536], P(None, 'fsdp'), may hold values from 0.5 to 1.5
- gains_first: float32 [2, 1536], P(None, 'fsdp'), may hold values from -120.75685 to 120.75685
- gains_second: float32 [2, 1536], P(None, 'fsdp'), may hold values from 1032.192 to 31132.297
- query_weight: float32 [1536, 1536], P('fsdp'), may hold values from -0.21875 to 0.21875
- query_first: float32 [1536, 1536], P('fsdp'), may hold values from -320 to 320
- query_second: float32 [1536, 1536], P('fsdp'), may hold values from 13762.56 to 55050.24
- key_matrix: float32 [1536, 256], P('fsdp'), may hold values from -0.21875 to 0.21875
- key_moment_first: float32 [1536, 256], P('fsdp'), may hold values from -768 to 768
- key_moment_second: float32 [1536, 256], P('fsdp'), may hold values from 69795.84 to 278528
- value_matrix: float32 [1536, 256], P('fsdp'), may hold values from -0.15625 to 0.15625
- value_moment_first: float32 [1536, 256], P('fsdp'), may hold values from -160 to 160
- value_moment_second: float32 [1536, 256], P('fsdp'), may hold values from 1727.3403 to 6904.34
- output_weight: float32 [1536, 1536], P('fsdp'), may hold values from -0.875 to 0.875
- output_first: float32 [1536, 1536], P('fsdp'), may hold values from -20 to 20
- output_second: float32 [1536, 1536], P('fsdp'), may hold values from 54.0672 to 212.992
- router_weight: float32 [1536, 32], P('fsdp'), may hold values from -0.078125 to 0.078125
- router_first: float32 [1536, 32], P('fsdp'), may hold values from -512 to 512
- router_second: float32 [1536, 32], P('fsdp'), may hold values from 31129.6 to 124518.4
- expert_in: float32 [32, 1536, 1536], P('expert', 'fsdp'), may hold values from -0.15625 to 0.15625
- in_first: float32 [32, 1536, 1536], P('expert', 'fsdp'), may hold values from -16 to 16
- in_second: float32 [32, 1536, 1536], P('expert', 'fsdp'), may hold values from 26.624 to 108.544
- expert_out: float32 [32, 768, 1536], P('expert', None, 'fsdp'), may hold values from -0.625 to 0.625
- out_first: float32 [32, 768, 1536], P('expert', None, 'fsdp'), may hold values from -4 to 4
- out_second: float32 [32, 768, 1536], P('expert', None, 'fsdp'), may hold values from 2.4576 to 9.6256
Outputs:
- layer_out: bfloat16 [16384, 1536], P(('expert', 'fsdp'))
- input_grad: bfloat16 [16384, 1536], P(('expert', 'fsdp'))
- gains_new: float32 [2, 1536], P(None, 'fsdp')
- gains_first_new: float32 [2, 1536], P(None, 'fsdp')
- gains_second_new: float32 [2, 1536], P(None, 'fsdp')
- query_new: float32 [1536, 1536], P('fsdp')
- query_first_new: float32 [1536, 1536], P('fsdp')
- query_second_new: float32 [1536, 1536], P('fsdp')
- key_new: float32 [1536, 256], P('fsdp')
- key_first_new: float32 [1536, 256], P('fsdp')
- key_second_new: float32 [1536, 256], P('fsdp')
- value_new: float32 [1536, 256], P('fsdp')
- value_first_new: float32 [1536, 256], P('fsdp')
- value_second_new: float32 [1536, 256], P('fsdp')
- output_new: float32 [1536, 1536], P('fsdp')
- output_first_new: float32 [1536, 1536], P('fsdp')
- output_second_new: float32 [1536, 1536], P('fsdp')
- router_new: float32 [1536, 32], P('fsdp')
- router_first_new: float32 [1536, 32], P('fsdp')
- router_second_new: float32 [1536, 32], P('fsdp')
- expert_in_new: float32 [32, 1536, 1536], P('expert', 'fsdp')
- in_first_new: float32 [32, 1536, 1536], P('expert', 'fsdp')
- in_second_new: float32 [32, 1536, 1536], P('expert', 'fsdp')
- expert_out_new: float32 [32, 768, 1536], P('expert', None, 'fsdp')
- out_first_new: float32 [32, 768, 1536], P('expert', None, 'fsdp')
- out_second_new: float32 [32, 768, 1536], P('expert', None, 'fsdp')
The draws below stay inside these ranges and needn't reach their ends.
Inputs may be any that keep to these rules, and one draw needn't show every extreme that they name: `routes`: within the rows of one device no expert is named more than 80 times, a bound that some block reaches.
All inputs are finite; a program needn't handle non-finite values.
Results may differ from the reference program's by a relative error of at most 0.028.
Values may be sent and summed in bfloat16 or wider, within the bound.
No kernel may reach another device: no remote copies, remote signals or barrier semaphores. Data moves between devices by JAX's collectives and lax.ppermute only.
A program may use at most 320 MiB of HBM per device.

```python
import math
import jax
import jax.numpy as jnp
import numpy as np
from jax import lax

MODEL_WIDTH = 1536
QUERY_HEADS = 12
KEY_VALUE_HEADS = 2
HEAD_SIZE = 128
EXPERTS = 32
FF = 768
TOPK = 4
TOK_DEV = 512
STEP = 10
CAP = 80
SEQUENCE_TOKENS = 2048
TOTAL_TOKENS = 16384


def draw_gains_first(key, part):
    key = jax.random.fold_in(key, 11)
    front_scale = 12.0 * (TOTAL_TOKENS * SEQUENCE_TOKENS ** (-0.85)) ** 0.5
    back_scale = 0.122 * TOTAL_TOKENS ** 0.5
    row_scale = jnp.stack([jnp.float32(front_scale), jnp.float32(back_scale)])[:, None]
    return jax.random.uniform(key, (2, MODEL_WIDTH), jnp.float32, -2.0, 2.0) * row_scale


def draw_gains_second(key, part):
    key = jax.random.fold_in(key, 12)
    front_scale = 309.0 * TOTAL_TOKENS * SEQUENCE_TOKENS ** (-0.85)
    back_scale = 0.0636 * TOTAL_TOKENS
    row_scale = jnp.stack([jnp.float32(front_scale), jnp.float32(back_scale)])[:, None]
    return jnp.exp(jax.random.uniform(key, (2, MODEL_WIDTH), jnp.float32, 0.0, math.log(4.0))) * row_scale


def block_levels(rng, shape, pieces, low, largest):
    level = 1.0
    for position, blocks in pieces:
        draws = jax.random.uniform(jax.random.fold_in(jax.random.fold_in(rng, 6), position), (blocks,), jnp.float32, low / len(pieces), largest / len(pieces))
        level = level * jnp.repeat(jnp.exp(draws), shape[position] // blocks).reshape((-1,) + (1,) * (len(shape) - 1 - position))
    return level


def routed_block(stream_key, own, number, rows, count, top, bound, lean):
    sequence = jax.random.permutation(stream_key, count)
    crowded, ordinary = portions_of(count, rows * top, bound, lean, True), portions_of(count, rows * top, bound, lean, False)
    places = jnp.arange(count)

    def named(sizes, turn):
        used = int((sizes > 0).sum())
        fixed = max(1, used // 4)
        passed = fixed + (places - fixed + turn * (used - fixed)) % max(1, count - fixed)
        return jnp.zeros((count,), jnp.int32).at[sequence[jnp.where(places < fixed, places, passed)]].set(jnp.asarray(sizes, jnp.int32))

    sizes = jnp.where(number % 4 == 0, named(crowded, number // 4), named(ordinary, number - number // 4 - 1))
    mixed = jax.random.permutation(jax.random.fold_in(own, 3), count)
    source_of, sink = mixed[0:count // 2 * 2:2], mixed[1:count // 2 * 2:2]
    slack = jnp.minimum(sizes[source_of] - 1, bound - sizes[sink]) // 2
    slack = jnp.where((source_of == sequence[0]) | (sink == sequence[0]) | (sizes[sink] == 0), 0, jnp.maximum(slack, 0))
    passed = jax.random.randint(jax.random.fold_in(own, 4), (count // 2,), 0, 1 << 20) % (slack + 1)
    sizes = sizes.at[source_of].add(-passed).at[sink].add(passed)
    labels = jnp.searchsorted(jnp.cumsum(sizes), jnp.arange(rows * top), side="right").astype(jnp.int32)
    listing = labels.reshape(top, rows).T
    listing = listing[jax.random.permutation(jax.random.fold_in(own, 1), rows)]
    turn = jax.random.randint(jax.random.fold_in(own, 2), (rows, 1), 0, top)
    return jnp.take_along_axis(listing, (jnp.arange(top)[None, :] + turn) % top, axis=1)


def portions_of(count, total, reach, skew, full):
    portions = [(1 << 20) // math.isqrt(standing ** skew) + 1 for standing in range(1, count + 1)]
    largest = reach if full else min(reach, max(-(-total // count), total * portions[0] // sum(portions)))
    least = 1 if total - largest >= count - 1 else 0
    given, rest = [largest] + [least] * (count - 1), total - largest - least * (count - 1)
    while rest > 0:
        free = [i for i in range(1, count) if given[i] < largest] or [i for i in range(1, count) if given[i] < reach]
        pool, remaining = sum([portions[i] for i in free]), rest
        for i in free:
            addition = min(reach - given[i], max(1, remaining * portions[i] // pool), rest)
            given[i] = given[i] + addition
            rest = rest - addition
    return np.array(given)


def scatter_about(stream_key, shape, spread, reach, shards=(), kind=jnp.bfloat16):
    drawn = spread * jax.random.normal(stream_key, shape, jnp.float32)
    if shards:
        drawn = drawn * block_levels(stream_key, shape, shards, -0.22, 0.18)
    return jnp.clip(drawn, -reach, reach).astype(kind)


def setup_inputs(seed: int = 0) -> dict:
    keys = jax.random.split(jax.random.key(seed), 28)
    tokens = scatter_about(keys[0], (TOTAL_TOKENS, MODEL_WIDTH), 1.0, 6.0, ((0, 32),))
    cotangent = scatter_about(keys[1], (TOTAL_TOKENS, MODEL_WIDTH), 1.0, 6.0, ((0, 32),))
    routes_keys = jax.random.split(jax.random.fold_in(keys[2], 1), TOTAL_TOKENS // TOK_DEV)
    routes_turns = jax.random.permutation(jax.random.fold_in(keys[2], 3), TOTAL_TOKENS // TOK_DEV)
    routes = jax.vmap(lambda own, number: routed_block(jax.random.fold_in(keys[2], 2), own, number, TOK_DEV, EXPERTS, TOPK, CAP, 1))(routes_keys, routes_turns).reshape((TOTAL_TOKENS, TOPK))
    gains = jnp.clip(1.0 + 0.1 * jax.random.normal(keys[3], (2, MODEL_WIDTH), jnp.float32), 0.5, 1.5)
    gains_first = draw_gains_first(jax.random.fold_in(keys[27], 71), 0)
    gains_second = draw_gains_second(jax.random.fold_in(keys[27], 71), 0)
    query_weight = scatter_about(keys[6], (MODEL_WIDTH, QUERY_HEADS * HEAD_SIZE), (MODEL_WIDTH // 2) ** -0.5, 0.21875, ((0, 4),), jnp.float32)
    query_first = scatter_about(keys[7], (MODEL_WIDTH, QUERY_HEADS * HEAD_SIZE), (0.444 * TOTAL_TOKENS ** 0.5), 320.0, ((0, 4),), jnp.float32)
    query_second = jnp.clip(jnp.exp(math.log(55050.24) - 1.3862944 * jax.random.uniform(keys[8], (MODEL_WIDTH, QUERY_HEADS * HEAD_SIZE), jnp.float32) ** block_levels(keys[8], (MODEL_WIDTH, QUERY_HEADS * HEAD_SIZE), ((0, 4),), -0.2, 0.2)), 13762.56, 55050.24)
    key_matrix = scatter_about(keys[9], (MODEL_WIDTH, KEY_VALUE_HEADS * HEAD_SIZE), (MODEL_WIDTH // 2) ** -0.5, 0.21875, ((0, 4),), jnp.float32)
    key_moment_first = scatter_about(keys[10], (MODEL_WIDTH, KEY_VALUE_HEADS * HEAD_SIZE), (1.0 * TOTAL_TOKENS ** 0.5), 768.0, ((0, 4),), jnp.float32)
    key_moment_second = jnp.clip(jnp.exp(math.log(278528.0) - 1.3839441 * jax.random.uniform(keys[11], (MODEL_WIDTH, KEY_VALUE_HEADS * HEAD_SIZE), jnp.float32) ** block_levels(keys[11], (MODEL_WIDTH, KEY_VALUE_HEADS * HEAD_SIZE), ((0, 4),), -0.2, 0.2)), 69795.84, 278528.0)
    value_matrix = scatter_about(keys[12], (MODEL_WIDTH, KEY_VALUE_HEADS * HEAD_SIZE), MODEL_WIDTH ** -0.5, 0.15625, ((0, 4),), jnp.float32)
    value_moment_first = scatter_about(keys[13], (MODEL_WIDTH, KEY_VALUE_HEADS * HEAD_SIZE), (5.68 * (QUERY_HEADS * HEAD_SIZE * TOTAL_TOKENS * SEQUENCE_TOKENS ** -0.85 * MODEL_WIDTH ** -1.0) ** 0.5), 160.0, ((0, 4),), jnp.float32)
    value_moment_second = jnp.clip(jnp.exp(math.log(6904.34) - 1.3855673 * jax.random.uniform(keys[14], (MODEL_WIDTH, KEY_VALUE_HEADS * HEAD_SIZE), jnp.float32) ** block_levels(keys[14], (MODEL_WIDTH, KEY_VALUE_HEADS * HEAD_SIZE), ((0, 4),), -0.2, 0.2)), 1727.3403, 6904.34)
    output_weight = scatter_about(keys[15], (QUERY_HEADS * HEAD_SIZE, MODEL_WIDTH), (MODEL_WIDTH // 32) ** -0.5, 0.875, ((0, 4),), jnp.float32)
    output_first = scatter_about(keys[16], (QUERY_HEADS * HEAD_SIZE, MODEL_WIDTH), (0.028 * TOTAL_TOKENS ** 0.5), 20.0, ((0, 4),), jnp.float32)
    output_second = jnp.clip(jnp.exp(math.log(212.992) - 1.3710269 * jax.random.uniform(keys[17], (QUERY_HEADS * HEAD_SIZE, MODEL_WIDTH), jnp.float32) ** block_levels(keys[17], (QUERY_HEADS * HEAD_SIZE, MODEL_WIDTH), ((0, 4),), -0.2, 0.2)), 54.0672, 212.992)
    router_weight = scatter_about(keys[18], (MODEL_WIDTH, EXPERTS), (4 * MODEL_WIDTH) ** -0.5, 0.078125, ((0, 4),), jnp.float32)
    router_first = scatter_about(keys[19], (MODEL_WIDTH, EXPERTS), (1.9 * (TOTAL_TOKENS * TOPK // EXPERTS) ** 0.5), 512.0, ((0, 4),), jnp.float32)
    router_second = jnp.clip(jnp.exp(math.log(124518.4) - 1.3862944 * jax.random.uniform(keys[20], (MODEL_WIDTH, EXPERTS), jnp.float32) ** block_levels(keys[20], (MODEL_WIDTH, EXPERTS), ((0, 4),), -0.2, 0.2)), 31129.6, 124518.4)
    expert_in = scatter_about(keys[21], (EXPERTS, MODEL_WIDTH, 2 * FF), MODEL_WIDTH ** -0.5, 0.15625, ((0, 8), (1, 4)), jnp.float32)
    in_first = scatter_about(keys[22], (EXPERTS, MODEL_WIDTH, 2 * FF), (0.056 * (TOTAL_TOKENS * TOPK // EXPERTS) ** 0.5), 16.0, ((0, 8), (1, 4)), jnp.float32)
    in_second = jnp.clip(jnp.exp(math.log(108.544) - 1.40534252 * jax.random.uniform(keys[23], (EXPERTS, MODEL_WIDTH, 2 * FF), jnp.float32) ** block_levels(keys[23], (EXPERTS, MODEL_WIDTH, 2 * FF), ((0, 8), (1, 4)), -0.2, 0.2)), 26.624, 108.544)
    expert_out = scatter_about(keys[24], (EXPERTS, FF, MODEL_WIDTH), (FF // 8) ** -0.5, 0.625, ((0, 8), (2, 4)), jnp.float32)
    out_first = scatter_about(keys[25], (EXPERTS, FF, MODEL_WIDTH), (0.0167 * (TOTAL_TOKENS * TOPK // EXPERTS) ** 0.5), 4.0, ((0, 8), (2, 4)), jnp.float32)
    out_second = jnp.clip(jnp.exp(math.log(9.6256) - 1.3652409 * jax.random.uniform(keys[26], (EXPERTS, FF, MODEL_WIDTH), jnp.float32) ** block_levels(keys[26], (EXPERTS, FF, MODEL_WIDTH), ((0, 8), (2, 4)), -0.2, 0.2)), 2.4576, 9.6256)
    return dict(tokens=tokens, cotangent=cotangent, routes=routes, gains=gains, gains_first=gains_first, gains_second=gains_second, query_weight=query_weight, query_first=query_first, query_second=query_second, key_matrix=key_matrix, key_moment_first=key_moment_first, key_moment_second=key_moment_second, value_matrix=value_matrix, value_moment_first=value_moment_first, value_moment_second=value_moment_second, output_weight=output_weight, output_first=output_first, output_second=output_second, router_weight=router_weight, router_first=router_first, router_second=router_second, expert_in=expert_in, in_first=in_first, in_second=in_second, expert_out=expert_out, out_first=out_first, out_second=out_second)


NORM_EPS = 1e-05
ROPE_BASE = 10000.0
BETA_ONE = 0.9
BETA_TWO = 0.95
ADAM_EPS = 1e-08
DECAY = 0.1
GAIN_RATE = 0.8
MASKED = -1e+30

@jax.custom_vjp
def reduced_precision(v):
    return lax.optimization_barrier(v.astype(jnp.bfloat16)).astype(jnp.float32)

@jax.custom_vjp
def low_back(v):
    return v

def low_keep(v):
    return (reduced_precision(v), None)

def low_pass(kept, grad):
    return (grad,)

def back_keep(v):
    return (v, None)

def back_low(kept, grad):
    return (reduced_precision(grad),)
reduced_precision.defvjp(low_keep, low_pass)
low_back.defvjp(back_keep, back_low)

def project(left, right):
    return jnp.dot(left, right, precision=lax.Precision.HIGHEST, preferred_element_type=jnp.float32)

def rotary_apply(values, token_positions, heads, sign):
    row_count = values.shape[0]
    head_width = values.shape[1] // heads
    half_width = head_width // 2
    shaped = values.reshape(row_count, heads, head_width)
    inverse = ROPE_BASE ** (-(jnp.arange(half_width, dtype=jnp.float32) * 2.0 / head_width))
    angle_grid = token_positions[:, None] * inverse[None, :]
    cosine = jnp.cos(angle_grid)[:, None, :]
    sine_part = sign * jnp.sin(angle_grid)[:, None, :]
    front_half = shaped[..., :half_width]
    back_half = shaped[..., half_width:]
    turned = jnp.concatenate([front_half * cosine - back_half * sine_part, back_half * cosine + front_half * sine_part], axis=-1)
    return turned.reshape(row_count, heads * head_width)

def norm_rows(values, gain):
    scale_rows = lax.rsqrt(lax.optimization_barrier(jnp.mean(values * values, axis=1, keepdims=True)) + NORM_EPS)
    return values * scale_rows * gain

def slot_positions(block_routes):
    flat_routes = block_routes.reshape(-1)
    onehot = (flat_routes[:, None] == jnp.arange(EXPERTS, dtype=jnp.int32)[None, :]).astype(jnp.int32)
    before = jnp.cumsum(onehot, axis=0) - onehot
    slot_index = lax.optimization_barrier(jnp.sum(before * onehot, axis=1))
    return flat_routes * CAP + slot_index

def attend_one_sequence(parts):
    query_rows, sequence_keys, sequence_values = parts
    sequence_length = query_rows.shape[0]
    block_row_count = min(512, sequence_length)
    grouped_queries = query_rows.reshape(sequence_length // block_row_count, block_row_count, KEY_VALUE_HEADS, QUERY_HEADS // KEY_VALUE_HEADS, HEAD_SIZE)
    key_head_rows = sequence_keys.reshape(sequence_length, KEY_VALUE_HEADS, HEAD_SIZE)
    value_head_rows = sequence_values.reshape(sequence_length, KEY_VALUE_HEADS, HEAD_SIZE)
    starts = jnp.arange(sequence_length // block_row_count, dtype=jnp.int32) * block_row_count
    score_scaling = 1.0 / math.sqrt(HEAD_SIZE)

    def one_block(block_parts):
        query_block, block_start = block_parts
        scores = low_back(jnp.einsum('tkgd,skd->kgts', query_block, key_head_rows, precision=lax.Precision.HIGHEST) * score_scaling)
        allowed = jnp.arange(sequence_length, dtype=jnp.int32)[None, :] <= (block_start + jnp.arange(block_row_count, dtype=jnp.int32))[:, None]
        scores = jnp.where(allowed, scores, MASKED)
        current_weights = reduced_precision(jax.nn.softmax(scores, axis=-1))
        return jnp.einsum('kgts,skd->tkgd', current_weights, value_head_rows, precision=lax.Precision.HIGHEST)
    outputs = lax.map(jax.checkpoint(one_block), (grouped_queries, starts))
    return outputs.reshape(sequence_length, QUERY_HEADS * HEAD_SIZE)

def expert_apply(parts):
    rows, gate_up_w, down_w = parts
    gate_up = low_back(project(rows, gate_up_w))
    expert_hidden = reduced_precision(jax.nn.silu(gate_up[:, :FF]) * gate_up[:, FF:])
    return reduced_precision(low_back(project(expert_hidden, down_w)))

def adamw_update(weight, moment_one, moment_two, gradient, step_rate, decay_rate):
    first_new = BETA_ONE * moment_one + (1.0 - BETA_ONE) * gradient
    second_new = BETA_TWO * moment_two + (1.0 - BETA_TWO) * gradient * gradient
    first_hat = first_new / (1.0 - BETA_ONE ** STEP)
    second_hat = second_new / (1.0 - BETA_TWO ** STEP)
    weight_new = weight - step_rate * (first_hat / (jnp.sqrt(second_hat) + ADAM_EPS) + decay_rate * weight)
    return (weight_new, first_new, second_new)

def reference(tokens, cotangent, routes, gains, gains_first, gains_second, query_weight, query_first, query_second, key_matrix, key_moment_first, key_moment_second, value_matrix, value_moment_first, value_moment_second, output_weight, output_first, output_second, router_weight, router_first, router_second, expert_in, in_first, in_second, expert_out, out_first, out_second):
    blocks = TOTAL_TOKENS // TOK_DEV
    span = blocks * CAP
    local_pos = jax.vmap(slot_positions)(routes.reshape(blocks, TOK_DEV, TOPK))
    global_pos = (local_pos // CAP * span + jnp.arange(blocks, dtype=jnp.int32)[:, None] * CAP + local_pos % CAP).reshape(-1)
    source = jnp.full((EXPERTS * span,), TOTAL_TOKENS * TOPK, jnp.int32).at[global_pos].set(jnp.arange(TOTAL_TOKENS * TOPK, dtype=jnp.int32))
    source_rows = source // TOPK
    token_positions = jnp.tile(jnp.arange(SEQUENCE_TOKENS, dtype=jnp.float32), TOTAL_TOKENS // SEQUENCE_TOKENS)
    sequence_count = TOTAL_TOKENS // SEQUENCE_TOKENS

    def forward(inputs, gain_pair, query_w, key_w, value_w, output_w, router_w, gate_up_w, down_w):
        gain_low = reduced_precision(gain_pair)
        first_hidden = reduced_precision(norm_rows(inputs, gain_low[0]))
        query_pre = low_back(project(first_hidden, reduced_precision(query_w)))
        key_before_rotation = low_back(project(first_hidden, reduced_precision(key_w)))
        value_pre = low_back(project(first_hidden, reduced_precision(value_w)))
        query_rows = reduced_precision(rotary_apply(query_pre, token_positions, QUERY_HEADS, 1.0))
        every_key = reduced_precision(rotary_apply(key_before_rotation, token_positions, KEY_VALUE_HEADS, 1.0))
        every_value = reduced_precision(value_pre)
        attended_rows = lax.map(attend_one_sequence, (query_rows.reshape(sequence_count, SEQUENCE_TOKENS, QUERY_HEADS * HEAD_SIZE), every_key.reshape(sequence_count, SEQUENCE_TOKENS, KEY_VALUE_HEADS * HEAD_SIZE), every_value.reshape(sequence_count, SEQUENCE_TOKENS, KEY_VALUE_HEADS * HEAD_SIZE)))
        attended_rows = reduced_precision(low_back(attended_rows.reshape(TOTAL_TOKENS, QUERY_HEADS * HEAD_SIZE)))
        residual = inputs + low_back(project(attended_rows, reduced_precision(output_w)))
        hidden_two = reduced_precision(norm_rows(residual, gain_low[1]))
        logits = low_back(project(hidden_two, reduced_precision(router_w)))
        gate_weights = jax.nn.softmax(jnp.take_along_axis(logits, routes, axis=1), axis=1)
        padded = jnp.concatenate([hidden_two, jnp.zeros((1, MODEL_WIDTH), jnp.float32)], axis=0)
        rows_all = low_back(padded[source_rows]).reshape(EXPERTS, span, MODEL_WIDTH)
        results = lax.map(jax.checkpoint(expert_apply), (rows_all, reduced_precision(gate_up_w), reduced_precision(down_w)))
        picked = results.reshape(EXPERTS * span, MODEL_WIDTH)[global_pos].reshape(TOTAL_TOKENS, TOPK, MODEL_WIDTH)
        return residual + lax.optimization_barrier(jnp.sum(gate_weights[:, :, None] * picked, axis=1))
    inputs = tokens.astype(jnp.float32)
    layer_value, pullback = jax.vjp(forward, inputs, gains, query_weight, key_matrix, value_matrix, output_weight, router_weight, expert_in, expert_out)
    grads = pullback(cotangent.astype(jnp.float32))
    gains_new, gains_first_new, gains_second_new = adamw_update(gains, gains_first, gains_second, grads[1], GAIN_RATE, 0.0)
    query_new, query_first_new, query_second_new = adamw_update(query_weight, query_first, query_second, grads[2], 0.5 / math.sqrt(MODEL_WIDTH // 2), DECAY)
    key_new, key_first_new, key_second_new = adamw_update(key_matrix, key_moment_first, key_moment_second, grads[3], 0.5 / math.sqrt(MODEL_WIDTH // 2), DECAY)
    value_new, value_first_new, value_second_new = adamw_update(value_matrix, value_moment_first, value_moment_second, grads[4], 0.5 / math.sqrt(MODEL_WIDTH), DECAY)
    output_new, output_first_new, output_second_new = adamw_update(output_weight, output_first, output_second, grads[5], 0.5 / math.sqrt(MODEL_WIDTH // 32), DECAY)
    router_new, router_first_new, router_second_new = adamw_update(router_weight, router_first, router_second, grads[6], 0.5 / math.sqrt(4 * MODEL_WIDTH), DECAY)
    expert_in_new, in_first_new, in_second_new = adamw_update(expert_in, in_first, in_second, grads[7], 0.5 / math.sqrt(MODEL_WIDTH), DECAY)
    expert_out_new, out_first_new, out_second_new = adamw_update(expert_out, out_first, out_second, grads[8], 0.5 / math.sqrt(FF // 8), DECAY)
    return (layer_value.astype(jnp.bfloat16), grads[0].astype(jnp.bfloat16), gains_new, gains_first_new, gains_second_new, query_new, query_first_new, query_second_new, key_new, key_first_new, key_second_new, value_new, value_first_new, value_second_new, output_new, output_first_new, output_second_new, router_new, router_first_new, router_second_new, expert_in_new, in_first_new, in_second_new, expert_out_new, out_first_new, out_second_new)
```

```python
import math

import jax
import jax.numpy as jnp
from jax import lax
from jax.experimental import pallas as pl
from jax.experimental.pallas import tpu as pltpu
from jax.sharding import PartitionSpec as P

MODEL_WIDTH = 1536
QUERY_HEADS = 12
KEY_VALUE_HEADS = 2
HEAD_SIZE = 128
GROUP = QUERY_HEADS // KEY_VALUE_HEADS
FF = 768
STEP = 10
CAP = 80
DEPTH = 4
HALF = MODEL_WIDTH // 2
KV = KEY_VALUE_HEADS * HEAD_SIZE
QKV = MODEL_WIDTH + 2 * KV


NORM_EPS = 1e-05
ROPE_BASE = 10000.0
BETA_ONE = 0.9
BETA_TWO = 0.95
ADAM_EPS = 1e-08
DECAY = 0.1
GAIN_RATE = 0.8
MASKED = -1e30
LOG2E = 1.0 / math.log(2.0)
SCORE_SCALE = 1.0 / math.sqrt(HEAD_SIZE)

f32 = jnp.float32
bf16 = jnp.bfloat16


def dot_nn(left, right):
    return lax.dot_general(left, right, (((1,), (0,)), ((), ())), preferred_element_type=f32)


def dot_nt(left, right):
    return lax.dot_general(left, right, (((1,), (1,)), ((), ())), preferred_element_type=f32)


def dot_tn(left, right):
    return lax.dot_general(left, right, (((0,), (0,)), ((), ())), preferred_element_type=f32)


def params(megabytes, axes):
    return pltpu.CompilerParams(
        vmem_limit_bytes=megabytes * 1024 * 1024, dimension_semantics=("arbitrary",) * axes
    )


def cost(flops, nbytes, trans=0):
    return pl.CostEstimate(flops=int(flops), bytes_accessed=int(nbytes), transcendentals=int(trans))


def causal(score_t):
    key_place = lax.broadcasted_iota(jnp.int32, score_t.shape, 0)
    query_place = lax.broadcasted_iota(jnp.int32, score_t.shape, 1)
    return key_place <= query_place


def attend_kernel(place, pre, cosine, sine, keys, values, out, log_total, turned):
    rows = pre[...]
    query = rows * cosine[...] + pltpu.roll(rows, HEAD_SIZE // 2, 1) * sine[...]
    turned[...] = query.astype(bf16)
    query_t = query.T.astype(bf16)
    factor = SCORE_SCALE * LOG2E

    score = dot_nn(keys[0], query_t) * factor
    score = jnp.where(causal(score), score, MASKED)
    biggest = jnp.max(score, axis=0, keepdims=True)
    weight = jnp.exp2(score - biggest)
    total = jnp.sum(weight, axis=0, keepdims=True)
    acc = dot_nn(values[0].T, weight.astype(bf16))

    def step(back, carry):
        biggest, total, acc = carry
        score = dot_nn(keys[back], query_t) * factor
        larger = jnp.maximum(biggest, jnp.max(score, axis=0, keepdims=True))
        weight = jnp.exp2(score - larger)
        shrink = jnp.exp2(biggest - larger)
        total = total * shrink + jnp.sum(weight, axis=0, keepdims=True)
        acc = acc * shrink + dot_nn(values[back].T, weight.astype(bf16))
        return larger, total, acc

    biggest, total, acc = lax.fori_loop(1, place[0] + 1, step, (biggest, total, acc))
    out[...] = (acc / total).T.astype(bf16)
    log_total[0] = biggest + jnp.log(total) * LOG2E


def attend(place, pre, cosine, sine, kv_blocks):
    token_rows = pre.shape[0]
    blocks = kv_blocks.shape[0]
    width = (token_rows, HEAD_SIZE)
    many = (blocks, token_rows, HEAD_SIZE)
    return pl.pallas_call(
        attend_kernel,
        out_shape=(
            jax.ShapeDtypeStruct((token_rows, MODEL_WIDTH), bf16),
            jax.ShapeDtypeStruct((QUERY_HEADS, 1, token_rows), f32),
            jax.ShapeDtypeStruct((token_rows, MODEL_WIDTH), bf16),
        ),
        grid_spec=pltpu.PrefetchScalarGridSpec(
            num_scalar_prefetch=1,
            grid=(QUERY_HEADS,),
            in_specs=[
                pl.BlockSpec(width, lambda h, p: (0, h)),
                pl.BlockSpec(width, lambda h, p: (0, 0)),
                pl.BlockSpec(width, lambda h, p: (0, 0)),
                pl.BlockSpec(many, lambda h, p: (0, 0, h // GROUP)),
                pl.BlockSpec(many, lambda h, p: (0, 0, KEY_VALUE_HEADS + h // GROUP)),
            ],
            out_specs=(
                pl.BlockSpec(width, lambda h, p: (0, h)),
                pl.BlockSpec((1, 1, token_rows), lambda h, p: (h, 0, 0)),
                pl.BlockSpec(width, lambda h, p: (0, h)),
            ),
        ),
        compiler_params=params(56, 1),
        cost_estimate=cost(16e9, 8e6, 6e6),
        name="attend",
    )(place, pre, cosine, sine, kv_blocks, kv_blocks)


def attend_back_kernel(
    place, query, keys, values, out, out_grad, log_total, cosine, sine, pre_grad, key_grad, value_grad, key_acc, value_acc
):
    head = pl.program_id(0)

    @pl.when(head % GROUP == 0)
    def _():
        key_acc[...] = jnp.zeros_like(key_acc)
        value_acc[...] = jnp.zeros_like(value_acc)

    factor = SCORE_SCALE * LOG2E
    query_rows = query[...]
    grad_rows = out_grad[...]
    query_t = query_rows.astype(f32).T.astype(bf16)
    grad_t32 = grad_rows.astype(f32).T
    grad_t = grad_t32.astype(bf16)
    row_dot = jnp.sum(out[...].astype(f32).T * grad_t32, axis=0, keepdims=True)
    level = log_total[0]

    def block(back, masked):
        key = keys[back]
        score = dot_nn(key, query_t) * factor - level
        weight = jnp.exp2(score)
        if masked:
            weight = jnp.where(causal(weight), weight, 0.0)
        value_acc[back] += dot_nn(weight.astype(bf16), grad_rows)
        prob_grad = dot_nn(values[back], grad_t)
        score_grad = (weight * (prob_grad - row_dot)).astype(bf16)
        key_acc[back] += dot_nn(score_grad, query_rows)
        return dot_nn(key.T, score_grad)

    query_grad = block(0, True)
    query_grad = lax.fori_loop(1, place[0] + 1, lambda b, acc: acc + block(b, False), query_grad)
    rows = query_grad.T * SCORE_SCALE
    pre_grad[...] = (rows * cosine[...] - pltpu.roll(rows, HEAD_SIZE // 2, 1) * sine[...]).astype(bf16)

    @pl.when(head % GROUP == GROUP - 1)
    def _():
        key_grad[...] = (key_acc[...] * SCORE_SCALE).astype(bf16)
        value_grad[...] = value_acc[...].astype(bf16)


def attend_back(place, query, kv_blocks, out, out_grad, log_total, cosine, sine):
    token_rows = query.shape[0]
    blocks = kv_blocks.shape[0]
    width = (token_rows, HEAD_SIZE)
    many = (blocks, token_rows, HEAD_SIZE)
    return pl.pallas_call(
        attend_back_kernel,
        out_shape=(
            jax.ShapeDtypeStruct((token_rows, MODEL_WIDTH), bf16),
            jax.ShapeDtypeStruct((blocks, token_rows, KV), bf16),
            jax.ShapeDtypeStruct((blocks, token_rows, KV), bf16),
        ),
        grid_spec=pltpu.PrefetchScalarGridSpec(
            num_scalar_prefetch=1,
            grid=(QUERY_HEADS,),
            in_specs=[
                pl.BlockSpec(width, lambda h, p: (0, h)),
                pl.BlockSpec(many, lambda h, p: (0, 0, h // GROUP)),
                pl.BlockSpec(many, lambda h, p: (0, 0, KEY_VALUE_HEADS + h // GROUP)),
                pl.BlockSpec(width, lambda h, p: (0, h)),
                pl.BlockSpec(width, lambda h, p: (0, h)),
                pl.BlockSpec((1, 1, token_rows), lambda h, p: (h, 0, 0)),
                pl.BlockSpec(width, lambda h, p: (0, 0)),
                pl.BlockSpec(width, lambda h, p: (0, 0)),
            ],
            out_specs=(
                pl.BlockSpec(width, lambda h, p: (0, h)),
                pl.BlockSpec(many, lambda h, p: (0, 0, h // GROUP)),
                pl.BlockSpec(many, lambda h, p: (0, 0, h // GROUP)),
            ),
            scratch_shapes=[pltpu.VMEM(many, f32), pltpu.VMEM(many, f32)],
        ),
        compiler_params=params(56, 1),
        cost_estimate=cost(40e9, 12e6, 6e6),
        name="attend_back",
    )(place, query, kv_blocks, kv_blocks, out, out_grad, log_total, cosine, sine)


def inner_kernel(first, second, down, inner):
    shards, span = down.shape[0], down.shape[3]
    acc = None
    for c in range(shards):
        side = first if c < shards // 2 else second
        at = (c % (shards // 2)) * span
        term = dot_nt(side[0, :, at : at + span], down[c, 0])
        acc = term if acc is None else acc + term
    inner[0] = acc


def inner_rows(first, second, down):
    experts, rows, _ = first.shape
    shards, _, _, span = down.shape
    tile = 256
    return pl.pallas_call(
        inner_kernel,
        out_shape=jax.ShapeDtypeStruct((experts, rows, FF), f32),
        grid=(experts, FF // tile),
        in_specs=[
            pl.BlockSpec((1, rows, HALF), lambda e, n: (e, 0, 0)),
            pl.BlockSpec((1, rows, HALF), lambda e, n: (e, 0, 0)),
            pl.BlockSpec((shards, 1, tile, span), lambda e, n: (0, e, n, 0)),
        ],
        out_specs=pl.BlockSpec((1, rows, tile), lambda e, n: (e, 0, n)),
        compiler_params=params(56, 2),
        cost_estimate=cost(2 * experts * rows * FF * MODEL_WIDTH, 30e6),
        name="inner_rows",
    )(first, second, down)


def gate_kernel(first, second, gate_w, up_w, inner, weight, scaled, gate_out, up_out, gate_grad):
    shards, _, span, tile = gate_w.shape
    near, far = first[0], second[0]

    def product(ref):
        low = ref[: shards // 2, 0].reshape(HALF, tile)
        high = ref[shards // 2 :, 0].reshape(HALF, tile)
        return dot_nn(near, low) + dot_nn(far, high)

    gate_pre = product(gate_w)
    up_part = product(up_w)
    sigmoid = 1.0 / (1.0 + jnp.exp(-gate_pre))
    silu = gate_pre * sigmoid
    hidden = silu * up_part
    factor = weight[0]
    raw = inner[0]
    scaled[0] = (hidden * factor).astype(bf16)
    part = jnp.sum(raw * hidden, axis=1, keepdims=True)
    raw = raw * factor
    gate_out[0] = (raw * up_part * (sigmoid * (1.0 + gate_pre * (1.0 - sigmoid)))).astype(bf16)
    up_out[0] = (raw * silu).astype(bf16)

    @pl.when(pl.program_id(1) == 0)
    def _():
        gate_grad[0] = part

    @pl.when(pl.program_id(1) > 0)
    def _():
        gate_grad[0] += part


def gate_rows(first, second, gate_up, inner, weight):
    experts, rows, _ = first.shape
    shards, _, span, _ = gate_up.shape
    tile = 256
    tiles = FF // tile
    wide = pl.BlockSpec((1, rows, tile), lambda e, n: (e, 0, n))
    column = pl.BlockSpec((1, rows, 1), lambda e, n: (e, 0, 0))
    low = jax.ShapeDtypeStruct((experts, rows, FF), bf16)
    return pl.pallas_call(
        gate_kernel,
        out_shape=(low, low, low, jax.ShapeDtypeStruct((experts, rows, 1), f32)),
        grid=(experts, tiles),
        in_specs=[
            pl.BlockSpec((1, rows, HALF), lambda e, n: (e, 0, 0)),
            pl.BlockSpec((1, rows, HALF), lambda e, n: (e, 0, 0)),
            pl.BlockSpec((shards, 1, span, tile), lambda e, n: (0, e, 0, n)),
            pl.BlockSpec((shards, 1, span, tile), lambda e, n: (0, e, 0, n + tiles)),
            wide,
            column,
        ],
        out_specs=(wide, wide, wide, column),
        compiler_params=params(56, 2),
        cost_estimate=cost(4 * experts * rows * FF * MODEL_WIDTH, 50e6, experts * rows * FF),
        name="gate_rows",
    )(first, second, gate_up, gate_up, inner, weight)


def row_grad_kernel(gate_side, up_side, weight, out):
    block = weight[0, 0]
    out[0] = (dot_nt(gate_side[0], block[:, :FF]) + dot_nt(up_side[0], block[:, FF:])).astype(bf16)


def row_grads(gate_side, up_side, gate_up):
    experts, rows, _ = gate_side.shape
    shards, _, span, _ = gate_up.shape
    span_all = MODEL_WIDTH // shards
    whole = pl.BlockSpec((1, rows, FF), lambda e, n: (e, 0, 0))
    if span_all % 128:
        joined = gate_up.transpose(1, 0, 2, 3).reshape(1, experts, MODEL_WIDTH, 2 * FF)
        spec = pl.BlockSpec((1, 1, 384, 2 * FF), lambda e, n: (0, e, n, 0))
        span, shards = 384, MODEL_WIDTH // 384
    else:
        joined = gate_up
        spec = pl.BlockSpec((1, 1, span, 2 * FF), lambda e, n: (n, e, 0, 0))
    return pl.pallas_call(
        row_grad_kernel,
        out_shape=jax.ShapeDtypeStruct((experts, rows, MODEL_WIDTH), bf16),
        grid=(experts, shards),
        in_specs=[whole, whole, spec],
        out_specs=pl.BlockSpec((1, rows, span), lambda e, n: (e, 0, n)),
        compiler_params=params(56, 2),
        cost_estimate=cost(4 * experts * rows * FF * MODEL_WIDTH, 40e6),
        name="row_grads",
    )(gate_side, up_side, joined)


def result_kernel(scaled, down, out):
    shards, span = down.shape[0], down.shape[3]
    rows = scaled[0]
    for c in range(shards):
        out[0, :, c * span : (c + 1) * span] = dot_nn(rows, down[c, 0]).astype(bf16)


def result_rows(scaled, down):
    experts, rows, _ = scaled.shape
    shards, _, _, span = down.shape
    return pl.pallas_call(
        result_kernel,
        out_shape=jax.ShapeDtypeStruct((experts, rows, MODEL_WIDTH), bf16),
        grid=(experts,),
        in_specs=[
            pl.BlockSpec((1, rows, FF), lambda e: (e, 0, 0)),
            pl.BlockSpec((shards, 1, FF, span), lambda e: (0, e, 0, 0)),
        ],
        out_specs=pl.BlockSpec((1, rows, MODEL_WIDTH), lambda e: (e, 0, 0)),
        compiler_params=params(56, 1),
        cost_estimate=cost(2 * experts * rows * FF * MODEL_WIDTH, 22e6),
        name="result_rows",
    )(scaled, down)


def down_grad_kernel(scaled, first, second, out):
    shards, span = out.shape[0], out.shape[3]
    rows_t = scaled[0].T
    for c in range(shards):
        side = first if c < shards // 2 else second
        at = (c % (shards // 2)) * span
        out[c, 0] = dot_nn(rows_t, side[0, :, at : at + span]).astype(bf16)


def down_grads(scaled, first, second, shards):
    experts, rows, _ = scaled.shape
    span = MODEL_WIDTH // shards
    half = pl.BlockSpec((1, rows, HALF), lambda e: (e, 0, 0))
    return pl.pallas_call(
        down_grad_kernel,
        out_shape=jax.ShapeDtypeStruct((shards, experts, FF, span), bf16),
        grid=(experts,),
        in_specs=[pl.BlockSpec((1, rows, FF), lambda e: (e, 0, 0)), half, half],
        out_specs=pl.BlockSpec((shards, 1, FF, span), lambda e: (0, e, 0, 0)),
        compiler_params=params(56, 1),
        cost_estimate=cost(2 * experts * rows * FF * MODEL_WIDTH, 22e6),
        name="down_grads",
    )(scaled, first, second)


def in_grads(first, second, gate_side, up_side, shards):
    experts, rows, _ = first.shape
    span = MODEL_WIDTH // shards
    half = pl.BlockSpec((1, rows, HALF), lambda e, n: (e, 0, 0))

    def kernel(first, second, gate_side, up_side, out):
        pick = pl.program_id(1)

        def fill(column):
            for side, base in ((first, 0), (second, shards // 2)):
                rows_t = side[0].T
                for c in range(shards // 2):
                    part = rows_t[c * span : (c + 1) * span]
                    out[base + c, 0] = dot_nn(part, column[0]).astype(bf16)

        @pl.when(pick == 0)
        def _():
            fill(gate_side)

        @pl.when(pick == 1)
        def _():
            fill(up_side)

    return pl.pallas_call(
        kernel,
        out_shape=jax.ShapeDtypeStruct((shards, experts, span, 2 * FF), bf16),
        grid=(experts, 2),
        in_specs=[half, half, half, half],
        out_specs=pl.BlockSpec((shards, 1, span, FF), lambda e, n: (0, e, 0, n)),
        compiler_params=params(56, 2),
        cost_estimate=cost(4 * experts * rows * FF * MODEL_WIDTH, 35e6),
        name="in_grads",
    )(first, second, gate_side, up_side)


def pick_kernel(picks_up, picks_down, up, down, own, away):
    per = own.shape[1]
    for half, (picks, rows) in enumerate(((picks_up, up), (picks_down, down))):
        picked = dot_nn(picks[0], rows[...]).astype(bf16)
        own[half] = picked[:per]
        for r in range(away.shape[0]):
            away[r, half] = picked[(r + 1) * per : (r + 2) * per]


def pick_rows(picks, k, mirror, up, down, wide):
    _, many, token_rows = picks.shape
    per = many // wide
    return pl.pallas_call(
        pick_kernel,
        out_shape=(
            jax.ShapeDtypeStruct((2, per, HALF), bf16),
            jax.ShapeDtypeStruct((wide - 1, 2, per, HALF), bf16),
        ),
        grid=(1,),
        in_specs=[
            pl.BlockSpec((1, many, token_rows), lambda g: (k, 0, 0)),
            pl.BlockSpec((1, many, token_rows), lambda g: (mirror, 0, 0)),
            pl.BlockSpec((token_rows, HALF), lambda g: (0, 0)),
            pl.BlockSpec((token_rows, HALF), lambda g: (0, 0)),
        ],
        out_specs=(
            pl.BlockSpec((2, per, HALF), lambda g: (0, 0, 0)),
            pl.BlockSpec((wide - 1, 2, per, HALF), lambda g: (0, 0, 0, 0)),
        ),
        compiler_params=params(32, 1),
        cost_estimate=cost(4 * many * token_rows * HALF, 5e6),
        name="pick_rows",
    )(picks, picks, up, down)


def weight_grad_kernel(rows, *refs):
    *grads, extra, out = refs
    rows_t = rows[...].T
    at = 0
    for side in grads:
        columns = side.shape[1]
        out[:, at : at + columns] = dot_nn(rows_t, side[...]).astype(bf16)
        at += columns
    out[:, at:] = extra[...].T.astype(bf16)


def weight_grads(rows, grads, extra):
    token_rows = rows.shape[0]
    tile = 384
    columns = sum(g.shape[1] for g in grads) + extra.shape[0]
    return pl.pallas_call(
        weight_grad_kernel,
        out_shape=jax.ShapeDtypeStruct((MODEL_WIDTH, columns), bf16),
        grid=(MODEL_WIDTH // tile,),
        in_specs=[pl.BlockSpec((token_rows, tile), lambda n: (0, n))]
        + [pl.BlockSpec(g.shape, lambda n: (0, 0)) for g in grads]
        + [pl.BlockSpec((extra.shape[0], tile), lambda n: (0, n))],
        out_specs=pl.BlockSpec((tile, columns), lambda n: (n, 0)),
        compiler_params=params(56, 1),
        cost_estimate=cost(2 * MODEL_WIDTH * token_rows * columns, 14e6),
        name="weight_grads",
    )(rows, *grads, extra)


def adamw_update(weight, moment_one, moment_two, gradient, step_rate, decay_rate):
    first_new = BETA_ONE * moment_one + (1.0 - BETA_ONE) * gradient
    second_new = BETA_TWO * moment_two + (1.0 - BETA_TWO) * gradient * gradient
    first_hat = first_new / (1.0 - BETA_ONE**STEP)
    second_hat = second_new / (1.0 - BETA_TWO**STEP)
    weight_new = weight - step_rate * (
        first_hat / (jnp.sqrt(second_hat) + ADAM_EPS) + decay_rate * weight
    )
    return (weight_new, first_new, second_new)


def body(
    tokens,
    cotangent,
    routes,
    gains,
    gains_first,
    gains_second,
    query_weight,
    query_first,
    query_second,
    key_matrix,
    key_moment_first,
    key_moment_second,
    value_matrix,
    value_moment_first,
    value_moment_second,
    output_weight,
    output_first,
    output_second,
    router_weight,
    router_first,
    router_second,
    expert_in,
    in_first,
    in_second,
    expert_out,
    out_first,
    out_second,
):
    token_rows, top_count = routes.shape
    shards = lax.axis_size("fsdp")
    place = lax.axis_index("fsdp")
    groups = lax.axis_size("expert")
    group = lax.axis_index("expert")
    depth = DEPTH
    wide = groups // depth
    level, column = group // wide, group % wide
    experts_local = expert_in.shape[0]
    experts_all = experts_local * groups
    near = wide * experts_local
    shard_rows = query_weight.shape[0]

    def z_shift(value, by):
        return lax.ppermute(
            value,
            "expert",
            [(a * wide + b, (a + by) % depth * wide + b) for a in range(depth) for b in range(wide)],
        )

    def x_shift(value, by):
        return lax.ppermute(
            value,
            "expert",
            [(a * wide + b, a * wide + (b + by) % wide) for a in range(depth) for b in range(wide)],
        )

    def back_shift(value, by):
        pairs = [(a, a + by) for a in range(shards) if 0 <= a + by < shards]
        return lax.ppermute(value, "fsdp", pairs)

    def z_spread(value):
        up, down = [value[:, :HALF]], [value[:, HALF:]]
        for _ in range(depth - 1):
            up.append(z_shift(up[-1], 1))
            down.append(z_shift(down[-1], -1))
        return up, down

    small = jnp.concatenate(
        [
            router_weight.astype(bf16),
            gains.T.astype(bf16),
            jnp.zeros((shard_rows, 128 - experts_all - 2), bf16),
        ],
        axis=1,
    )
    front_low = lax.all_gather(
        jnp.concatenate(
            [query_weight.astype(bf16), key_matrix.astype(bf16), value_matrix.astype(bf16), small], axis=1
        ),
        "fsdp",
        axis=0,
        tiled=True,
    )
    output_low = lax.all_gather(output_weight.astype(bf16), "fsdp", axis=0, tiled=True)
    gate_up_low = lax.all_gather(expert_in.astype(bf16), "fsdp", axis=0)
    down_low = lax.all_gather(expert_out.astype(bf16), "fsdp", axis=0)
    qkv_low = front_low[:, :QKV]
    router_low = front_low[:, QKV : QKV + experts_all]
    gain_pair = front_low[:, QKV + experts_all : QKV + experts_all + 2].astype(f32).T
    gain_one, gain_two = gain_pair[0], gain_pair[1]

    routes_t = routes.T
    routes_of = jnp.stack([routes_t] + [z_shift(routes_t, i) for i in range(1, depth)])

    def expert_ids(at_level):
        columns = (column + jnp.arange(wide, dtype=jnp.int32)) % wide
        first_ids = (at_level * wide + columns) * experts_local
        return (first_ids[:, None] + jnp.arange(experts_local, dtype=jnp.int32)[None, :]).reshape(near)

    named = (routes_of[:, None] == expert_ids(level)[None, :, None, None]).astype(f32)
    chosen_here = jnp.sum(named, axis=2)
    earlier = (
        jnp.arange(token_rows, dtype=jnp.int32)[:, None] < jnp.arange(token_rows, dtype=jnp.int32)[None, :]
    ).astype(bf16)
    slots = dot_nn(chosen_here.reshape(depth * near, token_rows).astype(bf16), earlier).reshape(
        depth, near, token_rows
    )
    code = jnp.where(chosen_here > 0, slots.astype(jnp.int32), -1)
    picks = code[:, :, None, :] == jnp.arange(CAP, dtype=jnp.int32)[None, None, :, None]
    picks_low = picks.astype(bf16).reshape(depth, near * CAP, token_rows)

    def pick_all(up, down):
        return [pick_rows(picks_low, k, (depth - k) % depth, up[k], down[k], wide) for k in range(depth)]

    def swap_all(picked):
        first = [[None] * depth for _ in range(wide)]
        second = [[None] * depth for _ in range(wide)]
        for k, (own, away) in enumerate(picked):
            for r in range(wide):
                pair = x_shift(away[r - 1], r) if r else own
                pair = pair.reshape(2, experts_local, CAP, HALF)
                first[r][k] = pair[0]
                second[r][(depth - k) % depth] = pair[1]
        shape = (experts_local, wide * depth * CAP, HALF)
        return (
            jnp.stack([first[r][i] for r in range(wide) for i in range(depth)], axis=1).reshape(shape),
            jnp.stack([second[r][i] for r in range(wide) for i in range(depth)], axis=1).reshape(shape),
        )

    def swap_back(rows):
        shaped = rows.reshape(experts_local, wide, depth, CAP, MODEL_WIDTH)
        steps = []
        for m in range(depth):
            i = (m + 1) % depth
            mirror = (depth - i) % depth
            pieces = []
            for r in range(wide):
                pair = jnp.stack([shaped[:, r, i, :, :HALF], shaped[:, r, mirror, :, HALF:]])
                if r:
                    pair = x_shift(pair, -r)
                pieces.append(pair.reshape(2, experts_local * CAP, HALF))
            steps.append(jnp.concatenate(pieces, axis=1))
        return steps

    def collect(steps):
        held = []
        for m, both in enumerate(steps):
            i = (m + 1) % depth
            mirror = (depth - i) % depth
            part_up = dot_tn(picks_low[i], both[0])
            part_down = dot_tn(picks_low[mirror], both[1])
            if m:
                part_up = part_up + z_shift(held[-1][0], 1).astype(f32)
                part_down = part_down + z_shift(held[-1][1], -1).astype(f32)
            held.append((part_up.astype(bf16), part_down.astype(bf16)))
        return jnp.concatenate([part_up, part_down], axis=1), held

    upstream = cotangent.astype(f32)
    upstream_picked = pick_all(*z_spread(cotangent))

    inputs = tokens.astype(f32)
    scale_one = lax.rsqrt(jnp.mean(inputs * inputs, axis=1, keepdims=True) + NORM_EPS)
    normed_one = inputs * scale_one
    first_hidden = (normed_one * gain_one).astype(bf16)
    inverse = ROPE_BASE ** (-(jnp.arange(HEAD_SIZE // 2, dtype=f32) * 2.0 / HEAD_SIZE))
    places = (place * token_rows + jnp.arange(token_rows, dtype=jnp.int32)).astype(f32)
    angles = places[:, None] * inverse[None, :]
    half_cos, half_sin = jnp.cos(angles), jnp.sin(angles)
    cosine = jnp.concatenate([half_cos, half_cos], axis=1)
    sine = jnp.concatenate([-half_sin, half_sin], axis=1)

    def turn_keys(rows, sign):
        parts = []
        for h in range(KEY_VALUE_HEADS):
            piece = rows[:, h * HEAD_SIZE : (h + 1) * HEAD_SIZE]
            swapped = jnp.concatenate([piece[:, HEAD_SIZE // 2 :], piece[:, : HEAD_SIZE // 2]], axis=1)
            parts.append(piece * cosine + swapped * (sign * sine))
        return jnp.concatenate(parts, axis=1)

    pre = dot_nn(first_hidden, qkv_low)
    keys_local = turn_keys(pre[:, MODEL_WIDTH : MODEL_WIDTH + KV], 1.0).astype(bf16)
    kv_local = jnp.concatenate([keys_local, pre[:, MODEL_WIDTH + KV :].astype(bf16)], axis=1)
    kv_blocks = jnp.stack([kv_local] + [back_shift(kv_local, s) for s in range(1, shards)])
    kv_blocks, upstream_picked = lax.optimization_barrier((kv_blocks, upstream_picked))
    upstream_rows = swap_all(upstream_picked)
    place_arg = place.astype(jnp.int32).reshape(1)
    attended, log_total, query_rows = attend(place_arg, pre, cosine, sine, kv_blocks)
    residual = inputs + dot_nn(attended, output_low)
    scale_two = lax.rsqrt(jnp.mean(residual * residual, axis=1, keepdims=True) + NORM_EPS)
    normed_two = residual * scale_two
    hidden_two = (normed_two * gain_two).astype(bf16)

    hidden_rows = swap_all(pick_all(*z_spread(hidden_two)))
    logits_t = lax.dot_general(
        router_low, hidden_two, (((0,), (1,)), ((), ())), preferred_element_type=f32
    )
    all_ids = jnp.arange(experts_all, dtype=jnp.int32)
    chosen_t = (routes_t[:, None, :] == all_ids[None, :, None]).astype(f32)
    gate_weights = jax.nn.softmax(jnp.sum(chosen_t * logits_t[None], axis=1), axis=0)
    gates_of = jnp.stack([gate_weights] + [z_shift(gate_weights, i) for i in range(1, depth)])
    gates_near = jnp.sum(named * gates_of[:, None], axis=2)
    row_gates = jnp.sum(jnp.where(picks, gates_near[:, :, None, :], 0.0), axis=3)
    row_gates = row_gates.reshape(depth, wide, experts_local, CAP)
    row_gates = jnp.stack(
        [row_gates[:, 0]] + [x_shift(row_gates[:, r], r) for r in range(1, wide)]
    )
    row_gates = row_gates.transpose(2, 0, 1, 3).reshape(experts_local, wide * depth * CAP, 1)

    inner = inner_rows(*upstream_rows, down_low)
    scaled_hidden, gate_side, up_side, gate_dots = gate_rows(*hidden_rows, gate_up_low, inner, row_gates)
    hidden_back, held = collect(swap_back(row_grads(gate_side, up_side, gate_up_low)))

    down_term = down_grads(scaled_hidden, *upstream_rows, shards)
    in_term = in_grads(*hidden_rows, gate_side, up_side, shards)
    results = result_rows(scaled_hidden, down_low)
    out_sum = lax.psum_scatter(down_term, "fsdp", scatter_dimension=0).astype(f32)
    in_sum = lax.psum_scatter(in_term, "fsdp", scatter_dimension=0).astype(f32)
    results, _ = lax.optimization_barrier((results, held[2]))
    result_steps = swap_back(results)

    gate_dots = gate_dots.reshape(experts_local, wide, depth, CAP)
    gate_dots = jnp.stack(
        [gate_dots[:, 0]] + [x_shift(gate_dots[:, r], -r) for r in range(1, wide)]
    )
    gate_dots, _ = lax.optimization_barrier((gate_dots, held[2]))
    gate_dots = gate_dots.transpose(2, 0, 1, 3).reshape(depth, near, CAP)
    token_dots = jnp.sum(jnp.where(picks, gate_dots[:, :, :, None], 0.0), axis=2)
    home_dots = [token_dots[0]] + [z_shift(token_dots[i], -i) for i in range(1, depth)]
    gate_grad = 0.0
    for i in range(depth):
        ids = expert_ids((level + i) % depth)
        same = (routes_t[:, None, :] == ids[None, :, None]).astype(f32)
        gate_grad = gate_grad + jnp.sum(same * home_dots[i][None], axis=1)
    picked_grad = gate_weights * (
        gate_grad - jnp.sum(gate_weights * gate_grad, axis=0, keepdims=True)
    )
    logit_grad_t = jnp.sum(chosen_t * picked_grad[:, None, :], axis=0).astype(bf16)
    router_term = dot_nn(logit_grad_t, hidden_two)
    hidden_two_grad = hidden_back + lax.dot_general(
        logit_grad_t, router_low, (((0,), (1,)), ((), ())), preferred_element_type=f32
    )

    gain_two_term = jnp.sum(hidden_two_grad * normed_two, axis=0)
    scaled_two = hidden_two_grad * gain_two
    residual_grad = upstream + scale_two * (
        scaled_two - normed_two * jnp.mean(scaled_two * normed_two, axis=1, keepdims=True)
    )
    branch_grad = residual_grad.astype(bf16)
    attended_grad = dot_nt(branch_grad, output_low).astype(bf16)
    attended_grad, in_term, down_term = lax.optimization_barrier((attended_grad, in_term, down_term))
    pre_grad, key_back, value_back = attend_back(
        place_arg, query_rows, kv_blocks, attended, attended_grad, log_total, cosine, sine
    )
    kv_back = jnp.concatenate([key_back, value_back], axis=2)
    kv_grad = kv_back[0].astype(f32)
    for s in range(1, shards):
        kv_grad = kv_grad + back_shift(kv_back[s], -s).astype(f32)
    key_pre_grad = turn_keys(kv_grad[:, :KV], -1.0)
    kv_pre_grad = jnp.concatenate([key_pre_grad, kv_grad[:, KV:]], axis=1).astype(bf16)

    moe_out, _ = collect(result_steps)
    layer_out = (residual + moe_out).astype(bf16)

    hidden_one_grad = dot_nt(pre_grad, qkv_low[:, :MODEL_WIDTH]) + dot_nt(kv_pre_grad, qkv_low[:, MODEL_WIDTH:])
    gain_one_term = jnp.sum(hidden_one_grad * normed_one, axis=0)
    scaled_one = hidden_one_grad * gain_one
    input_grad = (
        residual_grad
        + scale_one
        * (scaled_one - normed_one * jnp.mean(scaled_one * normed_one, axis=1, keepdims=True))
    ).astype(bf16)

    def extra_rows(*terms):
        used = sum(t.shape[0] for t in terms)
        return jnp.concatenate(list(terms) + [jnp.zeros((128 - used, MODEL_WIDTH), f32)], axis=0)

    def spread_sum(parts, index, shift):
        count = parts.shape[0]
        total = lax.dynamic_index_in_dim(parts, index, 0, keepdims=False).astype(f32)
        for s in range(1, count):
            sent = lax.dynamic_index_in_dim(parts, (index + s) % count, 0, keepdims=False)
            total = total + shift(sent, s).astype(f32)
        return total

    def join(part, index, count, shift):
        whole = jnp.zeros((count,) + part.shape, part.dtype)
        for s in range(count):
            piece = shift(part, s) if s else part
            whole = lax.dynamic_update_index_in_dim(whole, piece, (index - s) % count, 0)
        return whole

    def core_shift(value, by):
        return lax.ppermute(value, "fsdp", [(a, a // 2 * 2 + (a + by) % 2) for a in range(shards)])

    def y_shift(value, by):
        return lax.ppermute(value, "fsdp", [(a, (a + 2 * by) % shards) for a in range(shards)])

    def total_sum(terms):
        columns = terms.shape[1]
        parts = terms.reshape(shards // 2, 2, shard_rows, columns).transpose(1, 0, 2, 3)
        part = spread_sum(parts, place % 2, core_shift).astype(bf16)
        part = spread_sum(part, place // 2, y_shift).astype(bf16)
        part = spread_sum(part.reshape(wide, shard_rows // wide, columns), column, x_shift).astype(bf16)
        part = spread_sum(part.reshape(depth, shard_rows // wide // depth, columns), level, z_shift).astype(bf16)
        part = join(part, level, depth, z_shift).reshape(shard_rows // wide, columns)
        return join(part, column, wide, x_shift).reshape(shard_rows, columns).astype(f32)

    back_sum = total_sum(weight_grads(attended, [branch_grad], extra_rows(router_term, gain_two_term[None])))
    front_sum = total_sum(weight_grads(first_hidden, [pre_grad, kv_pre_grad], extra_rows(gain_one_term[None])))
    output_sum = back_sum[:, :MODEL_WIDTH]
    router_sum = back_sum[:, MODEL_WIDTH : MODEL_WIDTH + experts_all]
    query_sum = front_sum[:, :MODEL_WIDTH]
    key_sum = front_sum[:, MODEL_WIDTH : MODEL_WIDTH + KV]
    value_sum = front_sum[:, MODEL_WIDTH + KV : QKV]
    gain_sum = jnp.stack([front_sum[:, QKV], back_sum[:, MODEL_WIDTH + experts_all]])

    rate = 0.5 / math.sqrt(MODEL_WIDTH // 2)
    return (
        layer_out,
        input_grad,
        *adamw_update(gains, gains_first, gains_second, gain_sum, GAIN_RATE, 0.0),
        *adamw_update(query_weight, query_first, query_second, query_sum, rate, DECAY),
        *adamw_update(key_matrix, key_moment_first, key_moment_second, key_sum, rate, DECAY),
        *adamw_update(
            value_matrix,
            value_moment_first,
            value_moment_second,
            value_sum,
            0.5 / math.sqrt(MODEL_WIDTH),
            DECAY,
        ),
        *adamw_update(
            output_weight, output_first, output_second, output_sum, 0.5 / math.sqrt(MODEL_WIDTH // 32), DECAY
        ),
        *adamw_update(
            router_weight, router_first, router_second, router_sum, 0.5 / math.sqrt(4 * MODEL_WIDTH), DECAY
        ),
        *adamw_update(expert_in, in_first, in_second, in_sum, 0.5 / math.sqrt(MODEL_WIDTH), DECAY),
        *adamw_update(expert_out, out_first, out_second, out_sum, 0.5 / math.sqrt(FF // 8), DECAY),
    )


def solution(mesh):
    rows = P(("expert", "fsdp"), None)
    gains = P(None, "fsdp")
    matrix = P("fsdp", None)
    wide = P("expert", "fsdp", None)
    tall = P("expert", None, "fsdp")
    return jax.shard_map(
        body,
        mesh=mesh,
        in_specs=(rows,) * 3 + (gains,) * 3 + (matrix,) * 15 + (wide,) * 3 + (tall,) * 3,
        out_specs=(rows,) * 2 + (gains,) * 3 + (matrix,) * 15 + (wide,) * 3 + (tall,) * 3,
        check_vma=False,
    )
```

```python
import functools
import math

import jax
import jax.numpy as jnp
from jax import lax
from jax.experimental import pallas as pl
from jax.experimental.pallas import tpu as pltpu
from jax.sharding import PartitionSpec as P

MODEL_WIDTH = 1536
QUERY_HEADS = 12
KEY_VALUE_HEADS = 2
HEAD_SIZE = 128
GROUP = QUERY_HEADS // KEY_VALUE_HEADS
FF = 768
STEP = 10
CAP = 80
DEPTH = 4
HALF = MODEL_WIDTH // 2
KV = KEY_VALUE_HEADS * HEAD_SIZE
QKV = MODEL_WIDTH + 2 * KV


NORM_EPS = 1e-05
ROPE_BASE = 10000.0
BETA_ONE = 0.9
BETA_TWO = 0.95
ADAM_EPS = 1e-08
DECAY = 0.1
GAIN_RATE = 0.8
MASKED = -1e30
LOG2E = 1.0 / math.log(2.0)
SCORE_SCALE = 1.0 / math.sqrt(HEAD_SIZE)

f32 = jnp.float32
bf16 = jnp.bfloat16


def dot_nn(left, right):
    return lax.dot_general(left, right, (((1,), (0,)), ((), ())), preferred_element_type=f32)


def dot_nt(left, right):
    return lax.dot_general(left, right, (((1,), (1,)), ((), ())), preferred_element_type=f32)


def dot_tn(left, right):
    return lax.dot_general(left, right, (((0,), (0,)), ((), ())), preferred_element_type=f32)


def after(value, *others):
    return lax.optimization_barrier((value, others))[0]


def params(megabytes, axes):
    return pltpu.CompilerParams(
        vmem_limit_bytes=megabytes * 1024 * 1024, dimension_semantics=("arbitrary",) * axes
    )


def cost(flops, nbytes, trans=0):
    return pl.CostEstimate(flops=int(flops), bytes_accessed=int(nbytes), transcendentals=0)


def causal(score_t):
    key_place = lax.broadcasted_iota(jnp.int32, score_t.shape, 0)
    query_place = lax.broadcasted_iota(jnp.int32, score_t.shape, 1)
    return key_place <= query_place


def attend_kernel(place, pre, cosine, sine, keys, values, out, log_total, turned):
    rows = pre[...]
    query = rows * cosine[...] + pltpu.roll(rows, HEAD_SIZE // 2, 1) * sine[...]
    turned[...] = query.astype(bf16)
    query_t = query.T.astype(bf16)
    factor = SCORE_SCALE * LOG2E

    score = dot_nn(keys[0], query_t) * factor
    score = jnp.where(causal(score), score, MASKED)
    biggest = jnp.max(score, axis=0, keepdims=True)
    weight = jnp.exp2(score - biggest)
    total = jnp.sum(weight, axis=0, keepdims=True)
    acc = dot_nn(values[0].T, weight.astype(bf16))

    def step(back, carry):
        biggest, total, acc = carry
        score = dot_nn(keys[back], query_t) * factor
        larger = jnp.maximum(biggest, jnp.max(score, axis=0, keepdims=True))
        weight = jnp.exp2(score - larger)
        shrink = jnp.exp2(biggest - larger)
        total = total * shrink + jnp.sum(weight, axis=0, keepdims=True)
        acc = acc * shrink + dot_nn(values[back].T, weight.astype(bf16))
        return larger, total, acc

    biggest, total, acc = lax.fori_loop(1, place[0] + 1, step, (biggest, total, acc))
    out[...] = (acc / total).T.astype(bf16)
    log_total[0] = biggest + jnp.log(total) * LOG2E


def attend(place, pre, cosine, sine, kv_blocks):
    token_rows = pre.shape[0]
    blocks = kv_blocks.shape[0]
    width = (token_rows, HEAD_SIZE)
    many = (blocks, token_rows, HEAD_SIZE)
    return pl.pallas_call(
        attend_kernel,
        out_shape=(
            jax.ShapeDtypeStruct((token_rows, MODEL_WIDTH), bf16),
            jax.ShapeDtypeStruct((QUERY_HEADS, 1, token_rows), f32),
            jax.ShapeDtypeStruct((token_rows, MODEL_WIDTH), bf16),
        ),
        grid_spec=pltpu.PrefetchScalarGridSpec(
            num_scalar_prefetch=1,
            grid=(QUERY_HEADS,),
            in_specs=[
                pl.BlockSpec(width, lambda h, p: (0, h)),
                pl.BlockSpec(width, lambda h, p: (0, 0)),
                pl.BlockSpec(width, lambda h, p: (0, 0)),
                pl.BlockSpec(many, lambda h, p: (0, 0, h // GROUP)),
                pl.BlockSpec(many, lambda h, p: (0, 0, KEY_VALUE_HEADS + h // GROUP)),
            ],
            out_specs=(
                pl.BlockSpec(width, lambda h, p: (0, h)),
                pl.BlockSpec((1, 1, token_rows), lambda h, p: (h, 0, 0)),
                pl.BlockSpec(width, lambda h, p: (0, h)),
            ),
        ),
        compiler_params=params(56, 1),
        cost_estimate=cost(1e9, 1e6),
        name="attend",
    )(place, pre, cosine, sine, kv_blocks, kv_blocks)


def attend_back_kernel(
    place, query, keys, values, out, out_grad, log_total, cosine, sine, pre_grad, key_grad, value_grad, key_acc, value_acc
):
    head = pl.program_id(0)

    @pl.when(head % GROUP == 0)
    def _():
        key_acc[...] = jnp.zeros_like(key_acc)
        value_acc[...] = jnp.zeros_like(value_acc)

    factor = SCORE_SCALE * LOG2E
    query_rows = query[...]
    grad_rows = out_grad[...]
    query_t = query_rows.astype(f32).T.astype(bf16)
    grad_t32 = grad_rows.astype(f32).T
    grad_t = grad_t32.astype(bf16)
    row_dot = jnp.sum(out[...].astype(f32).T * grad_t32, axis=0, keepdims=True)
    level = log_total[0]

    def block(back, masked):
        key = keys[back]
        score = dot_nn(key, query_t) * factor - level
        weight = jnp.exp2(score)
        if masked:
            weight = jnp.where(causal(weight), weight, 0.0)
        value_acc[back] += dot_nn(weight.astype(bf16), grad_rows)
        prob_grad = dot_nn(values[back], grad_t)
        score_grad = (weight * (prob_grad - row_dot)).astype(bf16)
        key_acc[back] += dot_nn(score_grad, query_rows)
        return dot_nn(key.T, score_grad)

    query_grad = block(0, True)
    query_grad = lax.fori_loop(1, place[0] + 1, lambda b, acc: acc + block(b, False), query_grad)
    rows = query_grad.T * SCORE_SCALE
    pre_grad[...] = (rows * cosine[...] - pltpu.roll(rows, HEAD_SIZE // 2, 1) * sine[...]).astype(bf16)

    @pl.when(head % GROUP == GROUP - 1)
    def _():
        key_grad[...] = (key_acc[...] * SCORE_SCALE).astype(bf16)
        value_grad[...] = value_acc[...].astype(bf16)


def attend_back(place, query, kv_blocks, out, out_grad, log_total, cosine, sine):
    token_rows = query.shape[0]
    blocks = kv_blocks.shape[0]
    width = (token_rows, HEAD_SIZE)
    many = (blocks, token_rows, HEAD_SIZE)
    return pl.pallas_call(
        attend_back_kernel,
        out_shape=(
            jax.ShapeDtypeStruct((token_rows, MODEL_WIDTH), bf16),
            jax.ShapeDtypeStruct((blocks, token_rows, KV), bf16),
            jax.ShapeDtypeStruct((blocks, token_rows, KV), bf16),
        ),
        grid_spec=pltpu.PrefetchScalarGridSpec(
            num_scalar_prefetch=1,
            grid=(QUERY_HEADS,),
            in_specs=[
                pl.BlockSpec(width, lambda h, p: (0, h)),
                pl.BlockSpec(many, lambda h, p: (0, 0, h // GROUP)),
                pl.BlockSpec(many, lambda h, p: (0, 0, KEY_VALUE_HEADS + h // GROUP)),
                pl.BlockSpec(width, lambda h, p: (0, h)),
                pl.BlockSpec(width, lambda h, p: (0, h)),
                pl.BlockSpec((1, 1, token_rows), lambda h, p: (h, 0, 0)),
                pl.BlockSpec(width, lambda h, p: (0, 0)),
                pl.BlockSpec(width, lambda h, p: (0, 0)),
            ],
            out_specs=(
                pl.BlockSpec(width, lambda h, p: (0, h)),
                pl.BlockSpec(many, lambda h, p: (0, 0, h // GROUP)),
                pl.BlockSpec(many, lambda h, p: (0, 0, h // GROUP)),
            ),
            scratch_shapes=[pltpu.VMEM(many, f32), pltpu.VMEM(many, f32)],
        ),
        compiler_params=params(56, 1),
        cost_estimate=cost(1e9, 1e6),
        name="attend_back",
    )(place, query, kv_blocks, kv_blocks, out, out_grad, log_total, cosine, sine)


def gather_rows(pieces, rows):
    for p, piece in enumerate(pieces):
        rows[p * CAP : (p + 1) * CAP] = piece[...]


def scatter_rows(rows, pieces, at, span):
    low = rows.astype(bf16)
    for p, piece in enumerate(pieces):
        piece[:, at : at + span] = low[p * CAP : (p + 1) * CAP]


def piece_spec():
    return pl.BlockSpec((CAP, MODEL_WIDTH), lambda e, *_: (e, 0))


def row_scratch(count):
    return [pltpu.VMEM((count * CAP, MODEL_WIDTH), bf16)]


def inner_kernel(count, *refs):
    pieces, (down, inner, rows) = refs[:count], refs[count:]
    gather_rows(pieces, rows)
    shards, span = down.shape[0], down.shape[3]
    acc = None
    for c in range(shards):
        term = dot_nt(rows[:, c * span : (c + 1) * span], down[c, 0])
        acc = term if acc is None else acc + term
    inner[0] = acc.astype(bf16)


def inner_rows(pieces, down):
    shards, experts, _, span = down.shape
    rows = len(pieces) * CAP
    return pl.pallas_call(
        functools.partial(inner_kernel, len(pieces)),
        out_shape=jax.ShapeDtypeStruct((experts, rows, FF), bf16),
        grid=(experts,),
        in_specs=[piece_spec()] * len(pieces) + [pl.BlockSpec((shards, 1, FF, span), lambda e: (0, e, 0, 0))],
        out_specs=pl.BlockSpec((1, rows, FF), lambda e: (e, 0, 0)),
        scratch_shapes=row_scratch(len(pieces)),
        compiler_params=params(56, 1),
        cost_estimate=cost(2 * experts * rows * FF * MODEL_WIDTH, 20e6),
        name="inner_rows",
    )(*pieces, down)


def core_kernel(count, *refs):
    pieces, refs = refs[:count], refs[count:]
    gate_up, inner, weight, scaled, gate_side, up_side, gate_dots = refs[:7]
    back, (rows,) = refs[7 : 7 + count], refs[7 + count :]
    gather_rows(pieces, rows)
    span = gate_up.shape[2]
    tile = 256
    factor = weight[0]
    dots = None

    def product(at):
        return dot_nn(rows[...], gate_up[:, 0, :, at : at + tile].reshape(MODEL_WIDTH, tile))

    for n in range(FF // tile):
        at = n * tile
        gate_pre = product(at)
        up_part = product(FF + at)
        sigmoid = 1.0 / (1.0 + jnp.exp(-gate_pre))
        silu = gate_pre * sigmoid
        hidden = silu * up_part
        raw = inner[0, :, at : at + tile].astype(f32)
        part = jnp.sum(raw * hidden, axis=1, keepdims=True)
        dots = part if dots is None else dots + part
        scaled[0, :, at : at + tile] = (hidden * factor).astype(bf16)
        raw = raw * factor
        gate_side[0, :, at : at + tile] = (raw * up_part * (sigmoid + silu * (1.0 - sigmoid))).astype(bf16)
        up_side[0, :, at : at + tile] = (raw * silu).astype(bf16)
    gate_dots[0] = dots

    width = 384
    group = width // span
    for chunk in range(MODEL_WIDTH // width):
        block = gate_up[chunk * group : (chunk + 1) * group, 0].reshape(width, 2 * FF)
        grads = dot_nt(gate_side[0], block[:, :FF]) + dot_nt(up_side[0], block[:, FF:])
        scatter_rows(grads, back, chunk * width, width)


def core_rows(pieces, gate_up, inner, weight):
    count = len(pieces)
    shards, experts, span, _ = gate_up.shape
    rows = count * CAP
    whole = pl.BlockSpec((1, rows, FF), lambda e: (e, 0, 0))
    column = pl.BlockSpec((1, rows, 1), lambda e: (e, 0, 0))
    low = jax.ShapeDtypeStruct((experts, rows, FF), bf16)
    out = pl.pallas_call(
        functools.partial(core_kernel, count),
        out_shape=(low, low, low, jax.ShapeDtypeStruct((experts, rows, 1), f32))
        + (jax.ShapeDtypeStruct(pieces[0].shape, bf16),) * count,
        grid=(experts,),
        in_specs=[piece_spec()] * count
        + [pl.BlockSpec((shards, 1, span, 2 * FF), lambda e: (0, e, 0, 0)), whole, column],
        out_specs=(whole, whole, whole, column) + (piece_spec(),) * count,
        scratch_shapes=row_scratch(len(pieces)),
        compiler_params=params(60, 1),
        cost_estimate=cost(8 * experts * rows * FF * MODEL_WIDTH, 60e6),
        name="core_rows",
    )(*pieces, gate_up, inner, weight)
    return out[0], out[1], out[2], out[3], list(out[4:])


def result_kernel(scaled, down, *pieces):
    width = 384
    shards, span = down.shape[0], down.shape[3]
    group = width // span
    rows = scaled[0]
    for chunk in range(MODEL_WIDTH // width):
        parts = [down[c, 0] for c in range(chunk * group, (chunk + 1) * group)]
        block = parts[0] if group == 1 else jnp.concatenate(parts, axis=1)
        scatter_rows(dot_nn(rows, block), pieces, chunk * width, width)


def result_rows(scaled, down, count):
    experts, rows, _ = scaled.shape
    shards, _, _, span = down.shape
    return list(
        pl.pallas_call(
            result_kernel,
            out_shape=(jax.ShapeDtypeStruct((experts * CAP, MODEL_WIDTH), bf16),) * count,
            grid=(experts,),
            in_specs=[
                pl.BlockSpec((1, rows, FF), lambda e: (e, 0, 0)),
                pl.BlockSpec((shards, 1, FF, span), lambda e: (0, e, 0, 0)),
            ],
            out_specs=(piece_spec(),) * count,
            compiler_params=params(56, 1),
            cost_estimate=cost(2 * experts * rows * FF * MODEL_WIDTH, 22e6),
            name="result_rows",
        )(scaled, down)
    )


def down_grad_kernel(count, *refs):
    pieces, (scaled, out, rows) = refs[:count], refs[count:]
    gather_rows(pieces, rows)
    shards, span = out.shape[0], out.shape[3]
    scaled_t = scaled[0].T
    for c in range(shards):
        out[c, 0] = dot_nn(scaled_t, rows[:, c * span : (c + 1) * span]).astype(bf16)


def down_grads(pieces, scaled, shards):
    experts, rows, _ = scaled.shape
    span = MODEL_WIDTH // shards
    return pl.pallas_call(
        functools.partial(down_grad_kernel, len(pieces)),
        out_shape=jax.ShapeDtypeStruct((shards, experts, FF, span), bf16),
        grid=(experts,),
        in_specs=[piece_spec()] * len(pieces) + [pl.BlockSpec((1, rows, FF), lambda e: (e, 0, 0))],
        out_specs=pl.BlockSpec((shards, 1, FF, span), lambda e: (0, e, 0, 0)),
        scratch_shapes=row_scratch(len(pieces)),
        compiler_params=params(56, 1),
        cost_estimate=cost(2 * experts * rows * FF * MODEL_WIDTH, 22e6),
        name="down_grads",
    )(*pieces, scaled)


def in_grad_kernel(count, *refs):
    pieces, (gate_side, up_side, out, rows) = refs[:count], refs[count:]
    gather_rows(pieces, rows)
    shards, span = out.shape[0], out.shape[2]
    rows_t = rows[...].T
    for c in range(shards):
        part = rows_t[c * span : (c + 1) * span]
        out[c, 0, :, :FF] = dot_nn(part, gate_side[0]).astype(bf16)
        out[c, 0, :, FF:] = dot_nn(part, up_side[0]).astype(bf16)


def in_grads(pieces, gate_side, up_side, shards):
    experts, rows, _ = gate_side.shape
    span = MODEL_WIDTH // shards
    whole = pl.BlockSpec((1, rows, FF), lambda e: (e, 0, 0))
    return pl.pallas_call(
        functools.partial(in_grad_kernel, len(pieces)),
        out_shape=jax.ShapeDtypeStruct((shards, experts, span, 2 * FF), bf16),
        grid=(experts,),
        in_specs=[piece_spec()] * len(pieces) + [whole, whole],
        out_specs=pl.BlockSpec((shards, 1, span, 2 * FF), lambda e: (0, e, 0, 0)),
        scratch_shapes=row_scratch(len(pieces)),
        compiler_params=params(56, 1),
        cost_estimate=cost(4 * experts * rows * FF * MODEL_WIDTH, 35e6),
        name="in_grads",
    )(*pieces, gate_side, up_side)


def ring_kernel(wide, *refs):
    picks, pieces = refs[0], refs[1 : 1 + wide]
    arrived, out = refs[1 + wide : -1], refs[-1]
    rows = jnp.concatenate([piece[...] for piece in pieces], axis=0)
    total = dot_tn(picks[0], rows)
    if arrived:
        total = total + arrived[0][...].astype(f32)
    out[...] = total.astype(out.dtype)


def ring_rows(picks, level, pieces, arrived, last):
    _, many, token_rows = picks.shape
    tile = 512
    side = pl.BlockSpec((token_rows, tile), lambda n: (0, n))
    return pl.pallas_call(
        functools.partial(ring_kernel, len(pieces)),
        out_shape=jax.ShapeDtypeStruct((token_rows, MODEL_WIDTH), f32 if last else bf16),
        grid=(MODEL_WIDTH // tile,),
        in_specs=[pl.BlockSpec((1, many, token_rows), lambda n: (level, 0, 0))]
        + [pl.BlockSpec((p.shape[0], tile), lambda n: (0, n)) for p in pieces]
        + [side] * len(arrived),
        out_specs=side,
        compiler_params=params(48, 1),
        cost_estimate=cost(4 * many * token_rows * HALF, 8e6),
        name="ring_rows",
    )(picks, *pieces, *arrived)


def pick_kernel(picks, rows, own, away):
    per = own.shape[0]
    picked = dot_nn(picks[0], rows[...]).astype(bf16)
    own[...] = picked[:per]
    for r in range(away.shape[0]):
        away[r] = picked[(r + 1) * per : (r + 2) * per]


def pick_rows(picks, level, rows, wide):
    _, many, token_rows = picks.shape
    per = many // wide
    tile = 512
    return pl.pallas_call(
        pick_kernel,
        out_shape=(
            jax.ShapeDtypeStruct((per, MODEL_WIDTH), bf16),
            jax.ShapeDtypeStruct((wide - 1, per, MODEL_WIDTH), bf16),
        ),
        grid=(MODEL_WIDTH // tile,),
        in_specs=[
            pl.BlockSpec((1, many, token_rows), lambda n: (level, 0, 0)),
            pl.BlockSpec((token_rows, tile), lambda n: (0, n)),
        ],
        out_specs=(
            pl.BlockSpec((per, tile), lambda n: (0, n)),
            pl.BlockSpec((wide - 1, per, tile), lambda n: (0, 0, n)),
        ),
        compiler_params=params(32, 1),
        cost_estimate=cost(4 * many * token_rows * HALF, 5e6),
        name="pick_rows",
    )(picks, rows)


def weight_grad_kernel(rows, *refs):
    *grads, out = refs
    rows_t = rows[...].T
    at = 0
    for side in grads:
        if side.dtype == f32:
            out[:, at:] = side[...].T.astype(bf16)
        else:
            columns = side.shape[1]
            out[:, at : at + columns] = dot_nn(rows_t, side[...]).astype(bf16)
            at += columns


def weight_grads(rows, grads, extra=None):
    token_rows = rows.shape[0]
    tile = 384
    extras = [] if extra is None else [extra]
    columns = sum(g.shape[1] for g in grads) + sum(e.shape[0] for e in extras)
    return pl.pallas_call(
        weight_grad_kernel,
        out_shape=jax.ShapeDtypeStruct((MODEL_WIDTH, columns), bf16),
        grid=(MODEL_WIDTH // tile,),
        in_specs=[pl.BlockSpec((token_rows, tile), lambda n: (0, n))]
        + [pl.BlockSpec(g.shape, lambda n: (0, 0)) for g in grads]
        + [pl.BlockSpec((e.shape[0], tile), lambda n: (0, n)) for e in extras],
        out_specs=pl.BlockSpec((tile, columns), lambda n: (n, 0)),
        compiler_params=params(56, 1),
        cost_estimate=cost(2 * MODEL_WIDTH * token_rows * columns, 14e6),
        name="weight_grads",
    )(rows, *grads, *extras)


def adamw_update(weight, moment_one, moment_two, gradient, step_rate, decay_rate):
    first_new = BETA_ONE * moment_one + (1.0 - BETA_ONE) * gradient
    second_new = BETA_TWO * moment_two + (1.0 - BETA_TWO) * gradient * gradient
    first_hat = first_new / (1.0 - BETA_ONE**STEP)
    second_hat = second_new / (1.0 - BETA_TWO**STEP)
    weight_new = weight - step_rate * (
        first_hat / (jnp.sqrt(second_hat) + ADAM_EPS) + decay_rate * weight
    )
    return (weight_new, first_new, second_new)


def body(
    tokens,
    cotangent,
    routes,
    gains,
    gains_first,
    gains_second,
    query_weight,
    query_first,
    query_second,
    key_matrix,
    key_moment_first,
    key_moment_second,
    value_matrix,
    value_moment_first,
    value_moment_second,
    output_weight,
    output_first,
    output_second,
    router_weight,
    router_first,
    router_second,
    expert_in,
    in_first,
    in_second,
    expert_out,
    out_first,
    out_second,
):
    token_rows, top_count = routes.shape
    shards = lax.axis_size("fsdp")
    place = lax.axis_index("fsdp")
    groups = lax.axis_size("expert")
    group = lax.axis_index("expert")
    depth = DEPTH
    wide = groups // depth
    level, column = group // wide, group % wide
    experts_local = expert_in.shape[0]
    experts_all = experts_local * groups
    near = wide * experts_local
    shard_rows = query_weight.shape[0]

    def z_shift(value, by):
        return lax.ppermute(
            value,
            "expert",
            [(a * wide + b, (a + by) % depth * wide + b) for a in range(depth) for b in range(wide)],
        )

    def x_shift(value, by):
        return lax.ppermute(
            value,
            "expert",
            [(a * wide + b, a * wide + (b + by) % wide) for a in range(depth) for b in range(wide)],
        )

    def back_shift(value, by):
        pairs = [(a, a + by) for a in range(shards) if 0 <= a + by < shards]
        return lax.ppermute(value, "fsdp", pairs)

    def core_shift(value, by):
        return lax.ppermute(value, "fsdp", [(a, a // 2 * 2 + (a + by) % 2) for a in range(shards)])

    def y_shift(value, by):
        return lax.ppermute(value, "fsdp", [(a, (a + 2 * by) % shards) for a in range(shards)])

    def y_up(value, by):
        return lax.ppermute(value, "fsdp", [(a, a + 2 * by) for a in range(shards - 2 * by)])

    small = jnp.concatenate(
        [
            router_weight.astype(bf16),
            gains.T.astype(bf16),
            jnp.zeros((shard_rows, 128 - experts_all - 2), bf16),
        ],
        axis=1,
    )
    front_low = lax.all_gather(
        jnp.concatenate(
            [query_weight.astype(bf16), key_matrix.astype(bf16), value_matrix.astype(bf16), small], axis=1
        ),
        "fsdp",
        axis=0,
        tiled=True,
    )
    output_low = lax.all_gather(output_weight.astype(bf16), "fsdp", axis=0, tiled=True)
    qkv_low = front_low[:, :QKV]
    router_low = front_low[:, QKV : QKV + experts_all]
    gain_pair = front_low[:, QKV + experts_all : QKV + experts_all + 2].astype(f32).T
    gain_one, gain_two = gain_pair[0], gain_pair[1]

    routes_t = routes.T
    routes_of = jnp.stack([routes_t] + [z_shift(routes_t, i) for i in range(1, depth)])

    def expert_ids(at_level):
        columns = (column + jnp.arange(wide, dtype=jnp.int32)) % wide
        first_ids = (at_level * wide + columns) * experts_local
        return (first_ids[:, None] + jnp.arange(experts_local, dtype=jnp.int32)[None, :]).reshape(near)

    named = (routes_of[:, None] == expert_ids(level)[None, :, None, None]).astype(f32)
    chosen_here = jnp.sum(named, axis=2)
    earlier = (
        jnp.arange(token_rows, dtype=jnp.int32)[:, None] < jnp.arange(token_rows, dtype=jnp.int32)[None, :]
    ).astype(bf16)
    slots = dot_nn(chosen_here.reshape(depth * near, token_rows).astype(bf16), earlier).reshape(
        depth, near, token_rows
    )
    code = jnp.where(chosen_here > 0, slots.astype(jnp.int32), -1)
    picks = code[:, :, None, :] == jnp.arange(CAP, dtype=jnp.int32)[None, None, :, None]
    picks_low = picks.astype(bf16).reshape(depth, near * CAP, token_rows)

    def pick(rows, k):
        return pick_rows(picks_low, k, rows, wide)

    def swap(picked, *before):
        own, away = picked
        pairs = [own]
        for r in range(1, wide):
            pairs.append(x_shift(after(away[r - 1], pairs[1:], before), r))
        return pairs

    def order(swapped):
        return [swapped[k][r] for r in range(wide) for k in range(depth)]

    def swap_back(pieces, *before):
        steps = [None] * depth
        for m in range(depth):
            k = (m + 1) % depth
            steps[k] = [pieces[k]]
            for r in range(1, wide):
                piece = x_shift(after(pieces[r * depth + k], before), -r)
                steps[k].append(piece)
                if m % 2 == 0:
                    before = (piece,)
        return steps

    def ring_send(held):
        return [z_shift(held[-1], 1)]

    def ring_step(held, pieces, arrived=()):
        m = len(held)
        out = ring_rows(picks_low, (m + 1) % depth, pieces, arrived, m == depth - 1)
        if m == depth - 1:
            return out
        held.append(out)

    upstream = cotangent.astype(f32)
    level_one = z_shift(cotangent, 1)
    upstream_swapped = [swap(pick(cotangent, 0))]
    level_one = after(level_one, upstream_swapped)
    picked = pick(level_one, 1)
    upstream_swapped.append(swap(picked, upstream_swapped[-1]))

    inputs = tokens.astype(f32)
    scale_one = lax.rsqrt(jnp.mean(inputs * inputs, axis=1, keepdims=True) + NORM_EPS)
    normed_one = inputs * scale_one
    first_hidden = (normed_one * gain_one).astype(bf16)
    inverse = ROPE_BASE ** (-(jnp.arange(HEAD_SIZE // 2, dtype=f32) * 2.0 / HEAD_SIZE))
    places = (place * token_rows + jnp.arange(token_rows, dtype=jnp.int32)).astype(f32)
    angles = places[:, None] * inverse[None, :]
    half_cos, half_sin = jnp.cos(angles), jnp.sin(angles)
    cosine = jnp.concatenate([half_cos, half_cos], axis=1)
    sine = jnp.concatenate([-half_sin, half_sin], axis=1)

    def turn_keys(rows, sign):
        parts = []
        for h in range(KEY_VALUE_HEADS):
            piece = rows[:, h * HEAD_SIZE : (h + 1) * HEAD_SIZE]
            swapped = jnp.concatenate([piece[:, HEAD_SIZE // 2 :], piece[:, : HEAD_SIZE // 2]], axis=1)
            parts.append(piece * cosine + swapped * (sign * sine))
        return jnp.concatenate(parts, axis=1)

    pre = dot_nn(after(first_hidden, picked), qkv_low)
    keys_local = turn_keys(pre[:, MODEL_WIDTH : MODEL_WIDTH + KV], 1.0).astype(bf16)
    kv_local = jnp.concatenate([keys_local, pre[:, MODEL_WIDTH + KV :].astype(bf16)], axis=1)

    chips = shards // 2
    core = place % 2
    same = [kv_local] + [y_up(kv_local, s) for s in range(1, chips)]
    other = [core_shift(v, 1) for v in same]
    blocks = []
    for distance in range(shards):
        s = distance // 2
        if distance % 2 == 0:
            blocks.append(same[s])
        elif s + 1 < chips:
            blocks.append(jnp.where(core == 1, other[s], other[s + 1]))
        else:
            blocks.append(other[s])
    kv_blocks = jnp.stack(blocks)

    down_low = lax.all_gather(after(expert_out, kv_local).astype(bf16), "fsdp", axis=0)
    gate_up_low = lax.all_gather(after(expert_in, kv_local).astype(bf16), "fsdp", axis=0)

    level_two = after(z_shift(level_one, 1), kv_blocks)
    level_three = z_shift(level_two, 1)

    place_arg = place.astype(jnp.int32).reshape(1)
    attended, log_total, query_rows = attend(
        place_arg, pre, cosine, sine, after(kv_blocks, level_two)
    )
    residual = inputs + dot_nn(after(attended, level_three), output_low)
    scale_two = lax.rsqrt(jnp.mean(residual * residual, axis=1, keepdims=True) + NORM_EPS)
    normed_two = residual * scale_two
    hidden_two = (normed_two * gain_two).astype(bf16)

    upstream_swapped[1] = after(upstream_swapped[1], attended)
    upstream_swapped.append(swap(pick(after(level_two, attended), 2), upstream_swapped[1]))
    last_picked = pick(after(level_three, hidden_two), 3)

    levels = [hidden_two, z_shift(hidden_two, 1)]
    logits_t = lax.dot_general(
        router_low, hidden_two, (((0,), (1,)), ((), ())), preferred_element_type=f32
    )
    all_ids = jnp.arange(experts_all, dtype=jnp.int32)
    chosen_t = (routes_t[:, None, :] == all_ids[None, :, None]).astype(f32)
    gate_weights = jax.nn.softmax(jnp.sum(chosen_t * logits_t[None], axis=1), axis=0)
    gates_of = [gate_weights, z_shift(gate_weights, 1)]
    picked = pick(hidden_two, 0)
    hidden_swapped = [swap(picked, upstream_swapped[-1])]
    levels[1] = after(levels[1], picked)
    picked = pick(levels[1], 1)
    hidden_swapped.append(swap(picked, hidden_swapped[-1]))
    upstream_swapped.append(swap(last_picked, hidden_swapped[-1]))
    for k in range(2, depth):
        levels.append(after(z_shift(levels[-1], 1), picked, gates_of[1]))
        if k == depth - 1:
            upstream_pieces = order(after(upstream_swapped, levels[k - 1]))
            inner = inner_rows(upstream_pieces, down_low)
            gates_of[-1] = after(gates_of[-1], inner)
            levels[k] = after(levels[k], gates_of[-1])
        gates_of.append(z_shift(gates_of[-1], 1))
        picked = pick(levels[k], k)
        hidden_swapped.append(swap(picked, hidden_swapped[-1], upstream_swapped[-1]))
    gates_near = jnp.sum(named * jnp.stack(gates_of)[:, None], axis=2)
    row_gates = jnp.sum(jnp.where(picks, gates_near[:, :, None, :], 0.0), axis=3)
    row_gates = row_gates.reshape(depth, wide, experts_local, CAP)
    away_gates = [x_shift(row_gates[:, r], r) for r in range(1, wide)]
    hidden_swapped, away_gates = after((hidden_swapped, away_gates), levels[-1])
    hidden_pieces = order(hidden_swapped)
    row_gates = jnp.stack([row_gates[:, 0]] + away_gates)
    row_gates = row_gates.transpose(2, 0, 1, 3).reshape(experts_local, wide * depth * CAP, 1)

    scaled_hidden, gate_side, up_side, gate_dots, back_pieces = core_rows(
        hidden_pieces, gate_up_low, inner, row_gates
    )
    steps = swap_back(back_pieces)
    gate_dots = gate_dots.reshape(experts_local, wide, depth, CAP)
    away_dots = [x_shift(gate_dots[:, r], -r) for r in range(1, wide)]
    down_term = down_grads(upstream_pieces, scaled_hidden, shards)
    held = []
    ring_step(held, after(steps[1], down_term))
    out_part = lax.psum_scatter(after(down_term, held[0]), "fsdp", scatter_dimension=0)
    arrived = ring_send(held)
    in_term = in_grads(hidden_pieces, *after((gate_side, up_side), held[0]), shards)
    gate_dots = jnp.stack([gate_dots[:, 0]] + after(away_dots, in_term))
    gate_dots = gate_dots.transpose(2, 0, 1, 3).reshape(depth, near, CAP)
    token_dots = jnp.sum(jnp.where(picks, gate_dots[:, :, :, None], 0.0), axis=2)
    choice_dots = jnp.sum(named * token_dots[:, :, None, :], axis=1)
    lane = z_shift(choice_dots[1], 1)
    ring_step(held, after(steps[2], in_term, lane), arrived)
    in_part = lax.psum_scatter(after(in_term, held[1]), "fsdp", scatter_dimension=0)
    lane = z_shift(lane + choice_dots[2], 1)
    arrived = ring_send(held)
    results = result_rows(after(scaled_hidden, held[1]), down_low, len(back_pieces))
    ring_step(held, after(steps[3], results, lane), arrived)
    result_steps = swap_back(results, steps[0])
    lane = z_shift(lane + choice_dots[3], 1)
    arrived = ring_send(held)
    gate_grad = lane + choice_dots[0]
    picked_grad = gate_weights * (
        gate_grad - jnp.sum(gate_weights * gate_grad, axis=0, keepdims=True)
    )
    logit_grad_t = jnp.sum(chosen_t * picked_grad[:, None, :], axis=0).astype(bf16)
    router_term = dot_nn(logit_grad_t, hidden_two)
    hidden_back = ring_step(held, after(steps[0], router_term), arrived)
    hidden_two_grad = hidden_back + lax.dot_general(
        logit_grad_t, router_low, (((0,), (1,)), ((), ())), preferred_element_type=f32
    )

    gain_two_term = jnp.sum(hidden_two_grad * normed_two, axis=0)
    scaled_two = hidden_two_grad * gain_two
    residual_grad = upstream + scale_two * (
        scaled_two - normed_two * jnp.mean(scaled_two * normed_two, axis=1, keepdims=True)
    )
    branch_grad = residual_grad.astype(bf16)
    attended_grad = dot_nt(branch_grad, output_low).astype(bf16)
    result_held = []
    ring_step(result_held, after(result_steps[1], hidden_back))
    attended_grad = after(attended_grad, result_held[0], out_part)
    arrived = ring_send(result_held)
    pre_grad, key_back, value_back = attend_back(
        place_arg, query_rows, kv_blocks, attended, attended_grad, log_total, cosine, sine
    )

    def extra_rows(*terms):
        used = sum(t.shape[0] for t in terms)
        return jnp.concatenate(list(terms) + [jnp.zeros((128 - used, MODEL_WIDTH), f32)], axis=0)

    def send_parts(parts, index, shift):
        count = parts.shape[0]
        return [lax.dynamic_index_in_dim(parts, index, 0, keepdims=False)] + [
            shift(lax.dynamic_index_in_dim(parts, (index + s) % count, 0, keepdims=False), s)
            for s in range(1, count)
        ]

    def add_parts(parts):
        return functools.reduce(lambda total, part: total + part.astype(f32), parts[1:], parts[0].astype(f32)).astype(bf16)

    def join(part, index, count, shift):
        whole = jnp.zeros((count,) + part.shape, part.dtype)
        for s in range(count):
            piece = shift(part, s) if s else part
            whole = lax.dynamic_update_index_in_dim(whole, piece, (index - s) % count, 0)
        return whole

    def core_parts(terms):
        parts = terms.reshape(chips, 2, shard_rows, terms.shape[1]).transpose(1, 0, 2, 3)
        return send_parts(parts, core, core_shift)

    def y_parts(part):
        return send_parts(part, place // 2, y_shift)

    def x_parts(part):
        return send_parts(part.reshape(wide, shard_rows // wide, part.shape[1]), column, x_shift)

    def z_total(part):
        columns = part.shape[1]
        part = add_parts(send_parts(part.reshape(depth, shard_rows // wide // depth, columns), level, z_shift))
        part = join(part, level, depth, z_shift).reshape(shard_rows // wide, columns)
        return join(part, column, wide, x_shift).reshape(shard_rows, columns).astype(f32)

    kv_back = jnp.concatenate([key_back, value_back], axis=2)
    none = jnp.zeros_like(kv_back[:1])
    mate = jnp.where(core == 1, kv_back[1::2], jnp.concatenate([none, kv_back[1:-1:2]], axis=0))
    mate = core_shift(mate, 1)
    kv_chip = kv_back[0::2].astype(f32) + mate.astype(f32)
    kv_low = kv_chip.astype(bf16)
    kv_parts = [
        lax.ppermute(kv_low[s], "fsdp", [(a + 2 * s, a) for a in range(shards - 2 * s)]) for s in range(1, chips)
    ]
    kv_grad = functools.reduce(lambda total, part: total + part.astype(f32), kv_parts, kv_chip[0])
    key_pre_grad = turn_keys(kv_grad[:, :KV], -1.0)
    kv_pre_grad = jnp.concatenate([key_pre_grad, kv_grad[:, KV:]], axis=1).astype(bf16)

    front_terms = weight_grads(first_hidden, [pre_grad, kv_pre_grad])
    front_part = lax.psum_scatter(after(front_terms, in_part), "fsdp", scatter_dimension=0, tiled=True)
    front_sum = lax.psum(front_part, "expert").astype(f32)

    ring_step(result_held, after(result_steps[2], front_terms), arrived)
    arrived = ring_send(result_held)
    pre_late, kv_late = after((pre_grad, kv_pre_grad), result_held[1])
    hidden_one_grad = dot_nt(pre_late, qkv_low[:, :MODEL_WIDTH]) + dot_nt(kv_late, qkv_low[:, MODEL_WIDTH:])
    gain_one_term = jnp.sum(hidden_one_grad * normed_one, axis=0)
    scaled_one = hidden_one_grad * gain_one
    input_grad = (
        residual_grad
        + scale_one
        * (scaled_one - normed_one * jnp.mean(scaled_one * normed_one, axis=1, keepdims=True))
    ).astype(bf16)
    back_terms = weight_grads(
        attended, [branch_grad], extra_rows(router_term, gain_one_term[None], gain_two_term[None])
    )
    back_parts = core_parts(back_terms)
    ring_step(result_held, after(result_steps[3], back_terms), arrived)
    arrived = ring_send(result_held)
    out_state = adamw_update(
        expert_out,
        out_first,
        out_second,
        after(out_part, result_held[2]).astype(f32),
        0.5 / math.sqrt(FF // 8),
        DECAY,
    )
    back_part = add_parts(after(back_parts, out_state))
    back_parts = y_parts(back_part)
    in_state = adamw_update(
        expert_in,
        in_first,
        in_second,
        after(in_part, back_part).astype(f32),
        0.5 / math.sqrt(MODEL_WIDTH),
        DECAY,
    )
    moe_out = ring_step(result_held, after(result_steps[0], in_state), arrived)
    layer_out = (residual + moe_out).astype(bf16)
    back_sum = z_total(add_parts(x_parts(add_parts(after(back_parts, layer_out)))))
    output_sum = back_sum[:, :MODEL_WIDTH]
    router_sum = back_sum[:, MODEL_WIDTH : MODEL_WIDTH + experts_all]
    query_sum = front_sum[:, :MODEL_WIDTH]
    key_sum = front_sum[:, MODEL_WIDTH : MODEL_WIDTH + KV]
    value_sum = front_sum[:, MODEL_WIDTH + KV : QKV]
    at = MODEL_WIDTH + experts_all
    gain_sum = back_sum[:, at : at + 2].T

    rate = 0.5 / math.sqrt(MODEL_WIDTH // 2)
    return (
        layer_out,
        input_grad,
        *adamw_update(gains, gains_first, gains_second, gain_sum, GAIN_RATE, 0.0),
        *adamw_update(query_weight, query_first, query_second, query_sum, rate, DECAY),
        *adamw_update(key_matrix, key_moment_first, key_moment_second, key_sum, rate, DECAY),
        *adamw_update(
            value_matrix,
            value_moment_first,
            value_moment_second,
            value_sum,
            0.5 / math.sqrt(MODEL_WIDTH),
            DECAY,
        ),
        *adamw_update(
            output_weight, output_first, output_second, output_sum, 0.5 / math.sqrt(MODEL_WIDTH // 32), DECAY
        ),
        *adamw_update(
            router_weight, router_first, router_second, router_sum, 0.5 / math.sqrt(4 * MODEL_WIDTH), DECAY
        ),
        *in_state,
        *out_state,
    )


def solution(mesh):
    rows = P(("expert", "fsdp"), None)
    gains = P(None, "fsdp")
    matrix = P("fsdp", None)
    wide = P("expert", "fsdp", None)
    tall = P("expert", None, "fsdp")
    return jax.shard_map(
        body,
        mesh=mesh,
        in_specs=(rows,) * 3 + (gains,) * 3 + (matrix,) * 15 + (wide,) * 3 + (tall,) * 3,
        out_specs=(rows,) * 2 + (gains,) * 3 + (matrix,) * 15 + (wide,) * 3 + (tall,) * 3,
        check_vma=False,
    )
```

```python
import functools
import math

import jax
import jax.numpy as jnp
from jax import lax
from jax.experimental import pallas as pl
from jax.experimental.pallas import tpu as pltpu
from jax.sharding import PartitionSpec as P

MODEL_WIDTH = 1536
QUERY_HEADS = 12
KEY_VALUE_HEADS = 2
HEAD_SIZE = 128
GROUP = QUERY_HEADS // KEY_VALUE_HEADS
FF = 768
STEP = 10
CAP = 80
DEPTH = 4
HALF = MODEL_WIDTH // 2
KV = KEY_VALUE_HEADS * HEAD_SIZE
QKV = MODEL_WIDTH + 2 * KV


NORM_EPS = 1e-05
ROPE_BASE = 10000.0
BETA_ONE = 0.9
BETA_TWO = 0.95
ADAM_EPS = 1e-08
DECAY = 0.1
GAIN_RATE = 0.8
MASKED = -1e30
LOG2E = 1.0 / math.log(2.0)
SCORE_SCALE = 1.0 / math.sqrt(HEAD_SIZE)

f32 = jnp.float32
bf16 = jnp.bfloat16


def dot_nn(left, right):
    return lax.dot_general(left, right, (((1,), (0,)), ((), ())), preferred_element_type=f32)


def dot_nt(left, right):
    return lax.dot_general(left, right, (((1,), (1,)), ((), ())), preferred_element_type=f32)


def dot_tn(left, right):
    return lax.dot_general(left, right, (((0,), (0,)), ((), ())), preferred_element_type=f32)


def after(value, *others):
    return lax.optimization_barrier((value, others))[0]


def params(megabytes, axes):
    return pltpu.CompilerParams(
        vmem_limit_bytes=megabytes * 1024 * 1024, dimension_semantics=("arbitrary",) * axes
    )


def cost(flops, nbytes, trans=0):
    return pl.CostEstimate(flops=int(flops), bytes_accessed=int(nbytes), transcendentals=0)


def causal(score_t):
    key_place = lax.broadcasted_iota(jnp.int32, score_t.shape, 0)
    query_place = lax.broadcasted_iota(jnp.int32, score_t.shape, 1)
    return key_place <= query_place


def attend_kernel(place, pre, cosine, sine, keys, values, out, log_total, turned):
    rows = pre[...]
    query = rows * cosine[...] + pltpu.roll(rows, HEAD_SIZE // 2, 1) * sine[...]
    turned[...] = query.astype(bf16)
    query_t = query.T.astype(bf16)
    factor = SCORE_SCALE * LOG2E

    score = dot_nn(keys[0], query_t) * factor
    score = jnp.where(causal(score), score, MASKED)
    biggest = jnp.max(score, axis=0, keepdims=True)
    weight = jnp.exp2(score - biggest)
    total = jnp.sum(weight, axis=0, keepdims=True)
    acc = dot_nn(values[0].T, weight.astype(bf16))

    def step(back, carry):
        biggest, total, acc = carry
        score = dot_nn(keys[back], query_t) * factor
        larger = jnp.maximum(biggest, jnp.max(score, axis=0, keepdims=True))
        weight = jnp.exp2(score - larger)
        shrink = jnp.exp2(biggest - larger)
        total = total * shrink + jnp.sum(weight, axis=0, keepdims=True)
        acc = acc * shrink + dot_nn(values[back].T, weight.astype(bf16))
        return larger, total, acc

    biggest, total, acc = lax.fori_loop(1, place[0] + 1, step, (biggest, total, acc))
    out[...] = (acc / total).T.astype(bf16)
    log_total[0] = biggest + jnp.log(total) * LOG2E


def attend(place, pre, cosine, sine, kv_blocks):
    token_rows = pre.shape[0]
    blocks = kv_blocks.shape[0]
    width = (token_rows, HEAD_SIZE)
    many = (blocks, token_rows, HEAD_SIZE)
    return pl.pallas_call(
        attend_kernel,
        out_shape=(
            jax.ShapeDtypeStruct((token_rows, MODEL_WIDTH), bf16),
            jax.ShapeDtypeStruct((QUERY_HEADS, 1, token_rows), f32),
            jax.ShapeDtypeStruct((token_rows, MODEL_WIDTH), bf16),
        ),
        grid_spec=pltpu.PrefetchScalarGridSpec(
            num_scalar_prefetch=1,
            grid=(QUERY_HEADS,),
            in_specs=[
                pl.BlockSpec(width, lambda h, p: (0, h)),
                pl.BlockSpec(width, lambda h, p: (0, 0)),
                pl.BlockSpec(width, lambda h, p: (0, 0)),
                pl.BlockSpec(many, lambda h, p: (0, 0, h // GROUP)),
                pl.BlockSpec(many, lambda h, p: (0, 0, KEY_VALUE_HEADS + h // GROUP)),
            ],
            out_specs=(
                pl.BlockSpec(width, lambda h, p: (0, h)),
                pl.BlockSpec((1, 1, token_rows), lambda h, p: (h, 0, 0)),
                pl.BlockSpec(width, lambda h, p: (0, h)),
            ),
        ),
        compiler_params=params(56, 1),
        cost_estimate=cost(1e9, 1e6),
        name="attend",
    )(place, pre, cosine, sine, kv_blocks, kv_blocks)


def attend_back_kernel(
    place, query, keys, values, out, out_grad, log_total, cosine, sine, pre_grad, key_grad, value_grad, key_acc, value_acc
):
    head = pl.program_id(0)

    @pl.when(head % GROUP == 0)
    def _():
        key_acc[...] = jnp.zeros_like(key_acc)
        value_acc[...] = jnp.zeros_like(value_acc)

    factor = SCORE_SCALE * LOG2E
    query_rows = query[...]
    grad_rows = out_grad[...]
    query_t = query_rows.astype(f32).T.astype(bf16)
    grad_t32 = grad_rows.astype(f32).T
    grad_t = grad_t32.astype(bf16)
    row_dot = jnp.sum(out[...].astype(f32).T * grad_t32, axis=0, keepdims=True)
    level = log_total[0]

    def block(back, masked):
        key = keys[back]
        score = dot_nn(key, query_t) * factor - level
        weight = jnp.exp2(score)
        if masked:
            weight = jnp.where(causal(weight), weight, 0.0)
        value_acc[back] += dot_nn(weight.astype(bf16), grad_rows)
        prob_grad = dot_nn(values[back], grad_t)
        score_grad = (weight * (prob_grad - row_dot)).astype(bf16)
        key_acc[back] += dot_nn(score_grad, query_rows)
        return dot_nn(key.T, score_grad)

    query_grad = block(0, True)
    query_grad = lax.fori_loop(1, place[0] + 1, lambda b, acc: acc + block(b, False), query_grad)
    rows = query_grad.T * SCORE_SCALE
    pre_grad[...] = (rows * cosine[...] - pltpu.roll(rows, HEAD_SIZE // 2, 1) * sine[...]).astype(bf16)

    @pl.when(head % GROUP == GROUP - 1)
    def _():
        key_grad[...] = (key_acc[...] * SCORE_SCALE).astype(bf16)
        value_grad[...] = value_acc[...].astype(bf16)


def attend_back(place, query, kv_blocks, out, out_grad, log_total, cosine, sine):
    token_rows = query.shape[0]
    blocks = kv_blocks.shape[0]
    width = (token_rows, HEAD_SIZE)
    many = (blocks, token_rows, HEAD_SIZE)
    return pl.pallas_call(
        attend_back_kernel,
        out_shape=(
            jax.ShapeDtypeStruct((token_rows, MODEL_WIDTH), bf16),
            jax.ShapeDtypeStruct((blocks, token_rows, KV), bf16),
            jax.ShapeDtypeStruct((blocks, token_rows, KV), bf16),
        ),
        grid_spec=pltpu.PrefetchScalarGridSpec(
            num_scalar_prefetch=1,
            grid=(QUERY_HEADS,),
            in_specs=[
                pl.BlockSpec(width, lambda h, p: (0, h)),
                pl.BlockSpec(many, lambda h, p: (0, 0, h // GROUP)),
                pl.BlockSpec(many, lambda h, p: (0, 0, KEY_VALUE_HEADS + h // GROUP)),
                pl.BlockSpec(width, lambda h, p: (0, h)),
                pl.BlockSpec(width, lambda h, p: (0, h)),
                pl.BlockSpec((1, 1, token_rows), lambda h, p: (h, 0, 0)),
                pl.BlockSpec(width, lambda h, p: (0, 0)),
                pl.BlockSpec(width, lambda h, p: (0, 0)),
            ],
            out_specs=(
                pl.BlockSpec(width, lambda h, p: (0, h)),
                pl.BlockSpec(many, lambda h, p: (0, 0, h // GROUP)),
                pl.BlockSpec(many, lambda h, p: (0, 0, h // GROUP)),
            ),
            scratch_shapes=[pltpu.VMEM(many, f32), pltpu.VMEM(many, f32)],
        ),
        compiler_params=params(56, 1),
        cost_estimate=cost(1e9, 1e6),
        name="attend_back",
    )(place, query, kv_blocks, kv_blocks, out, out_grad, log_total, cosine, sine)


def gather_rows(pieces, rows):
    for p, piece in enumerate(pieces):
        rows[p * CAP : (p + 1) * CAP] = piece[...]


def scatter_rows(rows, pieces, at, span):
    low = rows.astype(bf16)
    for p, piece in enumerate(pieces):
        piece[:, at : at + span] = low[p * CAP : (p + 1) * CAP]


def piece_spec():
    return pl.BlockSpec((CAP, MODEL_WIDTH), lambda e, *_: (e, 0))


def row_scratch(count):
    return [pltpu.VMEM((count * CAP, MODEL_WIDTH), bf16)]


def inner_kernel(count, *refs):
    pieces, (down, inner, rows) = refs[:count], refs[count:]
    gather_rows(pieces, rows)
    shards, span = down.shape[0], down.shape[3]
    acc = None
    for c in range(shards):
        term = dot_nt(rows[:, c * span : (c + 1) * span], down[c, 0])
        acc = term if acc is None else acc + term
    inner[0] = acc.astype(bf16)


def inner_rows(pieces, down):
    shards, experts, _, span = down.shape
    rows = len(pieces) * CAP
    return pl.pallas_call(
        functools.partial(inner_kernel, len(pieces)),
        out_shape=jax.ShapeDtypeStruct((experts, rows, FF), bf16),
        grid=(experts,),
        in_specs=[piece_spec()] * len(pieces) + [pl.BlockSpec((shards, 1, FF, span), lambda e: (0, e, 0, 0))],
        out_specs=pl.BlockSpec((1, rows, FF), lambda e: (e, 0, 0)),
        scratch_shapes=row_scratch(len(pieces)),
        compiler_params=params(56, 1),
        cost_estimate=cost(2 * experts * rows * FF * MODEL_WIDTH, 20e6),
        name="inner_rows",
    )(*pieces, down)


def core_kernel(count, *refs):
    pieces, refs = refs[:count], refs[count:]
    gate_up, inner, weight, scaled, gate_side, up_side, gate_dots = refs[:7]
    back, (rows,) = refs[7 : 7 + count], refs[7 + count :]
    gather_rows(pieces, rows)
    span = gate_up.shape[2]
    tile = 256
    factor = weight[0]
    dots = None

    def product(at):
        return dot_nn(rows[...], gate_up[:, 0, :, at : at + tile].reshape(MODEL_WIDTH, tile))

    for n in range(FF // tile):
        at = n * tile
        gate_pre = product(at)
        up_part = product(FF + at)
        sigmoid = 1.0 / (1.0 + jnp.exp(-gate_pre))
        silu = gate_pre * sigmoid
        hidden = silu * up_part
        raw = inner[0, :, at : at + tile].astype(f32)
        part = jnp.sum(raw * hidden, axis=1, keepdims=True)
        dots = part if dots is None else dots + part
        scaled[0, :, at : at + tile] = (hidden * factor).astype(bf16)
        raw = raw * factor
        gate_side[0, :, at : at + tile] = (raw * up_part * (sigmoid + silu * (1.0 - sigmoid))).astype(bf16)
        up_side[0, :, at : at + tile] = (raw * silu).astype(bf16)
    gate_dots[0] = dots

    width = 384
    group = width // span
    for chunk in range(MODEL_WIDTH // width):
        block = gate_up[chunk * group : (chunk + 1) * group, 0].reshape(width, 2 * FF)
        grads = dot_nt(gate_side[0], block[:, :FF]) + dot_nt(up_side[0], block[:, FF:])
        scatter_rows(grads, back, chunk * width, width)


def core_rows(pieces, gate_up, inner, weight):
    count = len(pieces)
    shards, experts, span, _ = gate_up.shape
    rows = count * CAP
    whole = pl.BlockSpec((1, rows, FF), lambda e: (e, 0, 0))
    column = pl.BlockSpec((1, rows, 1), lambda e: (e, 0, 0))
    low = jax.ShapeDtypeStruct((experts, rows, FF), bf16)
    out = pl.pallas_call(
        functools.partial(core_kernel, count),
        out_shape=(low, low, low, jax.ShapeDtypeStruct((experts, rows, 1), f32))
        + (jax.ShapeDtypeStruct(pieces[0].shape, bf16),) * count,
        grid=(experts,),
        in_specs=[piece_spec()] * count
        + [pl.BlockSpec((shards, 1, span, 2 * FF), lambda e: (0, e, 0, 0)), whole, column],
        out_specs=(whole, whole, whole, column) + (piece_spec(),) * count,
        scratch_shapes=row_scratch(len(pieces)),
        compiler_params=params(60, 1),
        cost_estimate=cost(8 * experts * rows * FF * MODEL_WIDTH, 60e6),
        name="core_rows",
    )(*pieces, gate_up, inner, weight)
    return out[0], out[1], out[2], out[3], list(out[4:])


def result_kernel(scaled, down, *pieces):
    width = 384
    shards, span = down.shape[0], down.shape[3]
    group = width // span
    rows = scaled[0]
    for chunk in range(MODEL_WIDTH // width):
        parts = [down[c, 0] for c in range(chunk * group, (chunk + 1) * group)]
        block = parts[0] if group == 1 else jnp.concatenate(parts, axis=1)
        scatter_rows(dot_nn(rows, block), pieces, chunk * width, width)


def result_rows(scaled, down, count):
    experts, rows, _ = scaled.shape
    shards, _, _, span = down.shape
    return list(
        pl.pallas_call(
            result_kernel,
            out_shape=(jax.ShapeDtypeStruct((experts * CAP, MODEL_WIDTH), bf16),) * count,
            grid=(experts,),
            in_specs=[
                pl.BlockSpec((1, rows, FF), lambda e: (e, 0, 0)),
                pl.BlockSpec((shards, 1, FF, span), lambda e: (0, e, 0, 0)),
            ],
            out_specs=(piece_spec(),) * count,
            compiler_params=params(56, 1),
            cost_estimate=cost(2 * experts * rows * FF * MODEL_WIDTH, 22e6),
            name="result_rows",
        )(scaled, down)
    )


def keep_and_send(core, pair, mine, theirs):
    first, second = (p.astype(bf16) for p in pair)
    mine(jnp.where(core == 0, first, second))
    theirs(jnp.where(core == 0, second, first))


def down_grad_kernel(count, core, *refs):
    pieces, (scaled, mine, theirs, rows) = refs[:count], refs[count:]
    gather_rows(pieces, rows)
    chips, span = mine.shape[0], mine.shape[3]
    scaled_t = scaled[0].T
    for y in range(chips):
        pair = [
            dot_nn(scaled_t, rows[:, c * span : (c + 1) * span]) for c in (2 * y, 2 * y + 1)
        ]
        keep_and_send(
            core[0],
            pair,
            functools.partial(mine.__setitem__, (y, 0)),
            functools.partial(theirs.__setitem__, (y, 0)),
        )


def in_grad_kernel(count, core, *refs):
    pieces, (gate_side, up_side, mine, theirs, rows) = refs[:count], refs[count:]
    gather_rows(pieces, rows)
    chips, span = mine.shape[0], mine.shape[2]
    rows_t = rows[...].T
    for y in range(chips):
        for side, at in ((gate_side, 0), (up_side, FF)):
            pair = [dot_nn(rows_t[c * span : (c + 1) * span], side[0]) for c in (2 * y, 2 * y + 1)]
            where = (y, 0, slice(None), slice(at, at + FF))
            keep_and_send(
                core[0],
                pair,
                functools.partial(mine.__setitem__, where),
                functools.partial(theirs.__setitem__, where),
            )


def grads_by_core(kernel, name, core, pieces, sides, shape):
    experts, rows, _ = sides[0].shape
    count = len(pieces)
    out = jax.ShapeDtypeStruct(shape, bf16)
    whole = pl.BlockSpec((1, rows, FF), lambda e, *_: (e, 0, 0))
    block = pl.BlockSpec((shape[0], 1, shape[2], shape[3]), lambda e, *_: (0, e, 0, 0))
    return pl.pallas_call(
        functools.partial(kernel, count),
        out_shape=(out, out),
        grid_spec=pltpu.PrefetchScalarGridSpec(
            num_scalar_prefetch=1,
            grid=(experts,),
            in_specs=[piece_spec()] * count + [whole] * len(sides),
            out_specs=(block, block),
            scratch_shapes=row_scratch(count),
        ),
        compiler_params=params(56, 1),
        cost_estimate=cost(2 * len(sides) * experts * rows * FF * MODEL_WIDTH, 25e6),
        name=name,
    )(core, *pieces, *sides)


def down_grads(core, pieces, scaled, shards):
    shape = (shards // 2, scaled.shape[0], FF, MODEL_WIDTH // shards)
    return grads_by_core(down_grad_kernel, "down_grads", core, pieces, [scaled], shape)


def in_grads(core, pieces, gate_side, up_side, shards):
    shape = (shards // 2, gate_side.shape[0], MODEL_WIDTH // shards, 2 * FF)
    return grads_by_core(in_grad_kernel, "in_grads", core, pieces, [gate_side, up_side], shape)


def ring_kernel(wide, *refs):
    picks, pieces = refs[0], refs[1 : 1 + wide]
    arrived, out = refs[1 + wide : -1], refs[-1]
    rows = jnp.concatenate([piece[...] for piece in pieces], axis=0)
    total = dot_tn(picks[0], rows)
    if arrived:
        total = total + arrived[0][...].astype(f32)
    out[...] = total.astype(out.dtype)


def ring_rows(picks, level, pieces, arrived, last):
    _, many, token_rows = picks.shape
    tile = 512
    side = pl.BlockSpec((token_rows, tile), lambda n: (0, n))
    return pl.pallas_call(
        functools.partial(ring_kernel, len(pieces)),
        out_shape=jax.ShapeDtypeStruct((token_rows, MODEL_WIDTH), f32 if last else bf16),
        grid=(MODEL_WIDTH // tile,),
        in_specs=[pl.BlockSpec((1, many, token_rows), lambda n: (level, 0, 0))]
        + [pl.BlockSpec((p.shape[0], tile), lambda n: (0, n)) for p in pieces]
        + [side] * len(arrived),
        out_specs=side,
        compiler_params=params(48, 1),
        cost_estimate=cost(4 * many * token_rows * HALF, 8e6),
        name="ring_rows",
    )(picks, *pieces, *arrived)


def pick_kernel(picks, rows, own, away):
    per = own.shape[0]
    picked = dot_nn(picks[0], rows[...]).astype(bf16)
    own[...] = picked[:per]
    for r in range(away.shape[0]):
        away[r] = picked[(r + 1) * per : (r + 2) * per]


def pick_rows(picks, level, rows, wide):
    _, many, token_rows = picks.shape
    per = many // wide
    tile = 512
    return pl.pallas_call(
        pick_kernel,
        out_shape=(
            jax.ShapeDtypeStruct((per, MODEL_WIDTH), bf16),
            jax.ShapeDtypeStruct((wide - 1, per, MODEL_WIDTH), bf16),
        ),
        grid=(MODEL_WIDTH // tile,),
        in_specs=[
            pl.BlockSpec((1, many, token_rows), lambda n: (level, 0, 0)),
            pl.BlockSpec((token_rows, tile), lambda n: (0, n)),
        ],
        out_specs=(
            pl.BlockSpec((per, tile), lambda n: (0, n)),
            pl.BlockSpec((wide - 1, per, tile), lambda n: (0, 0, n)),
        ),
        compiler_params=params(32, 1),
        cost_estimate=cost(4 * many * token_rows * HALF, 5e6),
        name="pick_rows",
    )(picks, rows)


def weight_grad_kernel(core, rows, *refs):
    *grads, mine, theirs = refs
    span = mine.shape[1]
    rows_t = rows[...].T
    at = 0
    for side in grads:
        columns = side.shape[1]
        pair = [dot_nn(rows_t[c * span : (c + 1) * span], side[...]) for c in range(2)]
        where = (0, slice(None), slice(at, at + columns))
        keep_and_send(
            core[0],
            pair,
            functools.partial(mine.__setitem__, where),
            functools.partial(theirs.__setitem__, where),
        )
        at += columns


def weight_grads(core, rows, grads, shards):
    token_rows = rows.shape[0]
    span = MODEL_WIDTH // shards
    columns = sum(g.shape[1] for g in grads)
    out = jax.ShapeDtypeStruct((shards // 2, span, columns), bf16)
    block = pl.BlockSpec((1, span, columns), lambda n, c: (n, 0, 0))
    return pl.pallas_call(
        weight_grad_kernel,
        out_shape=(out, out),
        grid_spec=pltpu.PrefetchScalarGridSpec(
            num_scalar_prefetch=1,
            grid=(shards // 2,),
            in_specs=[pl.BlockSpec((token_rows, 2 * span), lambda n, c: (0, n))]
            + [pl.BlockSpec(g.shape, lambda n, c: (0, 0)) for g in grads],
            out_specs=(block, block),
        ),
        compiler_params=params(56, 1),
        cost_estimate=cost(2 * MODEL_WIDTH * token_rows * columns, 14e6),
        name="weight_grads",
    )(core, rows, *grads)


def adamw_update(weight, moment_one, moment_two, gradient, step_rate, decay_rate):
    first_new = BETA_ONE * moment_one + (1.0 - BETA_ONE) * gradient
    second_new = BETA_TWO * moment_two + (1.0 - BETA_TWO) * gradient * gradient
    first_hat = first_new / (1.0 - BETA_ONE**STEP)
    second_hat = second_new / (1.0 - BETA_TWO**STEP)
    weight_new = weight - step_rate * (
        first_hat / (jnp.sqrt(second_hat) + ADAM_EPS) + decay_rate * weight
    )
    return (weight_new, first_new, second_new)


def body(
    tokens,
    cotangent,
    routes,
    gains,
    gains_first,
    gains_second,
    query_weight,
    query_first,
    query_second,
    key_matrix,
    key_moment_first,
    key_moment_second,
    value_matrix,
    value_moment_first,
    value_moment_second,
    output_weight,
    output_first,
    output_second,
    router_weight,
    router_first,
    router_second,
    expert_in,
    in_first,
    in_second,
    expert_out,
    out_first,
    out_second,
):
    token_rows, top_count = routes.shape
    shards = lax.axis_size("fsdp")
    place = lax.axis_index("fsdp")
    groups = lax.axis_size("expert")
    group = lax.axis_index("expert")
    depth = DEPTH
    wide = groups // depth
    level, column = group // wide, group % wide
    experts_local = expert_in.shape[0]
    experts_all = experts_local * groups
    near = wide * experts_local
    shard_rows = query_weight.shape[0]

    def z_shift(value, by):
        return lax.ppermute(
            value,
            "expert",
            [(a * wide + b, (a + by) % depth * wide + b) for a in range(depth) for b in range(wide)],
        )

    def x_shift(value, by):
        return lax.ppermute(
            value,
            "expert",
            [(a * wide + b, a * wide + (b + by) % wide) for a in range(depth) for b in range(wide)],
        )

    def back_shift(value, by):
        pairs = [(a, a + by) for a in range(shards) if 0 <= a + by < shards]
        return lax.ppermute(value, "fsdp", pairs)

    chips = shards // 2
    chip, core = place // 2, place % 2

    def core_shift(value, by):
        return lax.ppermute(value, "fsdp", [(a, a // 2 * 2 + (a + by) % 2) for a in range(shards)])

    def y_shift(value, by):
        return lax.ppermute(value, "fsdp", [(a, (a + 2 * by) % shards) for a in range(shards)])

    def y_up(value, by):
        return lax.ppermute(value, "fsdp", [(a, a + 2 * by) for a in range(shards - 2 * by)])

    small = jnp.concatenate(
        [
            router_weight.astype(bf16),
            gains.T.astype(bf16),
            jnp.zeros((shard_rows, 128 - experts_all - 2), bf16),
        ],
        axis=1,
    )
    front_low = lax.all_gather(
        jnp.concatenate(
            [query_weight.astype(bf16), key_matrix.astype(bf16), value_matrix.astype(bf16), small], axis=1
        ),
        "fsdp",
        axis=0,
        tiled=True,
    )
    output_low = lax.all_gather(output_weight.astype(bf16), "fsdp", axis=0, tiled=True)
    qkv_low = front_low[:, :QKV]
    router_low = front_low[:, QKV : QKV + experts_all]
    gain_pair = front_low[:, QKV + experts_all : QKV + experts_all + 2].astype(f32).T
    gain_one, gain_two = gain_pair[0], gain_pair[1]

    routes_t = routes.T
    routes_of = jnp.stack([routes_t] + [z_shift(routes_t, i) for i in range(1, depth)])

    def expert_ids(at_level):
        columns = (column + jnp.arange(wide, dtype=jnp.int32)) % wide
        first_ids = (at_level * wide + columns) * experts_local
        return (first_ids[:, None] + jnp.arange(experts_local, dtype=jnp.int32)[None, :]).reshape(near)

    named = (routes_of[:, None] == expert_ids(level)[None, :, None, None]).astype(f32)
    chosen_here = jnp.sum(named, axis=2)
    earlier = (
        jnp.arange(token_rows, dtype=jnp.int32)[:, None] < jnp.arange(token_rows, dtype=jnp.int32)[None, :]
    ).astype(bf16)
    slots = dot_nn(chosen_here.reshape(depth * near, token_rows).astype(bf16), earlier).reshape(
        depth, near, token_rows
    )
    code = jnp.where(chosen_here > 0, slots.astype(jnp.int32), -1)
    picks = code[:, :, None, :] == jnp.arange(CAP, dtype=jnp.int32)[None, None, :, None]
    picks_low = picks.astype(bf16).reshape(depth, near * CAP, token_rows)

    def pick(rows, k):
        return pick_rows(picks_low, k, rows, wide)

    def swap(picked, *before):
        own, away = picked
        pairs = [own]
        for r in range(1, wide):
            pairs.append(x_shift(after(away[r - 1], pairs[1:], before), r))
        return pairs

    def order(swapped):
        return [swapped[k][r] for r in range(wide) for k in range(depth)]

    def swap_back(pieces, *before):
        steps = [None] * depth
        for m in range(depth):
            k = (m + 1) % depth
            steps[k] = [pieces[k]]
            for r in range(1, wide):
                piece = x_shift(after(pieces[r * depth + k], before), -r)
                steps[k].append(piece)
                if m % 2 == 0:
                    before = (piece,)
        return steps

    def chip_sum(mine, mate, chip):
        return lax.dynamic_index_in_dim(mine, chip, 0, keepdims=False).astype(
            f32
        ) + lax.dynamic_index_in_dim(mate, chip, 0, keepdims=False).astype(f32)

    def chip_low(mine, mate):
        return [chip_sum(mine, mate, (chip + s) % chips).astype(bf16) for s in range(1, chips)]

    def chip_send(low):
        return [y_shift(part, s) for s, part in enumerate(low, 1)]

    def chip_total(mine, mate, sent):
        return functools.reduce(lambda total, part: total + part.astype(f32), sent, chip_sum(mine, mate, chip))

    def ring_send(held):
        return [z_shift(held[-1], 1)]

    def ring_step(held, pieces, arrived=()):
        m = len(held)
        out = ring_rows(picks_low, (m + 1) % depth, pieces, arrived, m == depth - 1)
        if m == depth - 1:
            return out
        held.append(out)

    upstream = cotangent.astype(f32)
    level_one = z_shift(cotangent, 1)
    upstream_swapped = [swap(pick(cotangent, 0))]
    level_one = after(level_one, upstream_swapped)
    picked = pick(level_one, 1)
    upstream_swapped.append(swap(picked, upstream_swapped[-1]))

    inputs = tokens.astype(f32)
    scale_one = lax.rsqrt(jnp.mean(inputs * inputs, axis=1, keepdims=True) + NORM_EPS)
    normed_one = inputs * scale_one
    first_hidden = (normed_one * gain_one).astype(bf16)
    inverse = ROPE_BASE ** (-(jnp.arange(HEAD_SIZE // 2, dtype=f32) * 2.0 / HEAD_SIZE))
    places = (place * token_rows + jnp.arange(token_rows, dtype=jnp.int32)).astype(f32)
    angles = places[:, None] * inverse[None, :]
    half_cos, half_sin = jnp.cos(angles), jnp.sin(angles)
    cosine = jnp.concatenate([half_cos, half_cos], axis=1)
    sine = jnp.concatenate([-half_sin, half_sin], axis=1)

    def turn_keys(rows, sign):
        parts = []
        for h in range(KEY_VALUE_HEADS):
            piece = rows[:, h * HEAD_SIZE : (h + 1) * HEAD_SIZE]
            swapped = jnp.concatenate([piece[:, HEAD_SIZE // 2 :], piece[:, : HEAD_SIZE // 2]], axis=1)
            parts.append(piece * cosine + swapped * (sign * sine))
        return jnp.concatenate(parts, axis=1)

    pre = dot_nn(after(first_hidden, picked), qkv_low)
    keys_local = turn_keys(pre[:, MODEL_WIDTH : MODEL_WIDTH + KV], 1.0).astype(bf16)
    kv_local = jnp.concatenate([keys_local, pre[:, MODEL_WIDTH + KV :].astype(bf16)], axis=1)

    same = [kv_local] + [y_up(kv_local, s) for s in range(1, chips)]
    other = [core_shift(v, 1) for v in same]
    blocks = []
    for distance in range(shards):
        s = distance // 2
        if distance % 2 == 0:
            blocks.append(same[s])
        elif s + 1 < chips:
            blocks.append(jnp.where(core == 1, other[s], other[s + 1]))
        else:
            blocks.append(other[s])
    kv_blocks = jnp.stack(blocks)

    down_low = lax.all_gather(after(expert_out, kv_local).astype(bf16), "fsdp", axis=0)
    gate_up_low = lax.all_gather(after(expert_in, kv_local).astype(bf16), "fsdp", axis=0)

    level_two = after(z_shift(level_one, 1), kv_blocks)
    level_three = z_shift(level_two, 1)

    place_arg = place.astype(jnp.int32).reshape(1)
    attended, log_total, query_rows = attend(
        place_arg, pre, cosine, sine, after(kv_blocks, level_two)
    )
    residual = inputs + dot_nn(after(attended, level_three), output_low)
    scale_two = lax.rsqrt(jnp.mean(residual * residual, axis=1, keepdims=True) + NORM_EPS)
    normed_two = residual * scale_two
    hidden_two = (normed_two * gain_two).astype(bf16)

    upstream_swapped[1] = after(upstream_swapped[1], attended)
    upstream_swapped.append(swap(pick(after(level_two, attended), 2), upstream_swapped[1]))
    last_picked = pick(after(level_three, hidden_two), 3)

    levels = [hidden_two, z_shift(hidden_two, 1)]
    logits_t = lax.dot_general(
        router_low, hidden_two, (((0,), (1,)), ((), ())), preferred_element_type=f32
    )
    all_ids = jnp.arange(experts_all, dtype=jnp.int32)
    chosen_t = (routes_t[:, None, :] == all_ids[None, :, None]).astype(f32)
    gate_weights = jax.nn.softmax(jnp.sum(chosen_t * logits_t[None], axis=1), axis=0)
    gates_of = [gate_weights, z_shift(gate_weights, 1)]
    picked = pick(hidden_two, 0)
    hidden_swapped = [swap(picked, upstream_swapped[-1])]
    levels[1] = after(levels[1], picked)
    picked = pick(levels[1], 1)
    hidden_swapped.append(swap(picked, hidden_swapped[-1]))
    upstream_swapped.append(swap(last_picked, hidden_swapped[-1]))
    for k in range(2, depth):
        levels.append(after(z_shift(levels[-1], 1), picked, gates_of[1]))
        if k == depth - 1:
            upstream_pieces = order(after(upstream_swapped, levels[k - 1]))
            inner = inner_rows(upstream_pieces, down_low)
            gates_of[-1] = after(gates_of[-1], inner)
            levels[k] = after(levels[k], gates_of[-1])
        gates_of.append(z_shift(gates_of[-1], 1))
        picked = pick(levels[k], k)
        hidden_swapped.append(swap(picked, hidden_swapped[-1], upstream_swapped[-1]))
    gates_near = jnp.sum(named * jnp.stack(gates_of)[:, None], axis=2)
    row_gates = jnp.sum(jnp.where(picks, gates_near[:, :, None, :], 0.0), axis=3)
    row_gates = row_gates.reshape(depth, wide, experts_local, CAP)
    away_gates = [x_shift(row_gates[:, r], r) for r in range(1, wide)]
    hidden_swapped, away_gates = after((hidden_swapped, away_gates), levels[-1])
    hidden_pieces = order(hidden_swapped)
    row_gates = jnp.stack([row_gates[:, 0]] + away_gates)
    row_gates = row_gates.transpose(2, 0, 1, 3).reshape(experts_local, wide * depth * CAP, 1)

    scaled_hidden, gate_side, up_side, gate_dots, back_pieces = core_rows(
        hidden_pieces, gate_up_low, inner, row_gates
    )
    steps = swap_back(back_pieces)
    gate_dots = gate_dots.reshape(experts_local, wide, depth, CAP)
    away_dots = [x_shift(gate_dots[:, r], -r) for r in range(1, wide)]
    core_arg = core.astype(jnp.int32).reshape(1)
    in_term = in_grads(core_arg, hidden_pieces, gate_side, up_side, shards)
    in_mate = core_shift(in_term[1], 1)
    held = []
    ring_step(held, after(steps[1], in_term))
    arrived = ring_send(held)
    down_term = down_grads(core_arg, upstream_pieces, after(scaled_hidden, held[0]), shards)
    down_mate = core_shift(down_term[1], 1)
    in_mate = after(in_mate, down_term)
    in_low = chip_low(in_term[0], in_mate)
    in_sent = []
    for e in range(experts_local):
        in_sent.append(chip_send(after([low[e : e + 1] for low in in_low], in_sent[max(min(e, 2) - 1, 0) : min(e, 2)])))
    gate_dots = jnp.stack([gate_dots[:, 0]] + after(away_dots, down_term))
    gate_dots = gate_dots.transpose(2, 0, 1, 3).reshape(depth, near, CAP)
    token_dots = jnp.sum(jnp.where(picks, gate_dots[:, :, :, None], 0.0), axis=2)
    choice_dots = jnp.sum(named * token_dots[:, :, None, :], axis=1)
    lane = z_shift(choice_dots[1], 1)
    ring_step(held, after(steps[2], in_low, lane), arrived)
    lane = z_shift(lane + choice_dots[2], 1)
    arrived = ring_send(held)
    results = result_rows(after(scaled_hidden, held[1]), down_low, len(back_pieces))
    ring_step(held, after(steps[3], results, lane, in_sent[0]), arrived)
    down_mate = after(down_mate, held[1])
    down_low_sum = chip_low(down_term[0], down_mate)
    result_steps = swap_back(results, steps[0])
    lane = z_shift(lane + choice_dots[3], 1)
    arrived = ring_send(held)
    gate_grad = lane + choice_dots[0]
    picked_grad = gate_weights * (
        gate_grad - jnp.sum(gate_weights * gate_grad, axis=0, keepdims=True)
    )
    logit_grad_t = jnp.sum(chosen_t * picked_grad[:, None, :], axis=0).astype(bf16)
    router_term = dot_nn(logit_grad_t, hidden_two)
    hidden_back = ring_step(held, after(steps[0], router_term, down_low_sum, in_sent[1]), arrived)
    hidden_two_grad = hidden_back + lax.dot_general(
        logit_grad_t, router_low, (((0,), (1,)), ((), ())), preferred_element_type=f32
    )

    gain_two_term = jnp.sum(hidden_two_grad * normed_two, axis=0)
    scaled_two = hidden_two_grad * gain_two
    residual_grad = upstream + scale_two * (
        scaled_two - normed_two * jnp.mean(scaled_two * normed_two, axis=1, keepdims=True)
    )
    branch_grad = residual_grad.astype(bf16)
    attended_grad = dot_nt(branch_grad, output_low).astype(bf16)
    result_held = []
    ring_step(result_held, after(result_steps[1], hidden_back))
    attended_grad = after(attended_grad, result_held[0])
    arrived = ring_send(result_held)
    pre_grad, key_back, value_back = attend_back(
        place_arg, query_rows, kv_blocks, attended, attended_grad, log_total, cosine, sine
    )

    def send_parts(parts, index, shift):
        count = parts.shape[0]
        return [lax.dynamic_index_in_dim(parts, index, 0, keepdims=False)] + [
            shift(lax.dynamic_index_in_dim(parts, (index + s) % count, 0, keepdims=False), s)
            for s in range(1, count)
        ]

    def add_parts(parts):
        return functools.reduce(lambda total, part: total + part.astype(f32), parts[1:], parts[0].astype(f32)).astype(bf16)

    def join(part, index, count, shift):
        whole = jnp.zeros((count,) + part.shape, part.dtype)
        for s in range(count):
            piece = shift(part, s) if s else part
            whole = lax.dynamic_update_index_in_dim(whole, piece, (index - s) % count, 0)
        return whole

    def x_parts(part):
        return send_parts(part.reshape(wide, shard_rows // wide, part.shape[1]), column, x_shift)

    def z_parts(part):
        return send_parts(part.reshape(depth, shard_rows // wide // depth, part.shape[1]), level, z_shift)

    def z_join(part):
        return join(part, level, depth, z_shift).reshape(shard_rows // wide, part.shape[1])

    def x_join(part):
        return join(part, column, wide, x_shift).reshape(shard_rows, part.shape[1]).astype(f32)

    kv_back = jnp.concatenate([key_back, value_back], axis=2)
    none = jnp.zeros_like(kv_back[:1])
    mate = jnp.where(core == 1, kv_back[1::2], jnp.concatenate([none, kv_back[1:-1:2]], axis=0))
    mate = core_shift(mate, 1)
    kv_chip = kv_back[0::2].astype(f32) + mate.astype(f32)
    kv_low = after(kv_chip.astype(bf16), in_sent)
    in_sent = [jnp.concatenate(parts, axis=0) for parts in zip(*in_sent)]
    kv_parts = [
        lax.ppermute(kv_low[s], "fsdp", [(a + 2 * s, a) for a in range(shards - 2 * s)]) for s in range(1, chips)
    ]
    back_mine, back_mate = weight_grads(core_arg, attended, [after(branch_grad, kv_chip)], shards)
    back_mate = core_shift(back_mate, 1)
    kv_parts = after(kv_parts, back_mine)
    kv_grad = functools.reduce(lambda total, part: total + part.astype(f32), kv_parts, kv_chip[0])
    key_pre_grad = turn_keys(kv_grad[:, :KV], -1.0)
    kv_pre_grad = jnp.concatenate([key_pre_grad, kv_grad[:, KV:]], axis=1).astype(bf16)

    front_mine, front_mate = weight_grads(core_arg, first_hidden, [pre_grad, kv_pre_grad], shards)
    front_mate = core_shift(front_mate, 1)
    back_mate = after(back_mate, front_mine)
    back_sent = chip_send(chip_low(back_mine, back_mate))
    pre_late, kv_late = after((pre_grad, kv_pre_grad), front_mine)
    hidden_one_grad = dot_nt(pre_late, qkv_low[:, :MODEL_WIDTH]) + dot_nt(kv_late, qkv_low[:, MODEL_WIDTH:])
    gain_one_term = jnp.sum(hidden_one_grad * normed_one, axis=0)
    scaled_one = hidden_one_grad * gain_one
    input_grad = (
        residual_grad
        + scale_one
        * (scaled_one - normed_one * jnp.mean(scaled_one * normed_one, axis=1, keepdims=True))
    ).astype(bf16)
    extra = jnp.concatenate(
        [
            router_term,
            gain_one_term[None],
            gain_two_term[None],
            jnp.zeros((126 - experts_all, MODEL_WIDTH), f32),
        ],
        axis=0,
    )
    extra = extra.T.astype(bf16).reshape(chips, 2, shard_rows, 128)
    extra_mine = jnp.where(core == 0, extra[:, 0], extra[:, 1])
    extra_mate = core_shift(jnp.where(core == 0, extra[:, 1], extra[:, 0]), 1)
    ring_step(result_held, after(result_steps[2], front_mine), arrived)
    arrived = ring_send(result_held)
    front_mate, extra_mate = after((front_mate, extra_mate), extra_mine, result_held[1])
    front_mine = jnp.concatenate([front_mine, extra_mine], axis=2)
    front_mate = jnp.concatenate([front_mate, extra_mate], axis=2)
    front_low = chip_low(front_mine, front_mate)
    front_sent = chip_send(front_low)
    back_sent = after(back_sent, front_low)
    back_low = chip_total(back_mine, back_mate, back_sent).astype(bf16)
    back_parts = x_parts(back_low)
    in_state = adamw_update(
        expert_in,
        in_first,
        in_second,
        chip_total(after(in_term[0], back_low), in_mate, in_sent),
        0.5 / math.sqrt(MODEL_WIDTH),
        DECAY,
    )
    back_low = add_parts(after(back_parts, in_state))
    back_parts = z_parts(back_low)
    ring_step(result_held, after(result_steps[3], in_state), arrived)
    arrived = ring_send(result_held)
    front_sent = after(front_sent, back_low, result_held[2])
    front_low = chip_total(front_mine, front_mate, front_sent).astype(bf16)
    front_parts = x_parts(front_low)
    back_low = z_join(add_parts(after(back_parts, front_low)))
    down_sent = chip_send(after(down_low_sum, front_low))
    front_low = add_parts(after(front_parts, back_low))
    front_low = add_parts(z_parts(front_low))
    back_sum = x_join(back_low)
    moe_out = ring_step(result_held, after(result_steps[0], front_low), arrived)
    layer_out = (residual + moe_out).astype(bf16)
    front_sum = x_join(z_join(front_low))
    out_state = adamw_update(
        expert_out,
        out_first,
        out_second,
        chip_total(after(down_term[0], layer_out), down_mate, down_sent),
        0.5 / math.sqrt(FF // 8),
        DECAY,
    )
    output_sum = back_sum
    router_sum = front_sum[:, QKV : QKV + experts_all]
    query_sum = front_sum[:, :MODEL_WIDTH]
    key_sum = front_sum[:, MODEL_WIDTH : MODEL_WIDTH + KV]
    value_sum = front_sum[:, MODEL_WIDTH + KV : QKV]
    gain_sum = front_sum[:, QKV + experts_all : QKV + experts_all + 2].T

    rate = 0.5 / math.sqrt(MODEL_WIDTH // 2)
    return (
        layer_out,
        input_grad,
        *adamw_update(gains, gains_first, gains_second, gain_sum, GAIN_RATE, 0.0),
        *adamw_update(query_weight, query_first, query_second, query_sum, rate, DECAY),
        *adamw_update(key_matrix, key_moment_first, key_moment_second, key_sum, rate, DECAY),
        *adamw_update(
            value_matrix,
            value_moment_first,
            value_moment_second,
            value_sum,
            0.5 / math.sqrt(MODEL_WIDTH),
            DECAY,
        ),
        *adamw_update(
            output_weight, output_first, output_second, output_sum, 0.5 / math.sqrt(MODEL_WIDTH // 32), DECAY
        ),
        *adamw_update(
            router_weight, router_first, router_second, router_sum, 0.5 / math.sqrt(4 * MODEL_WIDTH), DECAY
        ),
        *in_state,
        *out_state,
    )


def solution(mesh):
    rows = P(("expert", "fsdp"), None)
    gains = P(None, "fsdp")
    matrix = P("fsdp", None)
    wide = P("expert", "fsdp", None)
    tall = P("expert", None, "fsdp")
    return jax.shard_map(
        body,
        mesh=mesh,
        in_specs=(rows,) * 3 + (gains,) * 3 + (matrix,) * 15 + (wide,) * 3 + (tall,) * 3,
        out_specs=(rows,) * 2 + (gains,) * 3 + (matrix,) * 15 + (wide,) * 3 + (tall,) * 3,
        check_vma=False,
    )
```

```python
import functools
import math

import jax
import jax.numpy as jnp
from jax import lax
from jax.experimental import pallas as pl
from jax.experimental.pallas import tpu as pltpu
from jax.sharding import PartitionSpec as P

MODEL_WIDTH = 1536
QUERY_HEADS = 12
KEY_VALUE_HEADS = 2
HEAD_SIZE = 128
GROUP = QUERY_HEADS // KEY_VALUE_HEADS
FF = 768
STEP = 10
CAP = 80
DEPTH = 4
HALF = MODEL_WIDTH // 2
KV = KEY_VALUE_HEADS * HEAD_SIZE
QKV = MODEL_WIDTH + 2 * KV


NORM_EPS = 1e-05
ROPE_BASE = 10000.0
BETA_ONE = 0.9
BETA_TWO = 0.95
ADAM_EPS = 1e-08
DECAY = 0.1
GAIN_RATE = 0.8
MASKED = -1e30
LOG2E = 1.0 / math.log(2.0)
SCORE_SCALE = 1.0 / math.sqrt(HEAD_SIZE)

f32 = jnp.float32
bf16 = jnp.bfloat16


def dot_nn(left, right):
    return lax.dot_general(left, right, (((1,), (0,)), ((), ())), preferred_element_type=f32)


def dot_nt(left, right):
    return lax.dot_general(left, right, (((1,), (1,)), ((), ())), preferred_element_type=f32)


def dot_tn(left, right):
    return lax.dot_general(left, right, (((0,), (0,)), ((), ())), preferred_element_type=f32)


def after(value, *others):
    return lax.optimization_barrier((value, others))[0]


def params(megabytes, axes):
    return pltpu.CompilerParams(
        vmem_limit_bytes=megabytes * 1024 * 1024, dimension_semantics=("arbitrary",) * axes
    )


def cost(flops, nbytes, trans=0):
    return pl.CostEstimate(flops=int(flops), bytes_accessed=int(nbytes), transcendentals=0)


def causal(score_t):
    key_place = lax.broadcasted_iota(jnp.int32, score_t.shape, 0)
    query_place = lax.broadcasted_iota(jnp.int32, score_t.shape, 1)
    return key_place <= query_place


def attend_kernel(place, pre, cosine, sine, keys, values, out, log_total, turned):
    rows = pre[...]
    query = rows * cosine[...] + pltpu.roll(rows, HEAD_SIZE // 2, 1) * sine[...]
    turned[...] = query.astype(bf16)
    query_t = query.T.astype(bf16)
    factor = SCORE_SCALE * LOG2E

    score = dot_nn(keys[0], query_t) * factor
    score = jnp.where(causal(score), score, MASKED)
    biggest = jnp.max(score, axis=0, keepdims=True)
    weight = jnp.exp2(score - biggest)
    total = jnp.sum(weight, axis=0, keepdims=True)
    acc = dot_nn(values[0].T, weight.astype(bf16))

    def step(back, carry):
        biggest, total, acc = carry
        score = dot_nn(keys[back], query_t) * factor
        larger = jnp.maximum(biggest, jnp.max(score, axis=0, keepdims=True))
        weight = jnp.exp2(score - larger)
        shrink = jnp.exp2(biggest - larger)
        total = total * shrink + jnp.sum(weight, axis=0, keepdims=True)
        acc = acc * shrink + dot_nn(values[back].T, weight.astype(bf16))
        return larger, total, acc

    biggest, total, acc = lax.fori_loop(1, place[0] + 1, step, (biggest, total, acc))
    out[...] = (acc / total).T.astype(bf16)
    log_total[0] = biggest + jnp.log(total) * LOG2E


def attend(place, pre, cosine, sine, kv_blocks):
    token_rows = pre.shape[0]
    blocks = kv_blocks.shape[0]
    width = (token_rows, HEAD_SIZE)
    many = (blocks, token_rows, HEAD_SIZE)
    return pl.pallas_call(
        attend_kernel,
        out_shape=(
            jax.ShapeDtypeStruct((token_rows, MODEL_WIDTH), bf16),
            jax.ShapeDtypeStruct((QUERY_HEADS, 1, token_rows), f32),
            jax.ShapeDtypeStruct((token_rows, MODEL_WIDTH), bf16),
        ),
        grid_spec=pltpu.PrefetchScalarGridSpec(
            num_scalar_prefetch=1,
            grid=(QUERY_HEADS,),
            in_specs=[
                pl.BlockSpec(width, lambda h, p: (0, h)),
                pl.BlockSpec(width, lambda h, p: (0, 0)),
                pl.BlockSpec(width, lambda h, p: (0, 0)),
                pl.BlockSpec(many, lambda h, p: (0, 0, h // GROUP)),
                pl.BlockSpec(many, lambda h, p: (0, 0, KEY_VALUE_HEADS + h // GROUP)),
            ],
            out_specs=(
                pl.BlockSpec(width, lambda h, p: (0, h)),
                pl.BlockSpec((1, 1, token_rows), lambda h, p: (h, 0, 0)),
                pl.BlockSpec(width, lambda h, p: (0, h)),
            ),
        ),
        compiler_params=params(56, 1),
        cost_estimate=cost(1e9, 1e6),
        name="attend",
    )(place, pre, cosine, sine, kv_blocks, kv_blocks)


def attend_back_kernel(
    place, query, keys, values, out, out_grad, log_total, cosine, sine, pre_grad, key_grad, value_grad, key_acc, value_acc
):
    head = pl.program_id(0)

    @pl.when(head % GROUP == 0)
    def _():
        key_acc[...] = jnp.zeros_like(key_acc)
        value_acc[...] = jnp.zeros_like(value_acc)

    factor = SCORE_SCALE * LOG2E
    query_rows = query[...]
    grad_rows = out_grad[...]
    query_t = query_rows.astype(f32).T.astype(bf16)
    grad_t32 = grad_rows.astype(f32).T
    grad_t = grad_t32.astype(bf16)
    row_dot = jnp.sum(out[...].astype(f32).T * grad_t32, axis=0, keepdims=True)
    level = log_total[0]

    def block(back, masked):
        key = keys[back]
        score = dot_nn(key, query_t) * factor - level
        weight = jnp.exp2(score)
        if masked:
            weight = jnp.where(causal(weight), weight, 0.0)
        value_acc[back] += dot_nn(weight.astype(bf16), grad_rows)
        prob_grad = dot_nn(values[back], grad_t)
        score_grad = (weight * (prob_grad - row_dot)).astype(bf16)
        key_acc[back] += dot_nn(score_grad, query_rows)
        return dot_nn(key.T, score_grad)

    query_grad = block(0, True)
    query_grad = lax.fori_loop(1, place[0] + 1, lambda b, acc: acc + block(b, False), query_grad)
    rows = query_grad.T * SCORE_SCALE
    pre_grad[...] = (rows * cosine[...] - pltpu.roll(rows, HEAD_SIZE // 2, 1) * sine[...]).astype(bf16)

    @pl.when(head % GROUP == GROUP - 1)
    def _():
        key_grad[...] = (key_acc[...] * SCORE_SCALE).astype(bf16)
        value_grad[...] = value_acc[...].astype(bf16)


def attend_back(place, query, kv_blocks, out, out_grad, log_total, cosine, sine):
    token_rows = query.shape[0]
    blocks = kv_blocks.shape[0]
    width = (token_rows, HEAD_SIZE)
    many = (blocks, token_rows, HEAD_SIZE)
    return pl.pallas_call(
        attend_back_kernel,
        out_shape=(
            jax.ShapeDtypeStruct((token_rows, MODEL_WIDTH), bf16),
            jax.ShapeDtypeStruct((blocks, token_rows, KV), bf16),
            jax.ShapeDtypeStruct((blocks, token_rows, KV), bf16),
        ),
        grid_spec=pltpu.PrefetchScalarGridSpec(
            num_scalar_prefetch=1,
            grid=(QUERY_HEADS,),
            in_specs=[
                pl.BlockSpec(width, lambda h, p: (0, h)),
                pl.BlockSpec(many, lambda h, p: (0, 0, h // GROUP)),
                pl.BlockSpec(many, lambda h, p: (0, 0, KEY_VALUE_HEADS + h // GROUP)),
                pl.BlockSpec(width, lambda h, p: (0, h)),
                pl.BlockSpec(width, lambda h, p: (0, h)),
                pl.BlockSpec((1, 1, token_rows), lambda h, p: (h, 0, 0)),
                pl.BlockSpec(width, lambda h, p: (0, 0)),
                pl.BlockSpec(width, lambda h, p: (0, 0)),
            ],
            out_specs=(
                pl.BlockSpec(width, lambda h, p: (0, h)),
                pl.BlockSpec(many, lambda h, p: (0, 0, h // GROUP)),
                pl.BlockSpec(many, lambda h, p: (0, 0, h // GROUP)),
            ),
            scratch_shapes=[pltpu.VMEM(many, f32), pltpu.VMEM(many, f32)],
        ),
        compiler_params=params(56, 1),
        cost_estimate=cost(1e9, 1e6),
        name="attend_back",
    )(place, query, kv_blocks, kv_blocks, out, out_grad, log_total, cosine, sine)


def gather_rows(pieces, rows):
    for p, piece in enumerate(pieces):
        rows[p * CAP : (p + 1) * CAP] = piece[...]


def scatter_rows(rows, pieces, at, span):
    low = rows.astype(bf16)
    for p, piece in enumerate(pieces):
        piece[:, at : at + span] = low[p * CAP : (p + 1) * CAP]


def piece_spec():
    return pl.BlockSpec((CAP, MODEL_WIDTH), lambda e, *_: (e, 0))


def row_scratch(count):
    return [pltpu.VMEM((count * CAP, MODEL_WIDTH), bf16)]


def inner_kernel(count, *refs):
    pieces, (down, inner, rows) = refs[:count], refs[count:]
    gather_rows(pieces, rows)
    shards, span = down.shape[0], down.shape[3]
    acc = None
    for c in range(shards):
        term = dot_nt(rows[:, c * span : (c + 1) * span], down[c, 0])
        acc = term if acc is None else acc + term
    inner[0] = acc.astype(bf16)


def inner_rows(pieces, down):
    shards, experts, _, span = down.shape
    rows = len(pieces) * CAP
    return pl.pallas_call(
        functools.partial(inner_kernel, len(pieces)),
        out_shape=jax.ShapeDtypeStruct((experts, rows, FF), bf16),
        grid=(experts,),
        in_specs=[piece_spec()] * len(pieces) + [pl.BlockSpec((shards, 1, FF, span), lambda e: (0, e, 0, 0))],
        out_specs=pl.BlockSpec((1, rows, FF), lambda e: (e, 0, 0)),
        scratch_shapes=row_scratch(len(pieces)),
        compiler_params=params(56, 1),
        cost_estimate=cost(2 * experts * rows * FF * MODEL_WIDTH, 20e6),
        name="inner_rows",
    )(*pieces, down)


def core_kernel(count, *refs):
    pieces, refs = refs[:count], refs[count:]
    gate_up, inner, weight, scaled, gate_side, up_side, gate_dots = refs[:7]
    back, (rows,) = refs[7 : 7 + count], refs[7 + count :]
    gather_rows(pieces, rows)
    span = gate_up.shape[2]
    tile = 256
    factor = weight[0]
    dots = None

    def product(at):
        return dot_nn(rows[...], gate_up[:, 0, :, at : at + tile].reshape(MODEL_WIDTH, tile))

    for n in range(FF // tile):
        at = n * tile
        gate_pre = product(at)
        up_part = product(FF + at)
        sigmoid = 1.0 / (1.0 + jnp.exp(-gate_pre))
        silu = gate_pre * sigmoid
        hidden = silu * up_part
        raw = inner[0, :, at : at + tile].astype(f32)
        part = jnp.sum(raw * hidden, axis=1, keepdims=True)
        dots = part if dots is None else dots + part
        scaled[0, :, at : at + tile] = (hidden * factor).astype(bf16)
        raw = raw * factor
        gate_side[0, :, at : at + tile] = (raw * up_part * (sigmoid + silu * (1.0 - sigmoid))).astype(bf16)
        up_side[0, :, at : at + tile] = (raw * silu).astype(bf16)
    gate_dots[0] = dots

    width = 384
    group = width // span
    for chunk in range(MODEL_WIDTH // width):
        block = gate_up[chunk * group : (chunk + 1) * group, 0].reshape(width, 2 * FF)
        grads = dot_nt(gate_side[0], block[:, :FF]) + dot_nt(up_side[0], block[:, FF:])
        scatter_rows(grads, back, chunk * width, width)


def core_rows(pieces, gate_up, inner, weight):
    count = len(pieces)
    shards, experts, span, _ = gate_up.shape
    rows = count * CAP
    whole = pl.BlockSpec((1, rows, FF), lambda e: (e, 0, 0))
    column = pl.BlockSpec((1, rows, 1), lambda e: (e, 0, 0))
    low = jax.ShapeDtypeStruct((experts, rows, FF), bf16)
    out = pl.pallas_call(
        functools.partial(core_kernel, count),
        out_shape=(low, low, low, jax.ShapeDtypeStruct((experts, rows, 1), f32))
        + (jax.ShapeDtypeStruct(pieces[0].shape, bf16),) * count,
        grid=(experts,),
        in_specs=[piece_spec()] * count
        + [pl.BlockSpec((shards, 1, span, 2 * FF), lambda e: (0, e, 0, 0)), whole, column],
        out_specs=(whole, whole, whole, column) + (piece_spec(),) * count,
        scratch_shapes=row_scratch(len(pieces)),
        compiler_params=params(60, 1),
        cost_estimate=cost(8 * experts * rows * FF * MODEL_WIDTH, 60e6),
        name="core_rows",
    )(*pieces, gate_up, inner, weight)
    return out[0], out[1], out[2], out[3], list(out[4:])


def result_kernel(scaled, down, *pieces):
    width = 384
    shards, span = down.shape[0], down.shape[3]
    group = width // span
    rows = scaled[0]
    for chunk in range(MODEL_WIDTH // width):
        parts = [down[c, 0] for c in range(chunk * group, (chunk + 1) * group)]
        block = parts[0] if group == 1 else jnp.concatenate(parts, axis=1)
        scatter_rows(dot_nn(rows, block), pieces, chunk * width, width)


def result_rows(scaled, down, count):
    experts, rows, _ = scaled.shape
    shards, _, _, span = down.shape
    return list(
        pl.pallas_call(
            result_kernel,
            out_shape=(jax.ShapeDtypeStruct((experts * CAP, MODEL_WIDTH), bf16),) * count,
            grid=(experts,),
            in_specs=[
                pl.BlockSpec((1, rows, FF), lambda e: (e, 0, 0)),
                pl.BlockSpec((shards, 1, FF, span), lambda e: (0, e, 0, 0)),
            ],
            out_specs=(piece_spec(),) * count,
            compiler_params=params(56, 1),
            cost_estimate=cost(2 * experts * rows * FF * MODEL_WIDTH, 22e6),
            name="result_rows",
        )(scaled, down)
    )


def down_grad_kernel(count, *refs):
    pieces, (scaled, out, rows) = refs[:count], refs[count:]
    gather_rows(pieces, rows)
    shards, span = out.shape[0], out.shape[3]
    scaled_t = scaled[0].T
    for c in range(shards):
        out[c, 0] = dot_nn(scaled_t, rows[:, c * span : (c + 1) * span]).astype(bf16)


def down_grads(pieces, scaled, shards):
    experts, rows, _ = scaled.shape
    span = MODEL_WIDTH // shards
    return pl.pallas_call(
        functools.partial(down_grad_kernel, len(pieces)),
        out_shape=jax.ShapeDtypeStruct((shards, experts, FF, span), bf16),
        grid=(experts,),
        in_specs=[piece_spec()] * len(pieces) + [pl.BlockSpec((1, rows, FF), lambda e: (e, 0, 0))],
        out_specs=pl.BlockSpec((shards, 1, FF, span), lambda e: (0, e, 0, 0)),
        scratch_shapes=row_scratch(len(pieces)),
        compiler_params=params(56, 1),
        cost_estimate=cost(2 * experts * rows * FF * MODEL_WIDTH, 22e6),
        name="down_grads",
    )(*pieces, scaled)


def in_grad_kernel(count, *refs):
    pieces, (gate_side, up_side, out, rows) = refs[:count], refs[count:]
    gather_rows(pieces, rows)
    shards, span = out.shape[0], out.shape[2]
    rows_t = rows[...].T
    for c in range(shards):
        part = rows_t[c * span : (c + 1) * span]
        out[c, 0, :, :FF] = dot_nn(part, gate_side[0]).astype(bf16)
        out[c, 0, :, FF:] = dot_nn(part, up_side[0]).astype(bf16)


def in_grads(pieces, gate_side, up_side, shards):
    experts, rows, _ = gate_side.shape
    span = MODEL_WIDTH // shards
    whole = pl.BlockSpec((1, rows, FF), lambda e: (e, 0, 0))
    return pl.pallas_call(
        functools.partial(in_grad_kernel, len(pieces)),
        out_shape=jax.ShapeDtypeStruct((shards, experts, span, 2 * FF), bf16),
        grid=(experts,),
        in_specs=[piece_spec()] * len(pieces) + [whole, whole],
        out_specs=pl.BlockSpec((shards, 1, span, 2 * FF), lambda e: (0, e, 0, 0)),
        scratch_shapes=row_scratch(len(pieces)),
        compiler_params=params(56, 1),
        cost_estimate=cost(4 * experts * rows * FF * MODEL_WIDTH, 35e6),
        name="in_grads",
    )(*pieces, gate_side, up_side)


def ring_kernel(wide, *refs):
    picks, pieces = refs[0], refs[1 : 1 + wide]
    arrived, out = refs[1 + wide : -1], refs[-1]
    rows = jnp.concatenate([piece[...] for piece in pieces], axis=0)
    total = dot_tn(picks[0], rows)
    if arrived:
        total = total + arrived[0][...].astype(f32)
    out[...] = total.astype(out.dtype)


def ring_rows(picks, level, pieces, arrived, last):
    _, many, token_rows = picks.shape
    tile = 512
    side = pl.BlockSpec((token_rows, tile), lambda n: (0, n))
    return pl.pallas_call(
        functools.partial(ring_kernel, len(pieces)),
        out_shape=jax.ShapeDtypeStruct((token_rows, MODEL_WIDTH), f32 if last else bf16),
        grid=(MODEL_WIDTH // tile,),
        in_specs=[pl.BlockSpec((1, many, token_rows), lambda n: (level, 0, 0))]
        + [pl.BlockSpec((p.shape[0], tile), lambda n: (0, n)) for p in pieces]
        + [side] * len(arrived),
        out_specs=side,
        compiler_params=params(48, 1),
        cost_estimate=cost(4 * many * token_rows * HALF, 8e6),
        name="ring_rows",
    )(picks, *pieces, *arrived)


def pick_kernel(picks, rows, own, away):
    per = own.shape[0]
    picked = dot_nn(picks[0], rows[...]).astype(bf16)
    own[...] = picked[:per]
    for r in range(away.shape[0]):
        away[r] = picked[(r + 1) * per : (r + 2) * per]


def pick_rows(picks, level, rows, wide):
    _, many, token_rows = picks.shape
    per = many // wide
    tile = 512
    return pl.pallas_call(
        pick_kernel,
        out_shape=(
            jax.ShapeDtypeStruct((per, MODEL_WIDTH), bf16),
            jax.ShapeDtypeStruct((wide - 1, per, MODEL_WIDTH), bf16),
        ),
        grid=(MODEL_WIDTH // tile,),
        in_specs=[
            pl.BlockSpec((1, many, token_rows), lambda n: (level, 0, 0)),
            pl.BlockSpec((token_rows, tile), lambda n: (0, n)),
        ],
        out_specs=(
            pl.BlockSpec((per, tile), lambda n: (0, n)),
            pl.BlockSpec((wide - 1, per, tile), lambda n: (0, 0, n)),
        ),
        compiler_params=params(32, 1),
        cost_estimate=cost(4 * many * token_rows * HALF, 5e6),
        name="pick_rows",
    )(picks, rows)


def weight_grad_kernel(rows, *refs):
    *grads, out = refs
    rows_t = rows[...].T
    at = 0
    for side in grads:
        if side.dtype == f32:
            out[:, at:] = side[...].T.astype(bf16)
        else:
            columns = side.shape[1]
            out[:, at : at + columns] = dot_nn(rows_t, side[...]).astype(bf16)
            at += columns


def weight_grads(rows, grads, extra=None):
    token_rows = rows.shape[0]
    tile = 384
    extras = [] if extra is None else [extra]
    columns = sum(g.shape[1] for g in grads) + sum(e.shape[0] for e in extras)
    return pl.pallas_call(
        weight_grad_kernel,
        out_shape=jax.ShapeDtypeStruct((MODEL_WIDTH, columns), bf16),
        grid=(MODEL_WIDTH // tile,),
        in_specs=[pl.BlockSpec((token_rows, tile), lambda n: (0, n))]
        + [pl.BlockSpec(g.shape, lambda n: (0, 0)) for g in grads]
        + [pl.BlockSpec((e.shape[0], tile), lambda n: (0, n)) for e in extras],
        out_specs=pl.BlockSpec((tile, columns), lambda n: (n, 0)),
        compiler_params=params(56, 1),
        cost_estimate=cost(2 * MODEL_WIDTH * token_rows * columns, 14e6),
        name="weight_grads",
    )(rows, *grads, *extras)


def keep_and_send(core, pair, mine, theirs):
    first, second = (p.astype(bf16) for p in pair)
    mine(jnp.where(core == 0, first, second))
    theirs(jnp.where(core == 0, second, first))


def core_grad_kernel(core, rows, *refs):
    *grads, mine, theirs = refs
    span = mine.shape[1]
    rows_t = rows[...].T
    at = 0
    for side in grads:
        columns = side.shape[1]
        pair = [dot_nn(rows_t[c * span : (c + 1) * span], side[...]) for c in range(2)]
        where = (0, slice(None), slice(at, at + columns))
        keep_and_send(
            core[0],
            pair,
            functools.partial(mine.__setitem__, where),
            functools.partial(theirs.__setitem__, where),
        )
        at += columns


def core_grads(core, rows, grads, shards):
    token_rows = rows.shape[0]
    span = MODEL_WIDTH // shards
    columns = sum(g.shape[1] for g in grads)
    out = jax.ShapeDtypeStruct((shards // 2, span, columns), bf16)
    block = pl.BlockSpec((1, span, columns), lambda n, c: (n, 0, 0))
    return pl.pallas_call(
        core_grad_kernel,
        out_shape=(out, out),
        grid_spec=pltpu.PrefetchScalarGridSpec(
            num_scalar_prefetch=1,
            grid=(shards // 2,),
            in_specs=[pl.BlockSpec((token_rows, 2 * span), lambda n, c: (0, n))]
            + [pl.BlockSpec(g.shape, lambda n, c: (0, 0)) for g in grads],
            out_specs=(block, block),
        ),
        compiler_params=params(56, 1),
        cost_estimate=cost(2 * MODEL_WIDTH * token_rows * columns, 14e6),
        name="core_grads",
    )(core, rows, *grads)


def adamw_update(weight, moment_one, moment_two, gradient, step_rate, decay_rate):
    first_new = BETA_ONE * moment_one + (1.0 - BETA_ONE) * gradient
    second_new = BETA_TWO * moment_two + (1.0 - BETA_TWO) * gradient * gradient
    first_hat = first_new / (1.0 - BETA_ONE**STEP)
    second_hat = second_new / (1.0 - BETA_TWO**STEP)
    weight_new = weight - step_rate * (
        first_hat / (jnp.sqrt(second_hat) + ADAM_EPS) + decay_rate * weight
    )
    return (weight_new, first_new, second_new)


def body(
    tokens,
    cotangent,
    routes,
    gains,
    gains_first,
    gains_second,
    query_weight,
    query_first,
    query_second,
    key_matrix,
    key_moment_first,
    key_moment_second,
    value_matrix,
    value_moment_first,
    value_moment_second,
    output_weight,
    output_first,
    output_second,
    router_weight,
    router_first,
    router_second,
    expert_in,
    in_first,
    in_second,
    expert_out,
    out_first,
    out_second,
):
    token_rows, top_count = routes.shape
    shards = lax.axis_size("fsdp")
    place = lax.axis_index("fsdp")
    groups = lax.axis_size("expert")
    group = lax.axis_index("expert")
    depth = DEPTH
    wide = groups // depth
    level, column = group // wide, group % wide
    experts_local = expert_in.shape[0]
    experts_all = experts_local * groups
    near = wide * experts_local
    shard_rows = query_weight.shape[0]

    def z_shift(value, by):
        return lax.ppermute(
            value,
            "expert",
            [(a * wide + b, (a + by) % depth * wide + b) for a in range(depth) for b in range(wide)],
        )

    def x_shift(value, by):
        return lax.ppermute(
            value,
            "expert",
            [(a * wide + b, a * wide + (b + by) % wide) for a in range(depth) for b in range(wide)],
        )

    def back_shift(value, by):
        pairs = [(a, a + by) for a in range(shards) if 0 <= a + by < shards]
        return lax.ppermute(value, "fsdp", pairs)

    chips = shards // 2
    chip, core = place // 2, place % 2
    core_arg = core.astype(jnp.int32).reshape(1)

    def core_shift(value, by):
        return lax.ppermute(value, "fsdp", [(a, a // 2 * 2 + (a + by) % 2) for a in range(shards)])

    def y_shift(value, by):
        return lax.ppermute(value, "fsdp", [(a, (a + 2 * by) % shards) for a in range(shards)])

    def y_up(value, by):
        return lax.ppermute(value, "fsdp", [(a, a + 2 * by) for a in range(shards - 2 * by)])

    small = jnp.concatenate(
        [
            router_weight.astype(bf16),
            gains.T.astype(bf16),
            jnp.zeros((shard_rows, 128 - experts_all - 2), bf16),
        ],
        axis=1,
    )
    front_low = lax.all_gather(
        jnp.concatenate(
            [query_weight.astype(bf16), key_matrix.astype(bf16), value_matrix.astype(bf16), small], axis=1
        ),
        "fsdp",
        axis=0,
        tiled=True,
    )
    output_low = lax.all_gather(output_weight.astype(bf16), "fsdp", axis=0, tiled=True)
    qkv_low = front_low[:, :QKV]
    router_low = front_low[:, QKV : QKV + experts_all]
    gain_pair = front_low[:, QKV + experts_all : QKV + experts_all + 2].astype(f32).T
    gain_one, gain_two = gain_pair[0], gain_pair[1]

    routes_t = routes.T
    routes_of = jnp.stack([routes_t] + [z_shift(routes_t, i) for i in range(1, depth)])

    def expert_ids(at_level):
        columns = (column + jnp.arange(wide, dtype=jnp.int32)) % wide
        first_ids = (at_level * wide + columns) * experts_local
        return (first_ids[:, None] + jnp.arange(experts_local, dtype=jnp.int32)[None, :]).reshape(near)

    named = (routes_of[:, None] == expert_ids(level)[None, :, None, None]).astype(f32)
    chosen_here = jnp.sum(named, axis=2)
    earlier = (
        jnp.arange(token_rows, dtype=jnp.int32)[:, None] < jnp.arange(token_rows, dtype=jnp.int32)[None, :]
    ).astype(bf16)
    slots = dot_nn(chosen_here.reshape(depth * near, token_rows).astype(bf16), earlier).reshape(
        depth, near, token_rows
    )
    code = jnp.where(chosen_here > 0, slots.astype(jnp.int32), -1)
    picks = code[:, :, None, :] == jnp.arange(CAP, dtype=jnp.int32)[None, None, :, None]
    picks_low = picks.astype(bf16).reshape(depth, near * CAP, token_rows)

    def pick(rows, k):
        return pick_rows(picks_low, k, rows, wide)

    def swap(picked, *before):
        own, away = picked
        pairs = [own]
        for r in range(1, wide):
            pairs.append(x_shift(after(away[r - 1], pairs[1:], before), r))
        return pairs

    def order(swapped):
        return [swapped[k][r] for r in range(wide) for k in range(depth)]

    def swap_back(pieces, *before):
        steps = [None] * depth
        for m in range(depth):
            k = (m + 1) % depth
            steps[k] = [pieces[k]]
            for r in range(1, wide):
                piece = x_shift(after(pieces[r * depth + k], before), -r)
                steps[k].append(piece)
                if m % 2 == 0:
                    before = (piece,)
        return steps

    def chip_sum(mine, mate, chip):
        return lax.dynamic_index_in_dim(mine, chip, 0, keepdims=False).astype(
            f32
        ) + lax.dynamic_index_in_dim(mate, chip, 0, keepdims=False).astype(f32)

    def chip_low(mine, mate):
        return [chip_sum(mine, mate, (chip + s) % chips).astype(bf16) for s in range(1, chips)]

    def chip_send(low):
        return [y_shift(part, s) for s, part in enumerate(low, 1)]

    def chip_total(mine, mate, sent):
        return functools.reduce(lambda total, part: total + part.astype(f32), sent, chip_sum(mine, mate, chip))

    def ring_send(held):
        return [z_shift(held[-1], 1)]

    def ring_step(held, pieces, arrived=()):
        m = len(held)
        out = ring_rows(picks_low, (m + 1) % depth, pieces, arrived, m == depth - 1)
        if m == depth - 1:
            return out
        held.append(out)

    upstream = cotangent.astype(f32)
    level_one = z_shift(cotangent, 1)
    upstream_swapped = [swap(pick(cotangent, 0))]
    level_one = after(level_one, upstream_swapped)
    picked = pick(level_one, 1)
    upstream_swapped.append(swap(picked, upstream_swapped[-1]))

    inputs = tokens.astype(f32)
    scale_one = lax.rsqrt(jnp.mean(inputs * inputs, axis=1, keepdims=True) + NORM_EPS)
    normed_one = inputs * scale_one
    first_hidden = (normed_one * gain_one).astype(bf16)
    inverse = ROPE_BASE ** (-(jnp.arange(HEAD_SIZE // 2, dtype=f32) * 2.0 / HEAD_SIZE))
    places = (place * token_rows + jnp.arange(token_rows, dtype=jnp.int32)).astype(f32)
    angles = places[:, None] * inverse[None, :]
    half_cos, half_sin = jnp.cos(angles), jnp.sin(angles)
    cosine = jnp.concatenate([half_cos, half_cos], axis=1)
    sine = jnp.concatenate([-half_sin, half_sin], axis=1)

    def turn_keys(rows, sign):
        parts = []
        for h in range(KEY_VALUE_HEADS):
            piece = rows[:, h * HEAD_SIZE : (h + 1) * HEAD_SIZE]
            swapped = jnp.concatenate([piece[:, HEAD_SIZE // 2 :], piece[:, : HEAD_SIZE // 2]], axis=1)
            parts.append(piece * cosine + swapped * (sign * sine))
        return jnp.concatenate(parts, axis=1)

    pre = dot_nn(after(first_hidden, picked), qkv_low)
    keys_local = turn_keys(pre[:, MODEL_WIDTH : MODEL_WIDTH + KV], 1.0).astype(bf16)
    kv_local = jnp.concatenate([keys_local, pre[:, MODEL_WIDTH + KV :].astype(bf16)], axis=1)

    same = [kv_local] + [y_up(kv_local, s) for s in range(1, chips)]
    other = [core_shift(v, 1) for v in same]
    blocks = []
    for distance in range(shards):
        s = distance // 2
        if distance % 2 == 0:
            blocks.append(same[s])
        elif s + 1 < chips:
            blocks.append(jnp.where(core == 1, other[s], other[s + 1]))
        else:
            blocks.append(other[s])
    kv_blocks = jnp.stack(blocks)

    down_low = lax.all_gather(after(expert_out, kv_local).astype(bf16), "fsdp", axis=0)
    gate_up_low = lax.all_gather(after(expert_in, kv_local).astype(bf16), "fsdp", axis=0)

    level_two = after(z_shift(level_one, 1), kv_blocks)
    level_three = z_shift(level_two, 1)

    place_arg = place.astype(jnp.int32).reshape(1)
    attended, log_total, query_rows = attend(
        place_arg, pre, cosine, sine, after(kv_blocks, level_two)
    )
    residual = inputs + dot_nn(after(attended, level_three), output_low)
    scale_two = lax.rsqrt(jnp.mean(residual * residual, axis=1, keepdims=True) + NORM_EPS)
    normed_two = residual * scale_two
    hidden_two = (normed_two * gain_two).astype(bf16)

    upstream_swapped[1] = after(upstream_swapped[1], attended)
    upstream_swapped.append(swap(pick(after(level_two, attended), 2), upstream_swapped[1]))
    last_picked = pick(after(level_three, hidden_two), 3)

    levels = [hidden_two, z_shift(hidden_two, 1)]
    logits_t = lax.dot_general(
        router_low, hidden_two, (((0,), (1,)), ((), ())), preferred_element_type=f32
    )
    all_ids = jnp.arange(experts_all, dtype=jnp.int32)
    chosen_t = (routes_t[:, None, :] == all_ids[None, :, None]).astype(f32)
    gate_weights = jax.nn.softmax(jnp.sum(chosen_t * logits_t[None], axis=1), axis=0)
    gates_of = [gate_weights, z_shift(gate_weights, 1)]
    picked = pick(hidden_two, 0)
    hidden_swapped = [swap(picked, upstream_swapped[-1])]
    levels[1] = after(levels[1], picked)
    picked = pick(levels[1], 1)
    hidden_swapped.append(swap(picked, hidden_swapped[-1]))
    upstream_swapped.append(swap(last_picked, hidden_swapped[-1]))
    for k in range(2, depth):
        levels.append(after(z_shift(levels[-1], 1), picked, gates_of[1]))
        if k == depth - 1:
            upstream_pieces = order(after(upstream_swapped, levels[k - 1]))
            inner = inner_rows(upstream_pieces, down_low)
            gates_of[-1] = after(gates_of[-1], inner)
            levels[k] = after(levels[k], gates_of[-1])
        gates_of.append(z_shift(gates_of[-1], 1))
        picked = pick(levels[k], k)
        hidden_swapped.append(swap(picked, hidden_swapped[-1], upstream_swapped[-1]))
    gates_near = jnp.sum(named * jnp.stack(gates_of)[:, None], axis=2)
    row_gates = jnp.sum(jnp.where(picks, gates_near[:, :, None, :], 0.0), axis=3)
    row_gates = row_gates.reshape(depth, wide, experts_local, CAP)
    away_gates = [x_shift(row_gates[:, r], r) for r in range(1, wide)]
    hidden_swapped, away_gates = after((hidden_swapped, away_gates), levels[-1])
    hidden_pieces = order(hidden_swapped)
    row_gates = jnp.stack([row_gates[:, 0]] + away_gates)
    row_gates = row_gates.transpose(2, 0, 1, 3).reshape(experts_local, wide * depth * CAP, 1)

    scaled_hidden, gate_side, up_side, gate_dots, back_pieces = core_rows(
        hidden_pieces, gate_up_low, inner, row_gates
    )
    steps = swap_back(back_pieces)
    gate_dots = gate_dots.reshape(experts_local, wide, depth, CAP)
    away_dots = [x_shift(gate_dots[:, r], -r) for r in range(1, wide)]
    down_term = down_grads(upstream_pieces, scaled_hidden, shards)
    held = []
    ring_step(held, after(steps[1], down_term))
    out_part = lax.psum_scatter(after(down_term, held[0]), "fsdp", scatter_dimension=0)
    arrived = ring_send(held)
    in_term = in_grads(hidden_pieces, *after((gate_side, up_side), held[0]), shards)
    gate_dots = jnp.stack([gate_dots[:, 0]] + after(away_dots, in_term))
    gate_dots = gate_dots.transpose(2, 0, 1, 3).reshape(depth, near, CAP)
    token_dots = jnp.sum(jnp.where(picks, gate_dots[:, :, :, None], 0.0), axis=2)
    choice_dots = jnp.sum(named * token_dots[:, :, None, :], axis=1)
    lane = z_shift(choice_dots[1], 1)
    ring_step(held, after(steps[2], in_term, lane), arrived)
    in_part = lax.psum_scatter(after(in_term, held[1]), "fsdp", scatter_dimension=0)
    lane = z_shift(lane + choice_dots[2], 1)
    arrived = ring_send(held)
    results = result_rows(after(scaled_hidden, held[1]), down_low, len(back_pieces))
    ring_step(held, after(steps[3], results, lane), arrived)
    result_steps = swap_back(results, steps[0])
    lane = z_shift(lane + choice_dots[3], 1)
    arrived = ring_send(held)
    gate_grad = lane + choice_dots[0]
    picked_grad = gate_weights * (
        gate_grad - jnp.sum(gate_weights * gate_grad, axis=0, keepdims=True)
    )
    logit_grad_t = jnp.sum(chosen_t * picked_grad[:, None, :], axis=0).astype(bf16)
    router_term = dot_nn(logit_grad_t, hidden_two)
    hidden_back = ring_step(held, after(steps[0], router_term), arrived)
    hidden_two_grad = hidden_back + lax.dot_general(
        logit_grad_t, router_low, (((0,), (1,)), ((), ())), preferred_element_type=f32
    )

    gain_two_term = jnp.sum(hidden_two_grad * normed_two, axis=0)
    scaled_two = hidden_two_grad * gain_two
    residual_grad = upstream + scale_two * (
        scaled_two - normed_two * jnp.mean(scaled_two * normed_two, axis=1, keepdims=True)
    )
    branch_grad = residual_grad.astype(bf16)
    attended_grad = dot_nt(branch_grad, output_low).astype(bf16)
    result_held = []
    ring_step(result_held, after(result_steps[1], hidden_back))
    attended_grad = after(attended_grad, result_held[0], out_part)
    arrived = ring_send(result_held)
    pre_grad, key_back, value_back = attend_back(
        place_arg, query_rows, kv_blocks, attended, attended_grad, log_total, cosine, sine
    )

    def send_parts(parts, index, shift):
        count = parts.shape[0]
        return [lax.dynamic_index_in_dim(parts, index, 0, keepdims=False)] + [
            shift(lax.dynamic_index_in_dim(parts, (index + s) % count, 0, keepdims=False), s)
            for s in range(1, count)
        ]

    def add_parts(parts):
        return functools.reduce(lambda total, part: total + part.astype(f32), parts[1:], parts[0].astype(f32)).astype(bf16)

    def join(part, index, count, shift):
        whole = jnp.zeros((count,) + part.shape, part.dtype)
        for s in range(count):
            piece = shift(part, s) if s else part
            whole = lax.dynamic_update_index_in_dim(whole, piece, (index - s) % count, 0)
        return whole

    def x_parts(part):
        return send_parts(part.reshape(wide, shard_rows // wide, part.shape[1]), column, x_shift)

    def z_parts(part):
        return send_parts(part.reshape(depth, shard_rows // wide // depth, part.shape[1]), level, z_shift)

    def z_join(part):
        return join(part, level, depth, z_shift).reshape(shard_rows // wide, part.shape[1])

    def x_join(part):
        return join(part, column, wide, x_shift).reshape(shard_rows, part.shape[1]).astype(f32)

    kv_back = jnp.concatenate([key_back, value_back], axis=2)
    none = jnp.zeros_like(kv_back[:1])
    mate = jnp.where(core == 1, kv_back[1::2], jnp.concatenate([none, kv_back[1:-1:2]], axis=0))
    mate = core_shift(mate, 1)
    kv_chip = kv_back[0::2].astype(f32) + mate.astype(f32)
    kv_low = kv_chip.astype(bf16)
    kv_parts = [
        lax.ppermute(kv_low[s], "fsdp", [(a + 2 * s, a) for a in range(shards - 2 * s)]) for s in range(1, chips)
    ]
    back_mine, back_mate = core_grads(core_arg, attended, [after(branch_grad, kv_chip)], shards)
    back_mate = core_shift(back_mate, 1)
    out_state = adamw_update(
        expert_out,
        out_first,
        out_second,
        after(out_part, back_mine).astype(f32),
        0.5 / math.sqrt(FF // 8),
        DECAY,
    )
    ring_step(result_held, after(result_steps[2], out_state), arrived)
    arrived = ring_send(result_held)
    kv_parts = after(kv_parts, result_held[1])
    kv_grad = functools.reduce(lambda total, part: total + part.astype(f32), kv_parts, kv_chip[0])
    key_pre_grad = turn_keys(kv_grad[:, :KV], -1.0)
    kv_pre_grad = jnp.concatenate([key_pre_grad, kv_grad[:, KV:]], axis=1).astype(bf16)

    front_terms = weight_grads(first_hidden, [pre_grad, kv_pre_grad])
    front_part = lax.psum_scatter(front_terms, "fsdp", scatter_dimension=0, tiled=True)
    pre_late, kv_late = after((pre_grad, kv_pre_grad), front_terms)
    hidden_one_grad = dot_nt(pre_late, qkv_low[:, :MODEL_WIDTH]) + dot_nt(kv_late, qkv_low[:, MODEL_WIDTH:])
    gain_one_term = jnp.sum(hidden_one_grad * normed_one, axis=0)
    scaled_one = hidden_one_grad * gain_one
    input_grad = (
        residual_grad
        + scale_one
        * (scaled_one - normed_one * jnp.mean(scaled_one * normed_one, axis=1, keepdims=True))
    ).astype(bf16)
    extra = jnp.concatenate(
        [
            router_term,
            gain_one_term[None],
            gain_two_term[None],
            jnp.zeros((126 - experts_all, MODEL_WIDTH), f32),
        ],
        axis=0,
    )
    extra = extra.T.astype(bf16).reshape(chips, 2, shard_rows, 128)
    extra_mine = jnp.where(core == 0, extra[:, 0], extra[:, 1])
    extra_mate = core_shift(jnp.where(core == 0, extra[:, 1], extra[:, 0]), 1)
    ring_step(result_held, after(result_steps[3], extra_mine), arrived)
    arrived = ring_send(result_held)
    back_mate, extra_mate = after((back_mate, extra_mate), result_held[2])
    back_mine = jnp.concatenate([back_mine, extra_mine], axis=2)
    back_mate = jnp.concatenate([back_mate, extra_mate], axis=2)
    back_low = chip_low(back_mine, back_mate)
    back_sent = chip_send(back_low)
    in_state = adamw_update(
        expert_in,
        in_first,
        in_second,
        after(in_part, back_low).astype(f32),
        0.5 / math.sqrt(MODEL_WIDTH),
        DECAY,
    )
    moe_out = ring_step(result_held, after(result_steps[0], in_state), arrived)
    layer_out = (residual + moe_out).astype(bf16)
    back_sent = after(back_sent, moe_out)
    back_parts = x_parts(chip_total(back_mine, back_mate, back_sent).astype(bf16))
    back_parts = z_parts(add_parts(back_parts))
    back_low = add_parts(back_parts)
    front_low = after(front_part, back_low)
    front_parts = x_parts(front_low)
    back_low = z_join(after(back_low, front_low))
    front_low = add_parts(after(front_parts, back_low))
    front_low = add_parts(z_parts(front_low))
    back_sum = x_join(after(back_low, front_low))
    front_sum = x_join(z_join(front_low))
    output_sum = back_sum[:, :MODEL_WIDTH]
    router_sum = back_sum[:, MODEL_WIDTH : MODEL_WIDTH + experts_all]
    query_sum = front_sum[:, :MODEL_WIDTH]
    key_sum = front_sum[:, MODEL_WIDTH : MODEL_WIDTH + KV]
    value_sum = front_sum[:, MODEL_WIDTH + KV : QKV]
    at = MODEL_WIDTH + experts_all
    gain_sum = back_sum[:, at : at + 2].T

    rate = 0.5 / math.sqrt(MODEL_WIDTH // 2)
    return (
        layer_out,
        input_grad,
        *adamw_update(gains, gains_first, gains_second, gain_sum, GAIN_RATE, 0.0),
        *adamw_update(query_weight, query_first, query_second, query_sum, rate, DECAY),
        *adamw_update(key_matrix, key_moment_first, key_moment_second, key_sum, rate, DECAY),
        *adamw_update(
            value_matrix,
            value_moment_first,
            value_moment_second,
            value_sum,
            0.5 / math.sqrt(MODEL_WIDTH),
            DECAY,
        ),
        *adamw_update(
            output_weight, output_first, output_second, output_sum, 0.5 / math.sqrt(MODEL_WIDTH // 32), DECAY
        ),
        *adamw_update(
            router_weight, router_first, router_second, router_sum, 0.5 / math.sqrt(4 * MODEL_WIDTH), DECAY
        ),
        *in_state,
        *out_state,
    )


def solution(mesh):
    rows = P(("expert", "fsdp"), None)
    gains = P(None, "fsdp")
    matrix = P("fsdp", None)
    wide = P("expert", "fsdp", None)
    tall = P("expert", None, "fsdp")
    return jax.shard_map(
        body,
        mesh=mesh,
        in_specs=(rows,) * 3 + (gains,) * 3 + (matrix,) * 15 + (wide,) * 3 + (tall,) * 3,
        out_specs=(rows,) * 2 + (gains,) * 3 + (matrix,) * 15 + (wide,) * 3 + (tall,) * 3,
        check_vma=False,
    )
```

```python
import functools
import math

import jax
import jax.numpy as jnp
from jax import lax
from jax.experimental import pallas as pl
from jax.experimental.pallas import tpu as pltpu
from jax.sharding import PartitionSpec as P

MODEL_WIDTH = 1536
QUERY_HEADS = 12
KEY_VALUE_HEADS = 2
HEAD_SIZE = 128
GROUP = QUERY_HEADS // KEY_VALUE_HEADS
FF = 768
STEP = 10
CAP = 80
DEPTH = 4
HALF = MODEL_WIDTH // 2
KV = KEY_VALUE_HEADS * HEAD_SIZE
QKV = MODEL_WIDTH + 2 * KV


NORM_EPS = 1e-05
ROPE_BASE = 10000.0
BETA_ONE = 0.9
BETA_TWO = 0.95
ADAM_EPS = 1e-08
DECAY = 0.1
GAIN_RATE = 0.8
MASKED = -1e30
LOG2E = 1.0 / math.log(2.0)
SCORE_SCALE = 1.0 / math.sqrt(HEAD_SIZE)

f32 = jnp.float32
bf16 = jnp.bfloat16


def dot_nn(left, right):
    return lax.dot_general(left, right, (((1,), (0,)), ((), ())), preferred_element_type=f32)


def dot_nt(left, right):
    return lax.dot_general(left, right, (((1,), (1,)), ((), ())), preferred_element_type=f32)


def dot_tn(left, right):
    return lax.dot_general(left, right, (((0,), (0,)), ((), ())), preferred_element_type=f32)


def after(value, *others):
    return lax.optimization_barrier((value, others))[0]


def params(megabytes, axes):
    return pltpu.CompilerParams(
        vmem_limit_bytes=megabytes * 1024 * 1024, dimension_semantics=("arbitrary",) * axes
    )


def cost(flops, nbytes, trans=0):
    return pl.CostEstimate(flops=int(flops), bytes_accessed=int(nbytes), transcendentals=0)


def causal(score_t):
    key_place = lax.broadcasted_iota(jnp.int32, score_t.shape, 0)
    query_place = lax.broadcasted_iota(jnp.int32, score_t.shape, 1)
    return key_place <= query_place


def attend_kernel(place, pre, cosine, sine, keys, values, out, log_total, turned):
    rows = pre[...]
    query = rows * cosine[...] + pltpu.roll(rows, HEAD_SIZE // 2, 1) * sine[...]
    turned[...] = query.astype(bf16)
    query_t = query.T.astype(bf16)
    factor = SCORE_SCALE * LOG2E

    score = dot_nn(keys[0], query_t) * factor
    score = jnp.where(causal(score), score, MASKED)
    biggest = jnp.max(score, axis=0, keepdims=True)
    weight = jnp.exp2(score - biggest)
    total = jnp.sum(weight, axis=0, keepdims=True)
    acc = dot_nn(values[0].T, weight.astype(bf16))

    def step(back, carry):
        biggest, total, acc = carry
        score = dot_nn(keys[back], query_t) * factor
        larger = jnp.maximum(biggest, jnp.max(score, axis=0, keepdims=True))
        weight = jnp.exp2(score - larger)
        shrink = jnp.exp2(biggest - larger)
        total = total * shrink + jnp.sum(weight, axis=0, keepdims=True)
        acc = acc * shrink + dot_nn(values[back].T, weight.astype(bf16))
        return larger, total, acc

    biggest, total, acc = lax.fori_loop(1, place[0] + 1, step, (biggest, total, acc))
    out[...] = (acc / total).T.astype(bf16)
    log_total[0] = biggest + jnp.log(total) * LOG2E


def attend(place, pre, cosine, sine, kv_blocks):
    token_rows = pre.shape[0]
    blocks = kv_blocks.shape[0]
    width = (token_rows, HEAD_SIZE)
    many = (blocks, token_rows, HEAD_SIZE)
    return pl.pallas_call(
        attend_kernel,
        out_shape=(
            jax.ShapeDtypeStruct((token_rows, MODEL_WIDTH), bf16),
            jax.ShapeDtypeStruct((QUERY_HEADS, 1, token_rows), f32),
            jax.ShapeDtypeStruct((token_rows, MODEL_WIDTH), bf16),
        ),
        grid_spec=pltpu.PrefetchScalarGridSpec(
            num_scalar_prefetch=1,
            grid=(QUERY_HEADS,),
            in_specs=[
                pl.BlockSpec(width, lambda h, p: (0, h)),
                pl.BlockSpec(width, lambda h, p: (0, 0)),
                pl.BlockSpec(width, lambda h, p: (0, 0)),
                pl.BlockSpec(many, lambda h, p: (0, 0, h // GROUP)),
                pl.BlockSpec(many, lambda h, p: (0, 0, KEY_VALUE_HEADS + h // GROUP)),
            ],
            out_specs=(
                pl.BlockSpec(width, lambda h, p: (0, h)),
                pl.BlockSpec((1, 1, token_rows), lambda h, p: (h, 0, 0)),
                pl.BlockSpec(width, lambda h, p: (0, h)),
            ),
        ),
        compiler_params=params(56, 1),
        cost_estimate=cost(1e9, 1e6),
        name="attend",
    )(place, pre, cosine, sine, kv_blocks, kv_blocks)


def attend_back_kernel(
    place, query, keys, values, out, out_grad, log_total, cosine, sine, pre_grad, key_grad, value_grad, key_acc, value_acc
):
    head = pl.program_id(0)

    @pl.when(head % GROUP == 0)
    def _():
        key_acc[...] = jnp.zeros_like(key_acc)
        value_acc[...] = jnp.zeros_like(value_acc)

    factor = SCORE_SCALE * LOG2E
    query_rows = query[...]
    grad_rows = out_grad[...]
    query_t = query_rows.astype(f32).T.astype(bf16)
    grad_t32 = grad_rows.astype(f32).T
    grad_t = grad_t32.astype(bf16)
    row_dot = jnp.sum(out[...].astype(f32).T * grad_t32, axis=0, keepdims=True)
    level = log_total[0]

    def block(back, masked):
        key = keys[back]
        score = dot_nn(key, query_t) * factor - level
        weight = jnp.exp2(score)
        if masked:
            weight = jnp.where(causal(weight), weight, 0.0)
        value_acc[back] += dot_nn(weight.astype(bf16), grad_rows)
        prob_grad = dot_nn(values[back], grad_t)
        score_grad = (weight * (prob_grad - row_dot)).astype(bf16)
        key_acc[back] += dot_nn(score_grad, query_rows)
        return dot_nn(key.T, score_grad)

    query_grad = block(0, True)
    query_grad = lax.fori_loop(1, place[0] + 1, lambda b, acc: acc + block(b, False), query_grad)
    rows = query_grad.T * SCORE_SCALE
    pre_grad[...] = (rows * cosine[...] - pltpu.roll(rows, HEAD_SIZE // 2, 1) * sine[...]).astype(bf16)

    @pl.when(head % GROUP == GROUP - 1)
    def _():
        key_grad[...] = (key_acc[...] * SCORE_SCALE).astype(bf16)
        value_grad[...] = value_acc[...].astype(bf16)


def attend_back(place, query, kv_blocks, out, out_grad, log_total, cosine, sine):
    token_rows = query.shape[0]
    blocks = kv_blocks.shape[0]
    width = (token_rows, HEAD_SIZE)
    many = (blocks, token_rows, HEAD_SIZE)
    return pl.pallas_call(
        attend_back_kernel,
        out_shape=(
            jax.ShapeDtypeStruct((token_rows, MODEL_WIDTH), bf16),
            jax.ShapeDtypeStruct((blocks, token_rows, KV), bf16),
            jax.ShapeDtypeStruct((blocks, token_rows, KV), bf16),
        ),
        grid_spec=pltpu.PrefetchScalarGridSpec(
            num_scalar_prefetch=1,
            grid=(QUERY_HEADS,),
            in_specs=[
                pl.BlockSpec(width, lambda h, p: (0, h)),
                pl.BlockSpec(many, lambda h, p: (0, 0, h // GROUP)),
                pl.BlockSpec(many, lambda h, p: (0, 0, KEY_VALUE_HEADS + h // GROUP)),
                pl.BlockSpec(width, lambda h, p: (0, h)),
                pl.BlockSpec(width, lambda h, p: (0, h)),
                pl.BlockSpec((1, 1, token_rows), lambda h, p: (h, 0, 0)),
                pl.BlockSpec(width, lambda h, p: (0, 0)),
                pl.BlockSpec(width, lambda h, p: (0, 0)),
            ],
            out_specs=(
                pl.BlockSpec(width, lambda h, p: (0, h)),
                pl.BlockSpec(many, lambda h, p: (0, 0, h // GROUP)),
                pl.BlockSpec(many, lambda h, p: (0, 0, h // GROUP)),
            ),
            scratch_shapes=[pltpu.VMEM(many, f32), pltpu.VMEM(many, f32)],
        ),
        compiler_params=params(56, 1),
        cost_estimate=cost(1e9, 1e6),
        name="attend_back",
    )(place, query, kv_blocks, kv_blocks, out, out_grad, log_total, cosine, sine)


def gather_rows(pieces, rows):
    for p, piece in enumerate(pieces):
        rows[p * CAP : (p + 1) * CAP] = piece[...]


def scatter_rows(rows, pieces, at, span):
    low = rows.astype(bf16)
    for p, piece in enumerate(pieces):
        piece[:, at : at + span] = low[p * CAP : (p + 1) * CAP]


def piece_spec():
    return pl.BlockSpec((CAP, MODEL_WIDTH), lambda e, *_: (e, 0))


def row_scratch(count):
    return [pltpu.VMEM((count * CAP, MODEL_WIDTH), bf16)]


def inner_kernel(count, *refs):
    pieces, (down, inner, rows) = refs[:count], refs[count:]
    gather_rows(pieces, rows)
    shards, span = down.shape[0], down.shape[3]
    acc = None
    for c in range(shards):
        term = dot_nt(rows[:, c * span : (c + 1) * span], down[c, 0])
        acc = term if acc is None else acc + term
    inner[0] = acc.astype(bf16)


def inner_rows(pieces, down):
    shards, experts, _, span = down.shape
    rows = len(pieces) * CAP
    return pl.pallas_call(
        functools.partial(inner_kernel, len(pieces)),
        out_shape=jax.ShapeDtypeStruct((experts, rows, FF), bf16),
        grid=(experts,),
        in_specs=[piece_spec()] * len(pieces) + [pl.BlockSpec((shards, 1, FF, span), lambda e: (0, e, 0, 0))],
        out_specs=pl.BlockSpec((1, rows, FF), lambda e: (e, 0, 0)),
        scratch_shapes=row_scratch(len(pieces)),
        compiler_params=params(56, 1),
        cost_estimate=cost(2 * experts * rows * FF * MODEL_WIDTH, 20e6),
        name="inner_rows",
    )(*pieces, down)


def core_kernel(count, *refs):
    pieces, refs = refs[:count], refs[count:]
    gate_up, inner, weight, scaled, gate_side, up_side, gate_dots = refs[:7]
    back, (rows,) = refs[7 : 7 + count], refs[7 + count :]
    gather_rows(pieces, rows)
    span = gate_up.shape[2]
    tile = 256
    factor = weight[0]
    dots = None

    def product(at):
        return dot_nn(rows[...], gate_up[:, 0, :, at : at + tile].reshape(MODEL_WIDTH, tile))

    for n in range(FF // tile):
        at = n * tile
        gate_pre = product(at)
        up_part = product(FF + at)
        sigmoid = 1.0 / (1.0 + jnp.exp(-gate_pre))
        silu = gate_pre * sigmoid
        hidden = silu * up_part
        raw = inner[0, :, at : at + tile].astype(f32)
        part = jnp.sum(raw * hidden, axis=1, keepdims=True)
        dots = part if dots is None else dots + part
        scaled[0, :, at : at + tile] = (hidden * factor).astype(bf16)
        raw = raw * factor
        gate_side[0, :, at : at + tile] = (raw * up_part * (sigmoid + silu * (1.0 - sigmoid))).astype(bf16)
        up_side[0, :, at : at + tile] = (raw * silu).astype(bf16)
    gate_dots[0] = dots

    width = 384
    group = width // span
    for chunk in range(MODEL_WIDTH // width):
        block = gate_up[chunk * group : (chunk + 1) * group, 0].reshape(width, 2 * FF)
        grads = dot_nt(gate_side[0], block[:, :FF]) + dot_nt(up_side[0], block[:, FF:])
        scatter_rows(grads, back, chunk * width, width)


def core_rows(pieces, gate_up, inner, weight):
    count = len(pieces)
    shards, experts, span, _ = gate_up.shape
    rows = count * CAP
    whole = pl.BlockSpec((1, rows, FF), lambda e: (e, 0, 0))
    column = pl.BlockSpec((1, rows, 1), lambda e: (e, 0, 0))
    low = jax.ShapeDtypeStruct((experts, rows, FF), bf16)
    out = pl.pallas_call(
        functools.partial(core_kernel, count),
        out_shape=(low, low, low, jax.ShapeDtypeStruct((experts, rows, 1), f32))
        + (jax.ShapeDtypeStruct(pieces[0].shape, bf16),) * count,
        grid=(experts,),
        in_specs=[piece_spec()] * count
        + [pl.BlockSpec((shards, 1, span, 2 * FF), lambda e: (0, e, 0, 0)), whole, column],
        out_specs=(whole, whole, whole, column) + (piece_spec(),) * count,
        scratch_shapes=row_scratch(len(pieces)),
        compiler_params=params(60, 1),
        cost_estimate=cost(8 * experts * rows * FF * MODEL_WIDTH, 60e6),
        name="core_rows",
    )(*pieces, gate_up, inner, weight)
    return out[0], out[1], out[2], out[3], list(out[4:])


def result_kernel(scaled, down, *pieces):
    width = 384
    shards, span = down.shape[0], down.shape[3]
    group = width // span
    rows = scaled[0]
    for chunk in range(MODEL_WIDTH // width):
        parts = [down[c, 0] for c in range(chunk * group, (chunk + 1) * group)]
        block = parts[0] if group == 1 else jnp.concatenate(parts, axis=1)
        scatter_rows(dot_nn(rows, block), pieces, chunk * width, width)


def result_rows(scaled, down, count):
    experts, rows, _ = scaled.shape
    shards, _, _, span = down.shape
    return list(
        pl.pallas_call(
            result_kernel,
            out_shape=(jax.ShapeDtypeStruct((experts * CAP, MODEL_WIDTH), bf16),) * count,
            grid=(experts,),
            in_specs=[
                pl.BlockSpec((1, rows, FF), lambda e: (e, 0, 0)),
                pl.BlockSpec((shards, 1, FF, span), lambda e: (0, e, 0, 0)),
            ],
            out_specs=(piece_spec(),) * count,
            compiler_params=params(56, 1),
            cost_estimate=cost(2 * experts * rows * FF * MODEL_WIDTH, 22e6),
            name="result_rows",
        )(scaled, down)
    )


def down_grad_kernel(count, *refs):
    pieces, (scaled, out, rows) = refs[:count], refs[count:]
    gather_rows(pieces, rows)
    shards, span = out.shape[0], out.shape[3]
    scaled_t = scaled[0].T
    for c in range(shards):
        out[c, 0] = dot_nn(scaled_t, rows[:, c * span : (c + 1) * span]).astype(bf16)


def down_grads(pieces, scaled, shards):
    experts, rows, _ = scaled.shape
    span = MODEL_WIDTH // shards
    return pl.pallas_call(
        functools.partial(down_grad_kernel, len(pieces)),
        out_shape=jax.ShapeDtypeStruct((shards, experts, FF, span), bf16),
        grid=(experts,),
        in_specs=[piece_spec()] * len(pieces) + [pl.BlockSpec((1, rows, FF), lambda e: (e, 0, 0))],
        out_specs=pl.BlockSpec((shards, 1, FF, span), lambda e: (0, e, 0, 0)),
        scratch_shapes=row_scratch(len(pieces)),
        compiler_params=params(56, 1),
        cost_estimate=cost(2 * experts * rows * FF * MODEL_WIDTH, 22e6),
        name="down_grads",
    )(*pieces, scaled)


def in_grad_kernel(count, *refs):
    pieces, (gate_side, up_side, out, rows) = refs[:count], refs[count:]
    gather_rows(pieces, rows)
    shards, span = out.shape[0], out.shape[2]
    rows_t = rows[...].T
    for c in range(shards):
        part = rows_t[c * span : (c + 1) * span]
        out[c, 0, :, :FF] = dot_nn(part, gate_side[0]).astype(bf16)
        out[c, 0, :, FF:] = dot_nn(part, up_side[0]).astype(bf16)


def in_grads(pieces, gate_side, up_side, shards):
    experts, rows, _ = gate_side.shape
    span = MODEL_WIDTH // shards
    whole = pl.BlockSpec((1, rows, FF), lambda e: (e, 0, 0))
    return pl.pallas_call(
        functools.partial(in_grad_kernel, len(pieces)),
        out_shape=jax.ShapeDtypeStruct((shards, experts, span, 2 * FF), bf16),
        grid=(experts,),
        in_specs=[piece_spec()] * len(pieces) + [whole, whole],
        out_specs=pl.BlockSpec((shards, 1, span, 2 * FF), lambda e: (0, e, 0, 0)),
        scratch_shapes=row_scratch(len(pieces)),
        compiler_params=params(56, 1),
        cost_estimate=cost(4 * experts * rows * FF * MODEL_WIDTH, 35e6),
        name="in_grads",
    )(*pieces, gate_side, up_side)


def ring_kernel(wide, *refs):
    picks, pieces = refs[0], refs[1 : 1 + wide]
    arrived, out = refs[1 + wide : -1], refs[-1]
    rows = jnp.concatenate([piece[...] for piece in pieces], axis=0)
    total = dot_tn(picks[0], rows)
    if arrived:
        total = total + arrived[0][...].astype(f32)
    out[...] = total.astype(out.dtype)


def ring_rows(picks, level, pieces, arrived, last):
    _, many, token_rows = picks.shape
    tile = 512
    side = pl.BlockSpec((token_rows, tile), lambda n: (0, n))
    return pl.pallas_call(
        functools.partial(ring_kernel, len(pieces)),
        out_shape=jax.ShapeDtypeStruct((token_rows, MODEL_WIDTH), f32 if last else bf16),
        grid=(MODEL_WIDTH // tile,),
        in_specs=[pl.BlockSpec((1, many, token_rows), lambda n: (level, 0, 0))]
        + [pl.BlockSpec((p.shape[0], tile), lambda n: (0, n)) for p in pieces]
        + [side] * len(arrived),
        out_specs=side,
        compiler_params=params(48, 1),
        cost_estimate=cost(4 * many * token_rows * HALF, 8e6),
        name="ring_rows",
    )(picks, *pieces, *arrived)


def pick_kernel(picks, rows, own, away):
    per = own.shape[0]
    picked = dot_nn(picks[0], rows[...]).astype(bf16)
    own[...] = picked[:per]
    for r in range(away.shape[0]):
        away[r] = picked[(r + 1) * per : (r + 2) * per]


def pick_rows(picks, level, rows, wide):
    _, many, token_rows = picks.shape
    per = many // wide
    tile = 512
    return pl.pallas_call(
        pick_kernel,
        out_shape=(
            jax.ShapeDtypeStruct((per, MODEL_WIDTH), bf16),
            jax.ShapeDtypeStruct((wide - 1, per, MODEL_WIDTH), bf16),
        ),
        grid=(MODEL_WIDTH // tile,),
        in_specs=[
            pl.BlockSpec((1, many, token_rows), lambda n: (level, 0, 0)),
            pl.BlockSpec((token_rows, tile), lambda n: (0, n)),
        ],
        out_specs=(
            pl.BlockSpec((per, tile), lambda n: (0, n)),
            pl.BlockSpec((wide - 1, per, tile), lambda n: (0, 0, n)),
        ),
        compiler_params=params(32, 1),
        cost_estimate=cost(4 * many * token_rows * HALF, 5e6),
        name="pick_rows",
    )(picks, rows)


def weight_grad_kernel(rows, *refs):
    *grads, out = refs
    rows_t = rows[...].T
    at = 0
    for side in grads:
        if side.dtype == f32:
            out[:, at:] = side[...].T.astype(bf16)
        else:
            columns = side.shape[1]
            out[:, at : at + columns] = dot_nn(rows_t, side[...]).astype(bf16)
            at += columns


def weight_grads(rows, grads, extra=None):
    token_rows = rows.shape[0]
    tile = 384
    extras = [] if extra is None else [extra]
    columns = sum(g.shape[1] for g in grads) + sum(e.shape[0] for e in extras)
    return pl.pallas_call(
        weight_grad_kernel,
        out_shape=jax.ShapeDtypeStruct((MODEL_WIDTH, columns), bf16),
        grid=(MODEL_WIDTH // tile,),
        in_specs=[pl.BlockSpec((token_rows, tile), lambda n: (0, n))]
        + [pl.BlockSpec(g.shape, lambda n: (0, 0)) for g in grads]
        + [pl.BlockSpec((e.shape[0], tile), lambda n: (0, n)) for e in extras],
        out_specs=pl.BlockSpec((tile, columns), lambda n: (n, 0)),
        compiler_params=params(56, 1),
        cost_estimate=cost(2 * MODEL_WIDTH * token_rows * columns, 14e6),
        name="weight_grads",
    )(rows, *grads, *extras)


def keep_and_send(core, pair, mine, theirs):
    first, second = (p.astype(bf16) for p in pair)
    mine(jnp.where(core == 0, first, second))
    theirs(jnp.where(core == 0, second, first))


def core_grad_kernel(core, rows, *refs):
    *grads, mine, theirs = refs
    span = mine.shape[1]
    rows_t = rows[...].T
    at = 0
    for side in grads:
        columns = side.shape[1]
        pair = [dot_nn(rows_t[c * span : (c + 1) * span], side[...]) for c in range(2)]
        where = (0, slice(None), slice(at, at + columns))
        keep_and_send(
            core[0],
            pair,
            functools.partial(mine.__setitem__, where),
            functools.partial(theirs.__setitem__, where),
        )
        at += columns


def core_grads(core, rows, grads, shards):
    token_rows = rows.shape[0]
    span = MODEL_WIDTH // shards
    columns = sum(g.shape[1] for g in grads)
    out = jax.ShapeDtypeStruct((shards // 2, span, columns), bf16)
    block = pl.BlockSpec((1, span, columns), lambda n, c: (n, 0, 0))
    return pl.pallas_call(
        core_grad_kernel,
        out_shape=(out, out),
        grid_spec=pltpu.PrefetchScalarGridSpec(
            num_scalar_prefetch=1,
            grid=(shards // 2,),
            in_specs=[pl.BlockSpec((token_rows, 2 * span), lambda n, c: (0, n))]
            + [pl.BlockSpec(g.shape, lambda n, c: (0, 0)) for g in grads],
            out_specs=(block, block),
        ),
        compiler_params=params(56, 1),
        cost_estimate=cost(2 * MODEL_WIDTH * token_rows * columns, 14e6),
        name="core_grads",
    )(core, rows, *grads)


def adamw_update(weight, moment_one, moment_two, gradient, step_rate, decay_rate):
    first_new = BETA_ONE * moment_one + (1.0 - BETA_ONE) * gradient
    second_new = BETA_TWO * moment_two + (1.0 - BETA_TWO) * gradient * gradient
    first_hat = first_new / (1.0 - BETA_ONE**STEP)
    second_hat = second_new / (1.0 - BETA_TWO**STEP)
    weight_new = weight - step_rate * (
        first_hat / (jnp.sqrt(second_hat) + ADAM_EPS) + decay_rate * weight
    )
    return (weight_new, first_new, second_new)


def body(
    tokens,
    cotangent,
    routes,
    gains,
    gains_first,
    gains_second,
    query_weight,
    query_first,
    query_second,
    key_matrix,
    key_moment_first,
    key_moment_second,
    value_matrix,
    value_moment_first,
    value_moment_second,
    output_weight,
    output_first,
    output_second,
    router_weight,
    router_first,
    router_second,
    expert_in,
    in_first,
    in_second,
    expert_out,
    out_first,
    out_second,
):
    token_rows, top_count = routes.shape
    shards = lax.axis_size("fsdp")
    place = lax.axis_index("fsdp")
    groups = lax.axis_size("expert")
    group = lax.axis_index("expert")
    depth = DEPTH
    wide = groups // depth
    level, column = group // wide, group % wide
    experts_local = expert_in.shape[0]
    experts_all = experts_local * groups
    near = wide * experts_local
    shard_rows = query_weight.shape[0]

    def z_shift(value, by):
        return lax.ppermute(
            value,
            "expert",
            [(a * wide + b, (a + by) % depth * wide + b) for a in range(depth) for b in range(wide)],
        )

    def x_shift(value, by):
        return lax.ppermute(
            value,
            "expert",
            [(a * wide + b, a * wide + (b + by) % wide) for a in range(depth) for b in range(wide)],
        )

    def back_shift(value, by):
        pairs = [(a, a + by) for a in range(shards) if 0 <= a + by < shards]
        return lax.ppermute(value, "fsdp", pairs)

    chips = shards // 2
    chip, core = place // 2, place % 2
    core_arg = core.astype(jnp.int32).reshape(1)

    def core_shift(value, by):
        return lax.ppermute(value, "fsdp", [(a, a // 2 * 2 + (a + by) % 2) for a in range(shards)])

    def y_shift(value, by):
        return lax.ppermute(value, "fsdp", [(a, (a + 2 * by) % shards) for a in range(shards)])

    def y_up(value, by):
        return lax.ppermute(value, "fsdp", [(a, a + 2 * by) for a in range(shards - 2 * by)])

    small = jnp.concatenate(
        [
            router_weight.astype(bf16),
            gains.T.astype(bf16),
            jnp.zeros((shard_rows, 128 - experts_all - 2), bf16),
        ],
        axis=1,
    )
    front_low = lax.all_gather(
        jnp.concatenate(
            [query_weight.astype(bf16), key_matrix.astype(bf16), value_matrix.astype(bf16), small], axis=1
        ),
        "fsdp",
        axis=0,
        tiled=True,
    )
    output_low = lax.all_gather(output_weight.astype(bf16), "fsdp", axis=0, tiled=True)
    qkv_low = front_low[:, :QKV]
    router_low = front_low[:, QKV : QKV + experts_all]
    gain_pair = front_low[:, QKV + experts_all : QKV + experts_all + 2].astype(f32).T
    gain_one, gain_two = gain_pair[0], gain_pair[1]

    routes_t = routes.T
    routes_of = jnp.stack([routes_t] + [z_shift(routes_t, i) for i in range(1, depth)])

    def expert_ids(at_level):
        columns = (column + jnp.arange(wide, dtype=jnp.int32)) % wide
        first_ids = (at_level * wide + columns) * experts_local
        return (first_ids[:, None] + jnp.arange(experts_local, dtype=jnp.int32)[None, :]).reshape(near)

    named = (routes_of[:, None] == expert_ids(level)[None, :, None, None]).astype(f32)
    chosen_here = jnp.sum(named, axis=2)
    earlier = (
        jnp.arange(token_rows, dtype=jnp.int32)[:, None] < jnp.arange(token_rows, dtype=jnp.int32)[None, :]
    ).astype(bf16)
    slots = dot_nn(chosen_here.reshape(depth * near, token_rows).astype(bf16), earlier).reshape(
        depth, near, token_rows
    )
    code = jnp.where(chosen_here > 0, slots.astype(jnp.int32), -1)
    picks = code[:, :, None, :] == jnp.arange(CAP, dtype=jnp.int32)[None, None, :, None]
    picks_low = picks.astype(bf16).reshape(depth, near * CAP, token_rows)

    def pick(rows, k):
        return pick_rows(picks_low, k, rows, wide)

    def swap(picked, *before):
        own, away = picked
        pairs = [own]
        for r in range(1, wide):
            pairs.append(x_shift(after(away[r - 1], pairs[1:], before), r))
        return pairs

    def order(swapped):
        return [swapped[k][r] for r in range(wide) for k in range(depth)]

    def swap_back(pieces, *before):
        steps = [None] * depth
        for m in range(depth):
            k = (m + 1) % depth
            steps[k] = [pieces[k]]
            for r in range(1, wide):
                piece = x_shift(after(pieces[r * depth + k], before), -r)
                steps[k].append(piece)
                if m % 2 == 0:
                    before = (piece,)
        return steps

    def chip_sum(mine, mate, chip):
        return lax.dynamic_index_in_dim(mine, chip, 0, keepdims=False).astype(
            f32
        ) + lax.dynamic_index_in_dim(mate, chip, 0, keepdims=False).astype(f32)

    def chip_low(mine, mate):
        return [chip_sum(mine, mate, (chip + s) % chips).astype(bf16) for s in range(1, chips)]

    def chip_send(low):
        return [y_shift(part, s) for s, part in enumerate(low, 1)]

    def chip_total(mine, mate, sent):
        return functools.reduce(lambda total, part: total + part.astype(f32), sent, chip_sum(mine, mate, chip))

    def ring_send(held):
        return [z_shift(held[-1], 1)]

    def ring_step(held, pieces, arrived=()):
        m = len(held)
        out = ring_rows(picks_low, (m + 1) % depth, pieces, arrived, m == depth - 1)
        if m == depth - 1:
            return out
        held.append(out)

    upstream = cotangent.astype(f32)
    level_one = z_shift(cotangent, 1)
    upstream_swapped = [swap(pick(cotangent, 0))]
    level_one = after(level_one, upstream_swapped)
    picked = pick(level_one, 1)
    upstream_swapped.append(swap(picked, upstream_swapped[-1]))

    inputs = tokens.astype(f32)
    scale_one = lax.rsqrt(jnp.mean(inputs * inputs, axis=1, keepdims=True) + NORM_EPS)
    normed_one = inputs * scale_one
    first_hidden = (normed_one * gain_one).astype(bf16)
    inverse = ROPE_BASE ** (-(jnp.arange(HEAD_SIZE // 2, dtype=f32) * 2.0 / HEAD_SIZE))
    places = (place * token_rows + jnp.arange(token_rows, dtype=jnp.int32)).astype(f32)
    angles = places[:, None] * inverse[None, :]
    half_cos, half_sin = jnp.cos(angles), jnp.sin(angles)
    cosine = jnp.concatenate([half_cos, half_cos], axis=1)
    sine = jnp.concatenate([-half_sin, half_sin], axis=1)

    def turn_keys(rows, sign):
        parts = []
        for h in range(KEY_VALUE_HEADS):
            piece = rows[:, h * HEAD_SIZE : (h + 1) * HEAD_SIZE]
            swapped = jnp.concatenate([piece[:, HEAD_SIZE // 2 :], piece[:, : HEAD_SIZE // 2]], axis=1)
            parts.append(piece * cosine + swapped * (sign * sine))
        return jnp.concatenate(parts, axis=1)

    pre = dot_nn(after(first_hidden, picked), qkv_low)
    keys_local = turn_keys(pre[:, MODEL_WIDTH : MODEL_WIDTH + KV], 1.0).astype(bf16)
    kv_local = jnp.concatenate([keys_local, pre[:, MODEL_WIDTH + KV :].astype(bf16)], axis=1)

    same = [kv_local] + [y_up(kv_local, s) for s in range(1, chips)]
    other = [core_shift(v, 1) for v in same]
    blocks = []
    for distance in range(shards):
        s = distance // 2
        if distance % 2 == 0:
            blocks.append(same[s])
        elif s + 1 < chips:
            blocks.append(jnp.where(core == 1, other[s], other[s + 1]))
        else:
            blocks.append(other[s])
    kv_blocks = jnp.stack(blocks)

    down_low = lax.all_gather(after(expert_out, kv_local).astype(bf16), "fsdp", axis=0)
    gate_up_low = lax.all_gather(after(expert_in, kv_local).astype(bf16), "fsdp", axis=0)

    level_two = after(z_shift(level_one, 1), kv_blocks)
    level_three = z_shift(level_two, 1)

    place_arg = place.astype(jnp.int32).reshape(1)
    attended, log_total, query_rows = attend(
        place_arg, pre, cosine, sine, after(kv_blocks, level_two)
    )
    residual = inputs + dot_nn(after(attended, level_three), output_low)
    scale_two = lax.rsqrt(jnp.mean(residual * residual, axis=1, keepdims=True) + NORM_EPS)
    normed_two = residual * scale_two
    hidden_two = (normed_two * gain_two).astype(bf16)

    upstream_swapped[1] = after(upstream_swapped[1], attended)
    upstream_swapped.append(swap(pick(after(level_two, attended), 2), upstream_swapped[1]))
    last_picked = pick(after(level_three, hidden_two), 3)

    levels = [hidden_two, z_shift(hidden_two, 1)]
    logits_t = lax.dot_general(
        router_low, hidden_two, (((0,), (1,)), ((), ())), preferred_element_type=f32
    )
    all_ids = jnp.arange(experts_all, dtype=jnp.int32)
    chosen_t = (routes_t[:, None, :] == all_ids[None, :, None]).astype(f32)
    gate_weights = jax.nn.softmax(jnp.sum(chosen_t * logits_t[None], axis=1), axis=0)
    gates_of = [gate_weights, z_shift(gate_weights, 1)]
    picked = pick(hidden_two, 0)
    hidden_swapped = [swap(picked, upstream_swapped[-1])]
    levels[1] = after(levels[1], picked)
    picked = pick(levels[1], 1)
    hidden_swapped.append(swap(picked, hidden_swapped[-1]))
    upstream_swapped.append(swap(last_picked, hidden_swapped[-1]))
    for k in range(2, depth):
        levels.append(after(z_shift(levels[-1], 1), picked, gates_of[1]))
        if k == depth - 1:
            upstream_pieces = order(after(upstream_swapped, levels[k - 1]))
            inner = inner_rows(upstream_pieces, down_low)
            gates_of[-1] = after(gates_of[-1], inner)
            levels[k] = after(levels[k], gates_of[-1])
        gates_of.append(z_shift(gates_of[-1], 1))
        picked = pick(levels[k], k)
        hidden_swapped.append(swap(picked, hidden_swapped[-1], upstream_swapped[-1]))
    gates_near = jnp.sum(named * jnp.stack(gates_of)[:, None], axis=2)
    row_gates = jnp.sum(jnp.where(picks, gates_near[:, :, None, :], 0.0), axis=3)
    row_gates = row_gates.reshape(depth, wide, experts_local, CAP)
    away_gates = [x_shift(row_gates[:, r], r) for r in range(1, wide)]
    hidden_swapped, away_gates = after((hidden_swapped, away_gates), levels[-1])
    hidden_pieces = order(hidden_swapped)
    row_gates = jnp.stack([row_gates[:, 0]] + away_gates)
    row_gates = row_gates.transpose(2, 0, 1, 3).reshape(experts_local, wide * depth * CAP, 1)

    scaled_hidden, gate_side, up_side, gate_dots, back_pieces = core_rows(
        hidden_pieces, gate_up_low, inner, row_gates
    )
    steps = swap_back(back_pieces)
    gate_dots = gate_dots.reshape(experts_local, wide, depth, CAP)
    away_dots = [x_shift(gate_dots[:, r], -r) for r in range(1, wide)]
    down_term = down_grads(upstream_pieces, scaled_hidden, shards)
    held = []
    ring_step(held, after(steps[1], down_term))
    out_part = lax.psum_scatter(after(down_term, held[0]), "fsdp", scatter_dimension=0)
    arrived = ring_send(held)
    in_term = in_grads(hidden_pieces, *after((gate_side, up_side), held[0]), shards)
    gate_dots = jnp.stack([gate_dots[:, 0]] + after(away_dots, in_term))
    gate_dots = gate_dots.transpose(2, 0, 1, 3).reshape(depth, near, CAP)
    token_dots = jnp.sum(jnp.where(picks, gate_dots[:, :, :, None], 0.0), axis=2)
    choice_dots = jnp.sum(named * token_dots[:, :, None, :], axis=1)
    lane = z_shift(choice_dots[1], 1)
    ring_step(held, after(steps[2], in_term, lane), arrived)
    in_part = lax.psum_scatter(after(in_term, held[1]), "fsdp", scatter_dimension=0)
    lane = z_shift(lane + choice_dots[2], 1)
    arrived = ring_send(held)
    results = result_rows(after(scaled_hidden, held[1]), down_low, len(back_pieces))
    ring_step(held, after(steps[3], results, lane), arrived)
    result_steps = swap_back(results, steps[0])
    lane = z_shift(lane + choice_dots[3], 1)
    arrived = ring_send(held)
    gate_grad = lane + choice_dots[0]
    picked_grad = gate_weights * (
        gate_grad - jnp.sum(gate_weights * gate_grad, axis=0, keepdims=True)
    )
    logit_grad_t = jnp.sum(chosen_t * picked_grad[:, None, :], axis=0).astype(bf16)
    router_term = dot_nn(logit_grad_t, hidden_two)
    hidden_back = ring_step(held, after(steps[0], router_term), arrived)
    hidden_two_grad = hidden_back + lax.dot_general(
        logit_grad_t, router_low, (((0,), (1,)), ((), ())), preferred_element_type=f32
    )

    gain_two_term = jnp.sum(hidden_two_grad * normed_two, axis=0)
    scaled_two = hidden_two_grad * gain_two
    residual_grad = upstream + scale_two * (
        scaled_two - normed_two * jnp.mean(scaled_two * normed_two, axis=1, keepdims=True)
    )
    branch_grad = residual_grad.astype(bf16)
    attended_grad = dot_nt(branch_grad, output_low).astype(bf16)
    result_held = []
    ring_step(result_held, after(result_steps[1], hidden_back))
    attended_grad = after(attended_grad, result_held[0], out_part)
    arrived = ring_send(result_held)
    pre_grad, key_back, value_back = attend_back(
        place_arg, query_rows, kv_blocks, attended, attended_grad, log_total, cosine, sine
    )

    def send_parts(parts, index, shift):
        count = parts.shape[0]
        return [lax.dynamic_index_in_dim(parts, index, 0, keepdims=False)] + [
            shift(lax.dynamic_index_in_dim(parts, (index + s) % count, 0, keepdims=False), s)
            for s in range(1, count)
        ]

    def add_parts(parts):
        return functools.reduce(lambda total, part: total + part.astype(f32), parts[1:], parts[0].astype(f32)).astype(bf16)

    def join(part, index, count, shift):
        whole = jnp.zeros((count,) + part.shape, part.dtype)
        for s in range(count):
            piece = shift(part, s) if s else part
            whole = lax.dynamic_update_index_in_dim(whole, piece, (index - s) % count, 0)
        return whole

    def x_parts(part):
        return send_parts(part.reshape(wide, shard_rows // wide, part.shape[1]), column, x_shift)

    def z_parts(part):
        return send_parts(part.reshape(depth, shard_rows // wide // depth, part.shape[1]), level, z_shift)

    def z_join(part):
        return join(part, level, depth, z_shift).reshape(shard_rows // wide, part.shape[1])

    def x_join(part):
        return join(part, column, wide, x_shift).reshape(shard_rows, part.shape[1]).astype(f32)

    kv_back = jnp.concatenate([key_back, value_back], axis=2)
    none = jnp.zeros_like(kv_back[:1])
    mate = jnp.where(core == 1, kv_back[1::2], jnp.concatenate([none, kv_back[1:-1:2]], axis=0))
    mate = core_shift(mate, 1)
    kv_chip = kv_back[0::2].astype(f32) + mate.astype(f32)
    kv_low = kv_chip.astype(bf16)
    kv_parts = [
        lax.ppermute(kv_low[s], "fsdp", [(a + 2 * s, a) for a in range(shards - 2 * s)]) for s in range(1, chips)
    ]
    back_mine, back_mate = core_grads(core_arg, attended, [after(branch_grad, kv_low)], shards)
    back_mate = core_shift(back_mate, 1)
    out_state = adamw_update(
        expert_out,
        out_first,
        out_second,
        after(out_part, back_mine).astype(f32),
        0.5 / math.sqrt(FF // 8),
        DECAY,
    )
    ring_step(result_held, after(result_steps[2], out_state), arrived)
    arrived = ring_send(result_held)
    back_low = chip_low(back_mine, after(back_mate, result_held[1]))
    back_sent = chip_send(back_low)
    kv_parts = after(kv_parts, back_low)
    kv_grad = functools.reduce(lambda total, part: total + part.astype(f32), kv_parts, kv_chip[0])
    key_pre_grad = turn_keys(kv_grad[:, :KV], -1.0)
    kv_pre_grad = jnp.concatenate([key_pre_grad, kv_grad[:, KV:]], axis=1).astype(bf16)

    front_terms = weight_grads(first_hidden, [pre_grad, kv_pre_grad])
    front_part = lax.psum_scatter(front_terms, "fsdp", scatter_dimension=0, tiled=True)
    ring_step(result_held, after(result_steps[3], front_terms), arrived)
    arrived = ring_send(result_held)
    pre_late, kv_late = after((pre_grad, kv_pre_grad), result_held[2])
    hidden_one_grad = dot_nt(pre_late, qkv_low[:, :MODEL_WIDTH]) + dot_nt(kv_late, qkv_low[:, MODEL_WIDTH:])
    gain_one_term = jnp.sum(hidden_one_grad * normed_one, axis=0)
    scaled_one = hidden_one_grad * gain_one
    input_grad = (
        residual_grad
        + scale_one
        * (scaled_one - normed_one * jnp.mean(scaled_one * normed_one, axis=1, keepdims=True))
    ).astype(bf16)
    extra = jnp.concatenate(
        [
            router_term,
            gain_one_term[None],
            gain_two_term[None],
            jnp.zeros((126 - experts_all, MODEL_WIDTH), f32),
        ],
        axis=0,
    )
    extra = extra.T.astype(bf16).reshape(chips, 2, shard_rows, 128)
    extra_mine = jnp.where(core == 0, extra[:, 0], extra[:, 1])
    extra_mate = core_shift(jnp.where(core == 0, extra[:, 1], extra[:, 0]), 1)
    extra_sent = chip_send(chip_low(extra_mine, extra_mate))
    back_sent = after(back_sent, extra_mine)
    back_low = chip_total(back_mine, back_mate, back_sent).astype(bf16)
    back_parts = x_parts(back_low)
    in_state = adamw_update(
        expert_in,
        in_first,
        in_second,
        after(in_part, back_low).astype(f32),
        0.5 / math.sqrt(MODEL_WIDTH),
        DECAY,
    )
    moe_out = ring_step(result_held, after(result_steps[0], in_state), arrived)
    layer_out = (residual + moe_out).astype(bf16)
    back_low = add_parts(z_parts(add_parts(after(back_parts, moe_out))))
    back_low = z_join(back_low)
    extra_low = chip_total(extra_mine, extra_mate, after(extra_sent, moe_out)).astype(bf16)
    front_low = jnp.concatenate([after(front_part, back_low), extra_low], axis=1)
    back_sum = x_join(back_low)
    front_low = add_parts(x_parts(front_low))
    front_low = add_parts(z_parts(front_low))
    front_sum = x_join(z_join(front_low))
    output_sum = back_sum
    router_sum = front_sum[:, QKV : QKV + experts_all]
    query_sum = front_sum[:, :MODEL_WIDTH]
    key_sum = front_sum[:, MODEL_WIDTH : MODEL_WIDTH + KV]
    value_sum = front_sum[:, MODEL_WIDTH + KV : QKV]
    gain_sum = front_sum[:, QKV + experts_all : QKV + experts_all + 2].T

    rate = 0.5 / math.sqrt(MODEL_WIDTH // 2)
    return (
        layer_out,
        input_grad,
        *adamw_update(gains, gains_first, gains_second, gain_sum, GAIN_RATE, 0.0),
        *adamw_update(query_weight, query_first, query_second, query_sum, rate, DECAY),
        *adamw_update(key_matrix, key_moment_first, key_moment_second, key_sum, rate, DECAY),
        *adamw_update(
            value_matrix,
            value_moment_first,
            value_moment_second,
            value_sum,
            0.5 / math.sqrt(MODEL_WIDTH),
            DECAY,
        ),
        *adamw_update(
            output_weight, output_first, output_second, output_sum, 0.5 / math.sqrt(MODEL_WIDTH // 32), DECAY
        ),
        *adamw_update(
            router_weight, router_first, router_second, router_sum, 0.5 / math.sqrt(4 * MODEL_WIDTH), DECAY
        ),
        *in_state,
        *out_state,
    )


def solution(mesh):
    rows = P(("expert", "fsdp"), None)
    gains = P(None, "fsdp")
    matrix = P("fsdp", None)
    wide = P("expert", "fsdp", None)
    tall = P("expert", None, "fsdp")
    return jax.shard_map(
        body,
        mesh=mesh,
        in_specs=(rows,) * 3 + (gains,) * 3 + (matrix,) * 15 + (wide,) * 3 + (tall,) * 3,
        out_specs=(rows,) * 2 + (gains,) * 3 + (matrix,) * 15 + (wide,) * 3 + (tall,) * 3,
        check_vma=False,
    )
```

```python
import functools
import math

import jax
import jax.numpy as jnp
from jax import lax
from jax.experimental import pallas as pl
from jax.experimental.pallas import tpu as pltpu
from jax.sharding import PartitionSpec as P

MODEL_WIDTH = 1536
QUERY_HEADS = 12
KEY_VALUE_HEADS = 2
HEAD_SIZE = 128
GROUP = QUERY_HEADS // KEY_VALUE_HEADS
FF = 768
STEP = 10
CAP = 80
DEPTH = 4
HALF = MODEL_WIDTH // 2
KV = KEY_VALUE_HEADS * HEAD_SIZE
QKV = MODEL_WIDTH + 2 * KV


NORM_EPS = 1e-05
ROPE_BASE = 10000.0
BETA_ONE = 0.9
BETA_TWO = 0.95
ADAM_EPS = 1e-08
DECAY = 0.1
GAIN_RATE = 0.8
MASKED = -1e30
LOG2E = 1.0 / math.log(2.0)
SCORE_SCALE = 1.0 / math.sqrt(HEAD_SIZE)

f32 = jnp.float32
bf16 = jnp.bfloat16


def dot_nn(left, right):
    return lax.dot_general(left, right, (((1,), (0,)), ((), ())), preferred_element_type=f32)


def dot_nt(left, right):
    return lax.dot_general(left, right, (((1,), (1,)), ((), ())), preferred_element_type=f32)


def dot_tn(left, right):
    return lax.dot_general(left, right, (((0,), (0,)), ((), ())), preferred_element_type=f32)


def after(value, *others):
    return lax.optimization_barrier((value, others))[0]


def params(megabytes, axes):
    return pltpu.CompilerParams(
        vmem_limit_bytes=megabytes * 1024 * 1024, dimension_semantics=("arbitrary",) * axes
    )


def cost(flops, nbytes, trans=0):
    return pl.CostEstimate(flops=int(flops), bytes_accessed=int(nbytes), transcendentals=0)


def causal(score_t):
    key_place = lax.broadcasted_iota(jnp.int32, score_t.shape, 0)
    query_place = lax.broadcasted_iota(jnp.int32, score_t.shape, 1)
    return key_place <= query_place


def attend_kernel(place, pre, cosine, sine, keys, values, out, log_total, turned):
    rows = pre[...]
    query = rows * cosine[...] + pltpu.roll(rows, HEAD_SIZE // 2, 1) * sine[...]
    turned[...] = query.astype(bf16)
    query_t = query.T.astype(bf16)
    factor = SCORE_SCALE * LOG2E

    score = dot_nn(keys[0], query_t) * factor
    score = jnp.where(causal(score), score, MASKED)
    biggest = jnp.max(score, axis=0, keepdims=True)
    weight = jnp.exp2(score - biggest)
    total = jnp.sum(weight, axis=0, keepdims=True)
    acc = dot_nn(values[0].T, weight.astype(bf16))

    def step(back, carry):
        biggest, total, acc = carry
        score = dot_nn(keys[back], query_t) * factor
        larger = jnp.maximum(biggest, jnp.max(score, axis=0, keepdims=True))
        weight = jnp.exp2(score - larger)
        shrink = jnp.exp2(biggest - larger)
        total = total * shrink + jnp.sum(weight, axis=0, keepdims=True)
        acc = acc * shrink + dot_nn(values[back].T, weight.astype(bf16))
        return larger, total, acc

    biggest, total, acc = lax.fori_loop(1, place[0] + 1, step, (biggest, total, acc))
    out[...] = (acc / total).T.astype(bf16)
    log_total[0] = biggest + jnp.log(total) * LOG2E


def attend(place, pre, cosine, sine, kv_blocks):
    token_rows = pre.shape[0]
    blocks = kv_blocks.shape[0]
    width = (token_rows, HEAD_SIZE)
    many = (blocks, token_rows, HEAD_SIZE)
    return pl.pallas_call(
        attend_kernel,
        out_shape=(
            jax.ShapeDtypeStruct((token_rows, MODEL_WIDTH), bf16),
            jax.ShapeDtypeStruct((QUERY_HEADS, 1, token_rows), f32),
            jax.ShapeDtypeStruct((token_rows, MODEL_WIDTH), bf16),
        ),
        grid_spec=pltpu.PrefetchScalarGridSpec(
            num_scalar_prefetch=1,
            grid=(QUERY_HEADS,),
            in_specs=[
                pl.BlockSpec(width, lambda h, p: (0, h)),
                pl.BlockSpec(width, lambda h, p: (0, 0)),
                pl.BlockSpec(width, lambda h, p: (0, 0)),
                pl.BlockSpec(many, lambda h, p: (0, 0, h // GROUP)),
                pl.BlockSpec(many, lambda h, p: (0, 0, KEY_VALUE_HEADS + h // GROUP)),
            ],
            out_specs=(
                pl.BlockSpec(width, lambda h, p: (0, h)),
                pl.BlockSpec((1, 1, token_rows), lambda h, p: (h, 0, 0)),
                pl.BlockSpec(width, lambda h, p: (0, h)),
            ),
        ),
        compiler_params=params(56, 1),
        cost_estimate=cost(1e9, 1e6),
        name="attend",
    )(place, pre, cosine, sine, kv_blocks, kv_blocks)


def attend_back_kernel(
    place, query, keys, values, out, out_grad, log_total, cosine, sine, pre_grad, key_grad, value_grad, key_acc, value_acc
):
    head = pl.program_id(0)

    @pl.when(head % GROUP == 0)
    def _():
        key_acc[...] = jnp.zeros_like(key_acc)
        value_acc[...] = jnp.zeros_like(value_acc)

    factor = SCORE_SCALE * LOG2E
    query_rows = query[...]
    grad_rows = out_grad[...]
    query_t = query_rows.astype(f32).T.astype(bf16)
    grad_t32 = grad_rows.astype(f32).T
    grad_t = grad_t32.astype(bf16)
    row_dot = jnp.sum(out[...].astype(f32).T * grad_t32, axis=0, keepdims=True)
    level = log_total[0]

    def block(back, masked):
        key = keys[back]
        score = dot_nn(key, query_t) * factor - level
        weight = jnp.exp2(score)
        if masked:
            weight = jnp.where(causal(weight), weight, 0.0)
        value_acc[back] += dot_nn(weight.astype(bf16), grad_rows)
        prob_grad = dot_nn(values[back], grad_t)
        score_grad = (weight * (prob_grad - row_dot)).astype(bf16)
        key_acc[back] += dot_nn(score_grad, query_rows)
        return dot_nn(key.T, score_grad)

    query_grad = block(0, True)
    query_grad = lax.fori_loop(1, place[0] + 1, lambda b, acc: acc + block(b, False), query_grad)
    rows = query_grad.T * SCORE_SCALE
    pre_grad[...] = (rows * cosine[...] - pltpu.roll(rows, HEAD_SIZE // 2, 1) * sine[...]).astype(bf16)

    @pl.when(head % GROUP == GROUP - 1)
    def _():
        key_grad[...] = (key_acc[...] * SCORE_SCALE).astype(bf16)
        value_grad[...] = value_acc[...].astype(bf16)


def attend_back(place, query, kv_blocks, out, out_grad, log_total, cosine, sine):
    token_rows = query.shape[0]
    blocks = kv_blocks.shape[0]
    width = (token_rows, HEAD_SIZE)
    many = (blocks, token_rows, HEAD_SIZE)
    return pl.pallas_call(
        attend_back_kernel,
        out_shape=(
            jax.ShapeDtypeStruct((token_rows, MODEL_WIDTH), bf16),
            jax.ShapeDtypeStruct((blocks, token_rows, KV), bf16),
            jax.ShapeDtypeStruct((blocks, token_rows, KV), bf16),
        ),
        grid_spec=pltpu.PrefetchScalarGridSpec(
            num_scalar_prefetch=1,
            grid=(QUERY_HEADS,),
            in_specs=[
                pl.BlockSpec(width, lambda h, p: (0, h)),
                pl.BlockSpec(many, lambda h, p: (0, 0, h // GROUP)),
                pl.BlockSpec(many, lambda h, p: (0, 0, KEY_VALUE_HEADS + h // GROUP)),
                pl.BlockSpec(width, lambda h, p: (0, h)),
                pl.BlockSpec(width, lambda h, p: (0, h)),
                pl.BlockSpec((1, 1, token_rows), lambda h, p: (h, 0, 0)),
                pl.BlockSpec(width, lambda h, p: (0, 0)),
                pl.BlockSpec(width, lambda h, p: (0, 0)),
            ],
            out_specs=(
                pl.BlockSpec(width, lambda h, p: (0, h)),
                pl.BlockSpec(many, lambda h, p: (0, 0, h // GROUP)),
                pl.BlockSpec(many, lambda h, p: (0, 0, h // GROUP)),
            ),
            scratch_shapes=[pltpu.VMEM(many, f32), pltpu.VMEM(many, f32)],
        ),
        compiler_params=params(56, 1),
        cost_estimate=cost(1e9, 1e6),
        name="attend_back",
    )(place, query, kv_blocks, kv_blocks, out, out_grad, log_total, cosine, sine)


def gather_rows(pieces, rows):
    for p, piece in enumerate(pieces):
        rows[p * CAP : (p + 1) * CAP] = piece[...]


def scatter_rows(rows, pieces, at, span):
    low = rows.astype(bf16)
    for p, piece in enumerate(pieces):
        piece[:, at : at + span] = low[p * CAP : (p + 1) * CAP]


def piece_spec():
    return pl.BlockSpec((CAP, MODEL_WIDTH), lambda e, *_: (e, 0))


def row_scratch(count):
    return [pltpu.VMEM((count * CAP, MODEL_WIDTH), bf16)]


def inner_kernel(count, *refs):
    pieces, (down, inner, rows) = refs[:count], refs[count:]
    gather_rows(pieces, rows)
    shards, span = down.shape[0], down.shape[3]
    acc = None
    for c in range(shards):
        term = dot_nt(rows[:, c * span : (c + 1) * span], down[c, 0])
        acc = term if acc is None else acc + term
    inner[0] = acc.astype(bf16)


def inner_rows(pieces, down):
    shards, experts, _, span = down.shape
    rows = len(pieces) * CAP
    return pl.pallas_call(
        functools.partial(inner_kernel, len(pieces)),
        out_shape=jax.ShapeDtypeStruct((experts, rows, FF), bf16),
        grid=(experts,),
        in_specs=[piece_spec()] * len(pieces) + [pl.BlockSpec((shards, 1, FF, span), lambda e: (0, e, 0, 0))],
        out_specs=pl.BlockSpec((1, rows, FF), lambda e: (e, 0, 0)),
        scratch_shapes=row_scratch(len(pieces)),
        compiler_params=params(56, 1),
        cost_estimate=cost(2 * experts * rows * FF * MODEL_WIDTH, 20e6),
        name="inner_rows",
    )(*pieces, down)


def core_kernel(count, *refs):
    pieces, refs = refs[:count], refs[count:]
    gate_up, inner, weight, scaled, gate_side, up_side, gate_dots = refs[:7]
    back, (rows,) = refs[7 : 7 + count], refs[7 + count :]
    gather_rows(pieces, rows)
    span = gate_up.shape[2]
    tile = 256
    factor = weight[0]
    dots = None

    def product(at):
        return dot_nn(rows[...], gate_up[:, 0, :, at : at + tile].reshape(MODEL_WIDTH, tile))

    for n in range(FF // tile):
        at = n * tile
        gate_pre = product(at)
        up_part = product(FF + at)
        sigmoid = 1.0 / (1.0 + jnp.exp(-gate_pre))
        silu = gate_pre * sigmoid
        hidden = silu * up_part
        raw = inner[0, :, at : at + tile].astype(f32)
        part = jnp.sum(raw * hidden, axis=1, keepdims=True)
        dots = part if dots is None else dots + part
        scaled[0, :, at : at + tile] = (hidden * factor).astype(bf16)
        raw = raw * factor
        gate_side[0, :, at : at + tile] = (raw * up_part * (sigmoid + silu * (1.0 - sigmoid))).astype(bf16)
        up_side[0, :, at : at + tile] = (raw * silu).astype(bf16)
    gate_dots[0] = dots

    width = 384
    group = width // span
    for chunk in range(MODEL_WIDTH // width):
        block = gate_up[chunk * group : (chunk + 1) * group, 0].reshape(width, 2 * FF)
        grads = dot_nt(gate_side[0], block[:, :FF]) + dot_nt(up_side[0], block[:, FF:])
        scatter_rows(grads, back, chunk * width, width)


def core_rows(pieces, gate_up, inner, weight):
    count = len(pieces)
    shards, experts, span, _ = gate_up.shape
    rows = count * CAP
    whole = pl.BlockSpec((1, rows, FF), lambda e: (e, 0, 0))
    column = pl.BlockSpec((1, rows, 1), lambda e: (e, 0, 0))
    low = jax.ShapeDtypeStruct((experts, rows, FF), bf16)
    out = pl.pallas_call(
        functools.partial(core_kernel, count),
        out_shape=(low, low, low, jax.ShapeDtypeStruct((experts, rows, 1), f32))
        + (jax.ShapeDtypeStruct(pieces[0].shape, bf16),) * count,
        grid=(experts,),
        in_specs=[piece_spec()] * count
        + [pl.BlockSpec((shards, 1, span, 2 * FF), lambda e: (0, e, 0, 0)), whole, column],
        out_specs=(whole, whole, whole, column) + (piece_spec(),) * count,
        scratch_shapes=row_scratch(len(pieces)),
        compiler_params=params(60, 1),
        cost_estimate=cost(8 * experts * rows * FF * MODEL_WIDTH, 60e6),
        name="core_rows",
    )(*pieces, gate_up, inner, weight)
    return out[0], out[1], out[2], out[3], list(out[4:])


def result_kernel(scaled, down, *pieces):
    width = 384
    shards, span = down.shape[0], down.shape[3]
    group = width // span
    rows = scaled[0]
    for chunk in range(MODEL_WIDTH // width):
        parts = [down[c, 0] for c in range(chunk * group, (chunk + 1) * group)]
        block = parts[0] if group == 1 else jnp.concatenate(parts, axis=1)
        scatter_rows(dot_nn(rows, block), pieces, chunk * width, width)


def result_rows(scaled, down, count):
    experts, rows, _ = scaled.shape
    shards, _, _, span = down.shape
    return list(
        pl.pallas_call(
            result_kernel,
            out_shape=(jax.ShapeDtypeStruct((experts * CAP, MODEL_WIDTH), bf16),) * count,
            grid=(experts,),
            in_specs=[
                pl.BlockSpec((1, rows, FF), lambda e: (e, 0, 0)),
                pl.BlockSpec((shards, 1, FF, span), lambda e: (0, e, 0, 0)),
            ],
            out_specs=(piece_spec(),) * count,
            compiler_params=params(56, 1),
            cost_estimate=cost(2 * experts * rows * FF * MODEL_WIDTH, 22e6),
            name="result_rows",
        )(scaled, down)
    )


def down_grad_kernel(count, *refs):
    pieces, (scaled, out, rows) = refs[:count], refs[count:]
    gather_rows(pieces, rows)
    shards, span = out.shape[0], out.shape[3]
    scaled_t = scaled[0].T
    for c in range(shards):
        out[c, 0] = dot_nn(scaled_t, rows[:, c * span : (c + 1) * span]).astype(bf16)


def down_grads(pieces, scaled, shards):
    experts, rows, _ = scaled.shape
    span = MODEL_WIDTH // shards
    return pl.pallas_call(
        functools.partial(down_grad_kernel, len(pieces)),
        out_shape=jax.ShapeDtypeStruct((shards, experts, FF, span), bf16),
        grid=(experts,),
        in_specs=[piece_spec()] * len(pieces) + [pl.BlockSpec((1, rows, FF), lambda e: (e, 0, 0))],
        out_specs=pl.BlockSpec((shards, 1, FF, span), lambda e: (0, e, 0, 0)),
        scratch_shapes=row_scratch(len(pieces)),
        compiler_params=params(56, 1),
        cost_estimate=cost(2 * experts * rows * FF * MODEL_WIDTH, 22e6),
        name="down_grads",
    )(*pieces, scaled)


def in_grad_kernel(count, *refs):
    pieces, (gate_side, up_side, out, rows) = refs[:count], refs[count:]
    gather_rows(pieces, rows)
    shards, span = out.shape[0], out.shape[2]
    rows_t = rows[...].T
    for c in range(shards):
        part = rows_t[c * span : (c + 1) * span]
        out[c, 0, :, :FF] = dot_nn(part, gate_side[0]).astype(bf16)
        out[c, 0, :, FF:] = dot_nn(part, up_side[0]).astype(bf16)


def in_grads(pieces, gate_side, up_side, shards):
    experts, rows, _ = gate_side.shape
    span = MODEL_WIDTH // shards
    whole = pl.BlockSpec((1, rows, FF), lambda e: (e, 0, 0))
    return pl.pallas_call(
        functools.partial(in_grad_kernel, len(pieces)),
        out_shape=jax.ShapeDtypeStruct((shards, experts, span, 2 * FF), bf16),
        grid=(experts,),
        in_specs=[piece_spec()] * len(pieces) + [whole, whole],
        out_specs=pl.BlockSpec((shards, 1, span, 2 * FF), lambda e: (0, e, 0, 0)),
        scratch_shapes=row_scratch(len(pieces)),
        compiler_params=params(56, 1),
        cost_estimate=cost(4 * experts * rows * FF * MODEL_WIDTH, 35e6),
        name="in_grads",
    )(*pieces, gate_side, up_side)


def ring_kernel(wide, *refs):
    picks, pieces = refs[0], refs[1 : 1 + wide]
    arrived, out = refs[1 + wide : -1], refs[-1]
    rows = jnp.concatenate([piece[...] for piece in pieces], axis=0)
    total = dot_tn(picks[0], rows)
    if arrived:
        total = total + arrived[0][...].astype(f32)
    out[...] = total.astype(out.dtype)


def ring_rows(picks, level, pieces, arrived, last):
    _, many, token_rows = picks.shape
    tile = 512
    side = pl.BlockSpec((token_rows, tile), lambda n: (0, n))
    return pl.pallas_call(
        functools.partial(ring_kernel, len(pieces)),
        out_shape=jax.ShapeDtypeStruct((token_rows, MODEL_WIDTH), f32 if last else bf16),
        grid=(MODEL_WIDTH // tile,),
        in_specs=[pl.BlockSpec((1, many, token_rows), lambda n: (level, 0, 0))]
        + [pl.BlockSpec((p.shape[0], tile), lambda n: (0, n)) for p in pieces]
        + [side] * len(arrived),
        out_specs=side,
        compiler_params=params(48, 1),
        cost_estimate=cost(4 * many * token_rows * HALF, 8e6),
        name="ring_rows",
    )(picks, *pieces, *arrived)


def pick_kernel(picks, rows, own, away):
    per = own.shape[0]
    picked = dot_nn(picks[0], rows[...]).astype(bf16)
    own[...] = picked[:per]
    for r in range(away.shape[0]):
        away[r] = picked[(r + 1) * per : (r + 2) * per]


def pick_rows(picks, level, rows, wide):
    _, many, token_rows = picks.shape
    per = many // wide
    tile = 512
    return pl.pallas_call(
        pick_kernel,
        out_shape=(
            jax.ShapeDtypeStruct((per, MODEL_WIDTH), bf16),
            jax.ShapeDtypeStruct((wide - 1, per, MODEL_WIDTH), bf16),
        ),
        grid=(MODEL_WIDTH // tile,),
        in_specs=[
            pl.BlockSpec((1, many, token_rows), lambda n: (level, 0, 0)),
            pl.BlockSpec((token_rows, tile), lambda n: (0, n)),
        ],
        out_specs=(
            pl.BlockSpec((per, tile), lambda n: (0, n)),
            pl.BlockSpec((wide - 1, per, tile), lambda n: (0, 0, n)),
        ),
        compiler_params=params(32, 1),
        cost_estimate=cost(4 * many * token_rows * HALF, 5e6),
        name="pick_rows",
    )(picks, rows)


def weight_grad_kernel(rows, *refs):
    *grads, out = refs
    rows_t = rows[...].T
    at = 0
    for side in grads:
        if side.dtype == f32:
            out[:, at:] = side[...].T.astype(bf16)
        else:
            columns = side.shape[1]
            out[:, at : at + columns] = dot_nn(rows_t, side[...]).astype(bf16)
            at += columns


def weight_grads(rows, grads, extra=None):
    token_rows = rows.shape[0]
    tile = 384
    extras = [] if extra is None else [extra]
    columns = sum(g.shape[1] for g in grads) + sum(e.shape[0] for e in extras)
    return pl.pallas_call(
        weight_grad_kernel,
        out_shape=jax.ShapeDtypeStruct((MODEL_WIDTH, columns), bf16),
        grid=(MODEL_WIDTH // tile,),
        in_specs=[pl.BlockSpec((token_rows, tile), lambda n: (0, n))]
        + [pl.BlockSpec(g.shape, lambda n: (0, 0)) for g in grads]
        + [pl.BlockSpec((e.shape[0], tile), lambda n: (0, n)) for e in extras],
        out_specs=pl.BlockSpec((tile, columns), lambda n: (n, 0)),
        compiler_params=params(56, 1),
        cost_estimate=cost(2 * MODEL_WIDTH * token_rows * columns, 14e6),
        name="weight_grads",
    )(rows, *grads, *extras)


def keep_and_send(core, pair, mine, theirs):
    first, second = (p.astype(bf16) for p in pair)
    mine(jnp.where(core == 0, first, second))
    theirs(jnp.where(core == 0, second, first))


def core_grad_kernel(core, rows, *refs):
    *grads, mine, theirs = refs
    span = mine.shape[1]
    rows_t = rows[...].T
    at = 0
    for side in grads:
        columns = side.shape[1]
        pair = [dot_nn(rows_t[c * span : (c + 1) * span], side[...]) for c in range(2)]
        where = (0, slice(None), slice(at, at + columns))
        keep_and_send(
            core[0],
            pair,
            functools.partial(mine.__setitem__, where),
            functools.partial(theirs.__setitem__, where),
        )
        at += columns


def core_grads(core, rows, grads, shards):
    token_rows = rows.shape[0]
    span = MODEL_WIDTH // shards
    columns = sum(g.shape[1] for g in grads)
    out = jax.ShapeDtypeStruct((shards // 2, span, columns), bf16)
    block = pl.BlockSpec((1, span, columns), lambda n, c: (n, 0, 0))
    return pl.pallas_call(
        core_grad_kernel,
        out_shape=(out, out),
        grid_spec=pltpu.PrefetchScalarGridSpec(
            num_scalar_prefetch=1,
            grid=(shards // 2,),
            in_specs=[pl.BlockSpec((token_rows, 2 * span), lambda n, c: (0, n))]
            + [pl.BlockSpec(g.shape, lambda n, c: (0, 0)) for g in grads],
            out_specs=(block, block),
        ),
        compiler_params=params(56, 1),
        cost_estimate=cost(2 * MODEL_WIDTH * token_rows * columns, 14e6),
        name="core_grads",
    )(core, rows, *grads)


def adamw_update(weight, moment_one, moment_two, gradient, step_rate, decay_rate):
    first_new = BETA_ONE * moment_one + (1.0 - BETA_ONE) * gradient
    second_new = BETA_TWO * moment_two + (1.0 - BETA_TWO) * gradient * gradient
    first_hat = first_new / (1.0 - BETA_ONE**STEP)
    second_hat = second_new / (1.0 - BETA_TWO**STEP)
    weight_new = weight - step_rate * (
        first_hat / (jnp.sqrt(second_hat) + ADAM_EPS) + decay_rate * weight
    )
    return (weight_new, first_new, second_new)


def body(
    tokens,
    cotangent,
    routes,
    gains,
    gains_first,
    gains_second,
    query_weight,
    query_first,
    query_second,
    key_matrix,
    key_moment_first,
    key_moment_second,
    value_matrix,
    value_moment_first,
    value_moment_second,
    output_weight,
    output_first,
    output_second,
    router_weight,
    router_first,
    router_second,
    expert_in,
    in_first,
    in_second,
    expert_out,
    out_first,
    out_second,
):
    token_rows, top_count = routes.shape
    shards = lax.axis_size("fsdp")
    place = lax.axis_index("fsdp")
    groups = lax.axis_size("expert")
    group = lax.axis_index("expert")
    depth = DEPTH
    wide = groups // depth
    level, column = group // wide, group % wide
    experts_local = expert_in.shape[0]
    experts_all = experts_local * groups
    near = wide * experts_local
    shard_rows = query_weight.shape[0]

    def z_shift(value, by):
        return lax.ppermute(
            value,
            "expert",
            [(a * wide + b, (a + by) % depth * wide + b) for a in range(depth) for b in range(wide)],
        )

    def x_shift(value, by):
        return lax.ppermute(
            value,
            "expert",
            [(a * wide + b, a * wide + (b + by) % wide) for a in range(depth) for b in range(wide)],
        )

    def back_shift(value, by):
        pairs = [(a, a + by) for a in range(shards) if 0 <= a + by < shards]
        return lax.ppermute(value, "fsdp", pairs)

    chips = shards // 2
    chip, core = place // 2, place % 2
    core_arg = core.astype(jnp.int32).reshape(1)

    def core_shift(value, by):
        return lax.ppermute(value, "fsdp", [(a, a // 2 * 2 + (a + by) % 2) for a in range(shards)])

    def y_shift(value, by):
        return lax.ppermute(value, "fsdp", [(a, (a + 2 * by) % shards) for a in range(shards)])

    def y_up(value, by):
        return lax.ppermute(value, "fsdp", [(a, a + 2 * by) for a in range(shards - 2 * by)])

    small = jnp.concatenate(
        [
            router_weight.astype(bf16),
            gains.T.astype(bf16),
            jnp.zeros((shard_rows, 128 - experts_all - 2), bf16),
        ],
        axis=1,
    )
    front_low = lax.all_gather(
        jnp.concatenate(
            [query_weight.astype(bf16), key_matrix.astype(bf16), value_matrix.astype(bf16), small], axis=1
        ),
        "fsdp",
        axis=0,
        tiled=True,
    )
    output_low = lax.all_gather(output_weight.astype(bf16), "fsdp", axis=0, tiled=True)
    qkv_low = front_low[:, :QKV]
    router_low = front_low[:, QKV : QKV + experts_all]
    gain_pair = front_low[:, QKV + experts_all : QKV + experts_all + 2].astype(f32).T
    gain_one, gain_two = gain_pair[0], gain_pair[1]

    routes_t = routes.T
    routes_of = jnp.stack([routes_t] + [z_shift(routes_t, i) for i in range(1, depth)])

    def expert_ids(at_level):
        columns = (column + jnp.arange(wide, dtype=jnp.int32)) % wide
        first_ids = (at_level * wide + columns) * experts_local
        return (first_ids[:, None] + jnp.arange(experts_local, dtype=jnp.int32)[None, :]).reshape(near)

    named = (routes_of[:, None] == expert_ids(level)[None, :, None, None]).astype(f32)
    chosen_here = jnp.sum(named, axis=2)
    earlier = (
        jnp.arange(token_rows, dtype=jnp.int32)[:, None] < jnp.arange(token_rows, dtype=jnp.int32)[None, :]
    ).astype(bf16)
    slots = dot_nn(chosen_here.reshape(depth * near, token_rows).astype(bf16), earlier).reshape(
        depth, near, token_rows
    )
    code = jnp.where(chosen_here > 0, slots.astype(jnp.int32), -1)
    picks = code[:, :, None, :] == jnp.arange(CAP, dtype=jnp.int32)[None, None, :, None]
    picks_low = picks.astype(bf16).reshape(depth, near * CAP, token_rows)

    def pick(rows, k):
        return pick_rows(picks_low, k, rows, wide)

    def swap(picked, *before):
        own, away = picked
        pairs = [own]
        for r in range(1, wide):
            pairs.append(x_shift(after(away[r - 1], pairs[1:], before), r))
        return pairs

    def order(swapped):
        return [swapped[k][r] for r in range(wide) for k in range(depth)]

    def swap_back(pieces, *before):
        steps = [None] * depth
        for m in range(depth):
            k = (m + 1) % depth
            steps[k] = [pieces[k]]
            for r in range(1, wide):
                piece = x_shift(after(pieces[r * depth + k], before), -r)
                steps[k].append(piece)
                if m % 2 == 0:
                    before = (piece,)
        return steps

    def chip_sum(mine, mate, chip):
        return lax.dynamic_index_in_dim(mine, chip, 0, keepdims=False).astype(
            f32
        ) + lax.dynamic_index_in_dim(mate, chip, 0, keepdims=False).astype(f32)

    def chip_low(mine, mate):
        return [chip_sum(mine, mate, (chip + s) % chips).astype(bf16) for s in range(1, chips)]

    def chip_send(low):
        return [y_shift(part, s) for s, part in enumerate(low, 1)]

    def chip_total(mine, mate, sent):
        return functools.reduce(lambda total, part: total + part.astype(f32), sent, chip_sum(mine, mate, chip))

    def ring_send(held):
        return [z_shift(held[-1], 1)]

    def ring_step(held, pieces, arrived=()):
        m = len(held)
        out = ring_rows(picks_low, (m + 1) % depth, pieces, arrived, m == depth - 1)
        if m == depth - 1:
            return out
        held.append(out)

    upstream = cotangent.astype(f32)
    level_one = z_shift(cotangent, 1)
    upstream_swapped = [swap(pick(cotangent, 0))]
    level_one = after(level_one, upstream_swapped)
    picked = pick(level_one, 1)
    upstream_swapped.append(swap(picked, upstream_swapped[-1]))

    inputs = tokens.astype(f32)
    scale_one = lax.rsqrt(jnp.mean(inputs * inputs, axis=1, keepdims=True) + NORM_EPS)
    normed_one = inputs * scale_one
    first_hidden = (normed_one * gain_one).astype(bf16)
    inverse = ROPE_BASE ** (-(jnp.arange(HEAD_SIZE // 2, dtype=f32) * 2.0 / HEAD_SIZE))
    places = (place * token_rows + jnp.arange(token_rows, dtype=jnp.int32)).astype(f32)
    angles = places[:, None] * inverse[None, :]
    half_cos, half_sin = jnp.cos(angles), jnp.sin(angles)
    cosine = jnp.concatenate([half_cos, half_cos], axis=1)
    sine = jnp.concatenate([-half_sin, half_sin], axis=1)

    def turn_keys(rows, sign):
        parts = []
        for h in range(KEY_VALUE_HEADS):
            piece = rows[:, h * HEAD_SIZE : (h + 1) * HEAD_SIZE]
            swapped = jnp.concatenate([piece[:, HEAD_SIZE // 2 :], piece[:, : HEAD_SIZE // 2]], axis=1)
            parts.append(piece * cosine + swapped * (sign * sine))
        return jnp.concatenate(parts, axis=1)

    pre = dot_nn(after(first_hidden, picked), qkv_low)
    keys_local = turn_keys(pre[:, MODEL_WIDTH : MODEL_WIDTH + KV], 1.0).astype(bf16)
    kv_local = jnp.concatenate([keys_local, pre[:, MODEL_WIDTH + KV :].astype(bf16)], axis=1)

    same = [kv_local] + [y_up(kv_local, s) for s in range(1, chips)]
    other = [core_shift(v, 1) for v in same]
    blocks = []
    for distance in range(shards):
        s = distance // 2
        if distance % 2 == 0:
            blocks.append(same[s])
        elif s + 1 < chips:
            blocks.append(jnp.where(core == 1, other[s], other[s + 1]))
        else:
            blocks.append(other[s])
    kv_blocks = jnp.stack(blocks)

    down_low = lax.all_gather(after(expert_out, kv_local).astype(bf16), "fsdp", axis=0)
    gate_up_low = lax.all_gather(after(expert_in, kv_local).astype(bf16), "fsdp", axis=0)

    level_two = after(z_shift(level_one, 1), kv_blocks)
    level_three = z_shift(level_two, 1)

    place_arg = place.astype(jnp.int32).reshape(1)
    attended, log_total, query_rows = attend(
        place_arg, pre, cosine, sine, after(kv_blocks, level_two)
    )
    residual = inputs + dot_nn(after(attended, level_three), output_low)
    scale_two = lax.rsqrt(jnp.mean(residual * residual, axis=1, keepdims=True) + NORM_EPS)
    normed_two = residual * scale_two
    hidden_two = (normed_two * gain_two).astype(bf16)

    upstream_swapped[1] = after(upstream_swapped[1], attended)
    upstream_swapped.append(swap(pick(after(level_two, attended), 2), upstream_swapped[1]))
    last_picked = pick(after(level_three, hidden_two), 3)

    levels = [hidden_two, z_shift(hidden_two, 1)]
    logits_t = lax.dot_general(
        router_low, hidden_two, (((0,), (1,)), ((), ())), preferred_element_type=f32
    )
    all_ids = jnp.arange(experts_all, dtype=jnp.int32)
    chosen_t = (routes_t[:, None, :] == all_ids[None, :, None]).astype(f32)
    gate_weights = jax.nn.softmax(jnp.sum(chosen_t * logits_t[None], axis=1), axis=0)
    gates_of = [gate_weights, z_shift(gate_weights, 1)]
    picked = pick(hidden_two, 0)
    hidden_swapped = [swap(picked, upstream_swapped[-1])]
    levels[1] = after(levels[1], picked)
    picked = pick(levels[1], 1)
    hidden_swapped.append(swap(picked, hidden_swapped[-1]))
    upstream_swapped.append(swap(last_picked, hidden_swapped[-1]))
    for k in range(2, depth):
        levels.append(after(z_shift(levels[-1], 1), picked, gates_of[1]))
        if k == depth - 1:
            upstream_pieces = order(after(upstream_swapped, levels[k - 1]))
            inner = inner_rows(upstream_pieces, down_low)
            gates_of[-1] = after(gates_of[-1], inner)
            levels[k] = after(levels[k], gates_of[-1])
        gates_of.append(z_shift(gates_of[-1], 1))
        picked = pick(levels[k], k)
        hidden_swapped.append(swap(picked, hidden_swapped[-1], upstream_swapped[-1]))
    gates_near = jnp.sum(named * jnp.stack(gates_of)[:, None], axis=2)
    row_gates = jnp.sum(jnp.where(picks, gates_near[:, :, None, :], 0.0), axis=3)
    row_gates = row_gates.reshape(depth, wide, experts_local, CAP)
    away_gates = [x_shift(row_gates[:, r], r) for r in range(1, wide)]
    hidden_swapped, away_gates = after((hidden_swapped, away_gates), levels[-1])
    hidden_pieces = order(hidden_swapped)
    row_gates = jnp.stack([row_gates[:, 0]] + away_gates)
    row_gates = row_gates.transpose(2, 0, 1, 3).reshape(experts_local, wide * depth * CAP, 1)

    scaled_hidden, gate_side, up_side, gate_dots, back_pieces = core_rows(
        hidden_pieces, gate_up_low, inner, row_gates
    )
    steps = swap_back(back_pieces)
    gate_dots = gate_dots.reshape(experts_local, wide, depth, CAP)
    away_dots = [x_shift(gate_dots[:, r], -r) for r in range(1, wide)]
    down_term = down_grads(upstream_pieces, scaled_hidden, shards)
    held = []
    ring_step(held, after(steps[1], down_term))
    out_part = lax.psum_scatter(after(down_term, held[0]), "fsdp", scatter_dimension=0)
    arrived = ring_send(held)
    in_term = in_grads(hidden_pieces, *after((gate_side, up_side), held[0]), shards)
    gate_dots = jnp.stack([gate_dots[:, 0]] + after(away_dots, in_term))
    gate_dots = gate_dots.transpose(2, 0, 1, 3).reshape(depth, near, CAP)
    token_dots = jnp.sum(jnp.where(picks, gate_dots[:, :, :, None], 0.0), axis=2)
    choice_dots = jnp.sum(named * token_dots[:, :, None, :], axis=1)
    lane = z_shift(choice_dots[1], 1)
    ring_step(held, after(steps[2], in_term, lane), arrived)
    in_part = lax.psum_scatter(after(in_term, held[1]), "fsdp", scatter_dimension=0)
    lane = z_shift(lane + choice_dots[2], 1)
    arrived = ring_send(held)
    results = result_rows(after(scaled_hidden, held[1]), down_low, len(back_pieces))
    ring_step(held, after(steps[3], results, lane), arrived)
    result_steps = swap_back(results, steps[0])
    lane = z_shift(lane + choice_dots[3], 1)
    arrived = ring_send(held)
    gate_grad = lane + choice_dots[0]
    picked_grad = gate_weights * (
        gate_grad - jnp.sum(gate_weights * gate_grad, axis=0, keepdims=True)
    )
    logit_grad_t = jnp.sum(chosen_t * picked_grad[:, None, :], axis=0).astype(bf16)
    router_term = dot_nn(logit_grad_t, hidden_two)
    hidden_back = ring_step(held, after(steps[0], router_term), arrived)
    hidden_two_grad = hidden_back + lax.dot_general(
        logit_grad_t, router_low, (((0,), (1,)), ((), ())), preferred_element_type=f32
    )

    gain_two_term = jnp.sum(hidden_two_grad * normed_two, axis=0)
    scaled_two = hidden_two_grad * gain_two
    residual_grad = upstream + scale_two * (
        scaled_two - normed_two * jnp.mean(scaled_two * normed_two, axis=1, keepdims=True)
    )
    branch_grad = residual_grad.astype(bf16)
    attended_grad = dot_nt(branch_grad, output_low).astype(bf16)
    result_held = []
    ring_step(result_held, after(result_steps[1], hidden_back))
    attended_grad = after(attended_grad, result_held[0], out_part)
    arrived = ring_send(result_held)
    pre_grad, key_back, value_back = attend_back(
        place_arg, query_rows, kv_blocks, attended, attended_grad, log_total, cosine, sine
    )

    def send_parts(parts, index, shift):
        count = parts.shape[0]
        return [lax.dynamic_index_in_dim(parts, index, 0, keepdims=False)] + [
            shift(lax.dynamic_index_in_dim(parts, (index + s) % count, 0, keepdims=False), s)
            for s in range(1, count)
        ]

    def add_parts(parts):
        return functools.reduce(lambda total, part: total + part.astype(f32), parts[1:], parts[0].astype(f32)).astype(bf16)

    def join(part, index, count, shift):
        whole = jnp.zeros((count,) + part.shape, part.dtype)
        for s in range(count):
            piece = shift(part, s) if s else part
            whole = lax.dynamic_update_index_in_dim(whole, piece, (index - s) % count, 0)
        return whole

    def x_parts(part):
        return send_parts(part.reshape(wide, shard_rows // wide, part.shape[1]), column, x_shift)

    def z_parts(part):
        return send_parts(part.reshape(depth, shard_rows // wide // depth, part.shape[1]), level, z_shift)

    def z_join(part):
        return join(part, level, depth, z_shift).reshape(shard_rows // wide, part.shape[1])

    def x_join(part):
        return join(part, column, wide, x_shift).reshape(shard_rows, part.shape[1]).astype(f32)

    kv_back = jnp.concatenate([key_back, value_back], axis=2)
    none = jnp.zeros_like(kv_back[:1])
    mate = jnp.where(core == 1, kv_back[1::2], jnp.concatenate([none, kv_back[1:-1:2]], axis=0))
    mate = core_shift(mate, 1)
    kv_chip = kv_back[0::2].astype(f32) + mate.astype(f32)
    kv_low = kv_chip.astype(bf16)
    kv_parts = [
        lax.ppermute(kv_low[s], "fsdp", [(a + 2 * s, a) for a in range(shards - 2 * s)]) for s in range(1, chips)
    ]
    back_mine, back_mate = core_grads(core_arg, attended, [after(branch_grad, kv_chip)], shards)
    back_mate = core_shift(back_mate, 1)
    out_state = adamw_update(
        expert_out,
        out_first,
        out_second,
        after(out_part, back_mine).astype(f32),
        0.5 / math.sqrt(FF // 8),
        DECAY,
    )
    ring_step(result_held, after(result_steps[2], out_state), arrived)
    arrived = ring_send(result_held)
    kv_parts = after(kv_parts, result_held[1])
    kv_grad = functools.reduce(lambda total, part: total + part.astype(f32), kv_parts, kv_chip[0])
    key_pre_grad = turn_keys(kv_grad[:, :KV], -1.0)
    kv_pre_grad = jnp.concatenate([key_pre_grad, kv_grad[:, KV:]], axis=1).astype(bf16)

    front_terms = weight_grads(first_hidden, [pre_grad, kv_pre_grad])
    front_part = lax.psum_scatter(front_terms, "fsdp", scatter_dimension=0, tiled=True)
    pre_late, kv_late = after((pre_grad, kv_pre_grad), front_terms)
    hidden_one_grad = dot_nt(pre_late, qkv_low[:, :MODEL_WIDTH]) + dot_nt(kv_late, qkv_low[:, MODEL_WIDTH:])
    gain_one_term = jnp.sum(hidden_one_grad * normed_one, axis=0)
    scaled_one = hidden_one_grad * gain_one
    input_grad = (
        residual_grad
        + scale_one
        * (scaled_one - normed_one * jnp.mean(scaled_one * normed_one, axis=1, keepdims=True))
    ).astype(bf16)
    extra = jnp.concatenate(
        [
            router_term,
            gain_one_term[None],
            gain_two_term[None],
            jnp.zeros((126 - experts_all, MODEL_WIDTH), f32),
        ],
        axis=0,
    )
    extra = extra.T.astype(bf16).reshape(chips, 2, shard_rows, 128)
    extra_mine = jnp.where(core == 0, extra[:, 0], extra[:, 1])
    extra_mate = core_shift(jnp.where(core == 0, extra[:, 1], extra[:, 0]), 1)
    back_mine = jnp.concatenate([back_mine, extra_mine], axis=2)
    back_mate = jnp.concatenate([back_mate, extra_mate], axis=2)
    back_low = chip_low(back_mine, back_mate)
    back_sent = chip_send(back_low)
    ring_step(result_held, after(result_steps[3], back_low), arrived)
    arrived = ring_send(result_held)
    in_state = adamw_update(
        expert_in,
        in_first,
        in_second,
        after(in_part, result_held[2]).astype(f32),
        0.5 / math.sqrt(MODEL_WIDTH),
        DECAY,
    )
    moe_out = ring_step(result_held, after(result_steps[0], in_state), arrived)
    layer_out = (residual + moe_out).astype(bf16)
    back_sent = after(back_sent, moe_out)
    back_part = chip_total(back_mine, back_mate, back_sent).astype(bf16)
    part = jnp.concatenate([front_part, back_part], axis=1)
    part = add_parts(x_parts(part))
    part = add_parts(z_parts(part))
    total = x_join(z_join(part))
    front_sum, back_sum = total[:, :QKV], total[:, QKV:]
    output_sum = back_sum[:, :MODEL_WIDTH]
    router_sum = back_sum[:, MODEL_WIDTH : MODEL_WIDTH + experts_all]
    query_sum = front_sum[:, :MODEL_WIDTH]
    key_sum = front_sum[:, MODEL_WIDTH : MODEL_WIDTH + KV]
    value_sum = front_sum[:, MODEL_WIDTH + KV : QKV]
    at = MODEL_WIDTH + experts_all
    gain_sum = back_sum[:, at : at + 2].T

    rate = 0.5 / math.sqrt(MODEL_WIDTH // 2)
    return (
        layer_out,
        input_grad,
        *adamw_update(gains, gains_first, gains_second, gain_sum, GAIN_RATE, 0.0),
        *adamw_update(query_weight, query_first, query_second, query_sum, rate, DECAY),
        *adamw_update(key_matrix, key_moment_first, key_moment_second, key_sum, rate, DECAY),
        *adamw_update(
            value_matrix,
            value_moment_first,
            value_moment_second,
            value_sum,
            0.5 / math.sqrt(MODEL_WIDTH),
            DECAY,
        ),
        *adamw_update(
            output_weight, output_first, output_second, output_sum, 0.5 / math.sqrt(MODEL_WIDTH // 32), DECAY
        ),
        *adamw_update(
            router_weight, router_first, router_second, router_sum, 0.5 / math.sqrt(4 * MODEL_WIDTH), DECAY
        ),
        *in_state,
        *out_state,
    )


def solution(mesh):
    rows = P(("expert", "fsdp"), None)
    gains = P(None, "fsdp")
    matrix = P("fsdp", None)
    wide = P("expert", "fsdp", None)
    tall = P("expert", None, "fsdp")
    return jax.shard_map(
        body,
        mesh=mesh,
        in_specs=(rows,) * 3 + (gains,) * 3 + (matrix,) * 15 + (wide,) * 3 + (tall,) * 3,
        out_specs=(rows,) * 2 + (gains,) * 3 + (matrix,) * 15 + (wide,) * 3 + (tall,) * 3,
        check_vma=False,
    )
```

```python
import functools
import math

import jax
import jax.numpy as jnp
from jax import lax
from jax.experimental import pallas as pl
from jax.experimental.pallas import tpu as pltpu
from jax.sharding import PartitionSpec as P

MODEL_WIDTH = 1536
QUERY_HEADS = 12
KEY_VALUE_HEADS = 2
HEAD_SIZE = 128
GROUP = QUERY_HEADS // KEY_VALUE_HEADS
FF = 768
STEP = 10
CAP = 80
DEPTH = 4
HALF = MODEL_WIDTH // 2
KV = KEY_VALUE_HEADS * HEAD_SIZE
QKV = MODEL_WIDTH + 2 * KV


NORM_EPS = 1e-05
ROPE_BASE = 10000.0
BETA_ONE = 0.9
BETA_TWO = 0.95
ADAM_EPS = 1e-08
DECAY = 0.1
GAIN_RATE = 0.8
MASKED = -1e30
LOG2E = 1.0 / math.log(2.0)
SCORE_SCALE = 1.0 / math.sqrt(HEAD_SIZE)

f32 = jnp.float32
bf16 = jnp.bfloat16


def dot_nn(left, right):
    return lax.dot_general(left, right, (((1,), (0,)), ((), ())), preferred_element_type=f32)


def dot_nt(left, right):
    return lax.dot_general(left, right, (((1,), (1,)), ((), ())), preferred_element_type=f32)


def dot_tn(left, right):
    return lax.dot_general(left, right, (((0,), (0,)), ((), ())), preferred_element_type=f32)


def after(value, *others):
    return lax.optimization_barrier((value, others))[0]


def params(megabytes, axes):
    return pltpu.CompilerParams(
        vmem_limit_bytes=megabytes * 1024 * 1024, dimension_semantics=("arbitrary",) * axes
    )


def cost(flops, nbytes, trans=0):
    return pl.CostEstimate(flops=int(flops), bytes_accessed=int(nbytes), transcendentals=0)


def causal(score_t):
    key_place = lax.broadcasted_iota(jnp.int32, score_t.shape, 0)
    query_place = lax.broadcasted_iota(jnp.int32, score_t.shape, 1)
    return key_place <= query_place


def attend_kernel(place, pre, cosine, sine, keys, values, out, log_total, turned):
    rows = pre[...]
    query = rows * cosine[...] + pltpu.roll(rows, HEAD_SIZE // 2, 1) * sine[...]
    turned[...] = query.astype(bf16)
    query_t = query.T.astype(bf16)
    factor = SCORE_SCALE * LOG2E

    score = dot_nn(keys[0], query_t) * factor
    score = jnp.where(causal(score), score, MASKED)
    biggest = jnp.max(score, axis=0, keepdims=True)
    weight = jnp.exp2(score - biggest)
    total = jnp.sum(weight, axis=0, keepdims=True)
    acc = dot_nn(values[0].T, weight.astype(bf16))

    def step(back, carry):
        biggest, total, acc = carry
        score = dot_nn(keys[back], query_t) * factor
        larger = jnp.maximum(biggest, jnp.max(score, axis=0, keepdims=True))
        weight = jnp.exp2(score - larger)
        shrink = jnp.exp2(biggest - larger)
        total = total * shrink + jnp.sum(weight, axis=0, keepdims=True)
        acc = acc * shrink + dot_nn(values[back].T, weight.astype(bf16))
        return larger, total, acc

    biggest, total, acc = lax.fori_loop(1, place[0] + 1, step, (biggest, total, acc))
    out[...] = (acc / total).T.astype(bf16)
    log_total[0] = biggest + jnp.log(total) * LOG2E


def attend(place, pre, cosine, sine, kv_blocks):
    token_rows = pre.shape[0]
    blocks = kv_blocks.shape[0]
    width = (token_rows, HEAD_SIZE)
    many = (blocks, token_rows, HEAD_SIZE)
    return pl.pallas_call(
        attend_kernel,
        out_shape=(
            jax.ShapeDtypeStruct((token_rows, MODEL_WIDTH), bf16),
            jax.ShapeDtypeStruct((QUERY_HEADS, 1, token_rows), f32),
            jax.ShapeDtypeStruct((token_rows, MODEL_WIDTH), bf16),
        ),
        grid_spec=pltpu.PrefetchScalarGridSpec(
            num_scalar_prefetch=1,
            grid=(QUERY_HEADS,),
            in_specs=[
                pl.BlockSpec(width, lambda h, p: (0, h)),
                pl.BlockSpec(width, lambda h, p: (0, 0)),
                pl.BlockSpec(width, lambda h, p: (0, 0)),
                pl.BlockSpec(many, lambda h, p: (0, 0, h // GROUP)),
                pl.BlockSpec(many, lambda h, p: (0, 0, KEY_VALUE_HEADS + h // GROUP)),
            ],
            out_specs=(
                pl.BlockSpec(width, lambda h, p: (0, h)),
                pl.BlockSpec((1, 1, token_rows), lambda h, p: (h, 0, 0)),
                pl.BlockSpec(width, lambda h, p: (0, h)),
            ),
        ),
        compiler_params=params(56, 1),
        cost_estimate=cost(1e9, 1e6),
        name="attend",
    )(place, pre, cosine, sine, kv_blocks, kv_blocks)


def attend_back_kernel(
    place, query, keys, values, out, out_grad, log_total, cosine, sine, pre_grad, key_grad, value_grad, key_acc, value_acc
):
    head = pl.program_id(0)

    @pl.when(head % GROUP == 0)
    def _():
        key_acc[...] = jnp.zeros_like(key_acc)
        value_acc[...] = jnp.zeros_like(value_acc)

    factor = SCORE_SCALE * LOG2E
    query_rows = query[...]
    grad_rows = out_grad[...]
    query_t = query_rows.astype(f32).T.astype(bf16)
    grad_t32 = grad_rows.astype(f32).T
    grad_t = grad_t32.astype(bf16)
    row_dot = jnp.sum(out[...].astype(f32).T * grad_t32, axis=0, keepdims=True)
    level = log_total[0]

    def block(back, masked):
        key = keys[back]
        score = dot_nn(key, query_t) * factor - level
        weight = jnp.exp2(score)
        if masked:
            weight = jnp.where(causal(weight), weight, 0.0)
        value_acc[back] += dot_nn(weight.astype(bf16), grad_rows)
        prob_grad = dot_nn(values[back], grad_t)
        score_grad = (weight * (prob_grad - row_dot)).astype(bf16)
        key_acc[back] += dot_nn(score_grad, query_rows)
        return dot_nn(key.T, score_grad)

    query_grad = block(0, True)
    query_grad = lax.fori_loop(1, place[0] + 1, lambda b, acc: acc + block(b, False), query_grad)
    rows = query_grad.T * SCORE_SCALE
    pre_grad[...] = (rows * cosine[...] - pltpu.roll(rows, HEAD_SIZE // 2, 1) * sine[...]).astype(bf16)

    @pl.when(head % GROUP == GROUP - 1)
    def _():
        key_grad[...] = (key_acc[...] * SCORE_SCALE).astype(bf16)
        value_grad[...] = value_acc[...].astype(bf16)


def attend_back(place, query, kv_blocks, out, out_grad, log_total, cosine, sine):
    token_rows = query.shape[0]
    blocks = kv_blocks.shape[0]
    width = (token_rows, HEAD_SIZE)
    many = (blocks, token_rows, HEAD_SIZE)
    return pl.pallas_call(
        attend_back_kernel,
        out_shape=(
            jax.ShapeDtypeStruct((token_rows, MODEL_WIDTH), bf16),
            jax.ShapeDtypeStruct((blocks, token_rows, KV), bf16),
            jax.ShapeDtypeStruct((blocks, token_rows, KV), bf16),
        ),
        grid_spec=pltpu.PrefetchScalarGridSpec(
            num_scalar_prefetch=1,
            grid=(QUERY_HEADS,),
            in_specs=[
                pl.BlockSpec(width, lambda h, p: (0, h)),
                pl.BlockSpec(many, lambda h, p: (0, 0, h // GROUP)),
                pl.BlockSpec(many, lambda h, p: (0, 0, KEY_VALUE_HEADS + h // GROUP)),
                pl.BlockSpec(width, lambda h, p: (0, h)),
                pl.BlockSpec(width, lambda h, p: (0, h)),
                pl.BlockSpec((1, 1, token_rows), lambda h, p: (h, 0, 0)),
                pl.BlockSpec(width, lambda h, p: (0, 0)),
                pl.BlockSpec(width, lambda h, p: (0, 0)),
            ],
            out_specs=(
                pl.BlockSpec(width, lambda h, p: (0, h)),
                pl.BlockSpec(many, lambda h, p: (0, 0, h // GROUP)),
                pl.BlockSpec(many, lambda h, p: (0, 0, h // GROUP)),
            ),
            scratch_shapes=[pltpu.VMEM(many, f32), pltpu.VMEM(many, f32)],
        ),
        compiler_params=params(56, 1),
        cost_estimate=cost(1e9, 1e6),
        name="attend_back",
    )(place, query, kv_blocks, kv_blocks, out, out_grad, log_total, cosine, sine)


def gather_rows(pieces, rows):
    for p, piece in enumerate(pieces):
        rows[p * CAP : (p + 1) * CAP] = piece[...]


def scatter_rows(rows, pieces, at, span):
    low = rows.astype(bf16)
    for p, piece in enumerate(pieces):
        piece[:, at : at + span] = low[p * CAP : (p + 1) * CAP]


def piece_spec():
    return pl.BlockSpec((CAP, MODEL_WIDTH), lambda e, *_: (e, 0))


def row_scratch(count):
    return [pltpu.VMEM((count * CAP, MODEL_WIDTH), bf16)]


def inner_kernel(count, *refs):
    pieces, (down, inner, rows) = refs[:count], refs[count:]
    gather_rows(pieces, rows)
    shards, span = down.shape[0], down.shape[3]
    acc = None
    for c in range(shards):
        term = dot_nt(rows[:, c * span : (c + 1) * span], down[c, 0])
        acc = term if acc is None else acc + term
    inner[0] = acc.astype(bf16)


def inner_rows(pieces, down):
    shards, experts, _, span = down.shape
    rows = len(pieces) * CAP
    return pl.pallas_call(
        functools.partial(inner_kernel, len(pieces)),
        out_shape=jax.ShapeDtypeStruct((experts, rows, FF), bf16),
        grid=(experts,),
        in_specs=[piece_spec()] * len(pieces) + [pl.BlockSpec((shards, 1, FF, span), lambda e: (0, e, 0, 0))],
        out_specs=pl.BlockSpec((1, rows, FF), lambda e: (e, 0, 0)),
        scratch_shapes=row_scratch(len(pieces)),
        compiler_params=params(56, 1),
        cost_estimate=cost(2 * experts * rows * FF * MODEL_WIDTH, 20e6),
        name="inner_rows",
    )(*pieces, down)


def core_kernel(count, *refs):
    pieces, refs = refs[:count], refs[count:]
    gate_up, inner, weight, scaled, gate_side, up_side, gate_dots = refs[:7]
    back, (rows,) = refs[7 : 7 + count], refs[7 + count :]
    gather_rows(pieces, rows)
    span = gate_up.shape[2]
    tile = 256
    factor = weight[0]
    dots = None

    def product(at):
        return dot_nn(rows[...], gate_up[:, 0, :, at : at + tile].reshape(MODEL_WIDTH, tile))

    for n in range(FF // tile):
        at = n * tile
        gate_pre = product(at)
        up_part = product(FF + at)
        sigmoid = 1.0 / (1.0 + jnp.exp(-gate_pre))
        silu = gate_pre * sigmoid
        hidden = silu * up_part
        raw = inner[0, :, at : at + tile].astype(f32)
        part = jnp.sum(raw * hidden, axis=1, keepdims=True)
        dots = part if dots is None else dots + part
        scaled[0, :, at : at + tile] = (hidden * factor).astype(bf16)
        raw = raw * factor
        gate_side[0, :, at : at + tile] = (raw * up_part * (sigmoid + silu * (1.0 - sigmoid))).astype(bf16)
        up_side[0, :, at : at + tile] = (raw * silu).astype(bf16)
    gate_dots[0] = dots

    width = 384
    group = width // span
    for chunk in range(MODEL_WIDTH // width):
        block = gate_up[chunk * group : (chunk + 1) * group, 0].reshape(width, 2 * FF)
        grads = dot_nt(gate_side[0], block[:, :FF]) + dot_nt(up_side[0], block[:, FF:])
        scatter_rows(grads, back, chunk * width, width)


def core_rows(pieces, gate_up, inner, weight):
    count = len(pieces)
    shards, experts, span, _ = gate_up.shape
    rows = count * CAP
    whole = pl.BlockSpec((1, rows, FF), lambda e: (e, 0, 0))
    column = pl.BlockSpec((1, rows, 1), lambda e: (e, 0, 0))
    low = jax.ShapeDtypeStruct((experts, rows, FF), bf16)
    out = pl.pallas_call(
        functools.partial(core_kernel, count),
        out_shape=(low, low, low, jax.ShapeDtypeStruct((experts, rows, 1), f32))
        + (jax.ShapeDtypeStruct(pieces[0].shape, bf16),) * count,
        grid=(experts,),
        in_specs=[piece_spec()] * count
        + [pl.BlockSpec((shards, 1, span, 2 * FF), lambda e: (0, e, 0, 0)), whole, column],
        out_specs=(whole, whole, whole, column) + (piece_spec(),) * count,
        scratch_shapes=row_scratch(len(pieces)),
        compiler_params=params(60, 1),
        cost_estimate=cost(8 * experts * rows * FF * MODEL_WIDTH, 60e6),
        name="core_rows",
    )(*pieces, gate_up, inner, weight)
    return out[0], out[1], out[2], out[3], list(out[4:])


def result_kernel(scaled, down, *pieces):
    width = 384
    shards, span = down.shape[0], down.shape[3]
    group = width // span
    rows = scaled[0]
    for chunk in range(MODEL_WIDTH // width):
        parts = [down[c, 0] for c in range(chunk * group, (chunk + 1) * group)]
        block = parts[0] if group == 1 else jnp.concatenate(parts, axis=1)
        scatter_rows(dot_nn(rows, block), pieces, chunk * width, width)


def result_rows(scaled, down, count):
    experts, rows, _ = scaled.shape
    shards, _, _, span = down.shape
    return list(
        pl.pallas_call(
            result_kernel,
            out_shape=(jax.ShapeDtypeStruct((experts * CAP, MODEL_WIDTH), bf16),) * count,
            grid=(experts,),
            in_specs=[
                pl.BlockSpec((1, rows, FF), lambda e: (e, 0, 0)),
                pl.BlockSpec((shards, 1, FF, span), lambda e: (0, e, 0, 0)),
            ],
            out_specs=(piece_spec(),) * count,
            compiler_params=params(56, 1),
            cost_estimate=cost(2 * experts * rows * FF * MODEL_WIDTH, 22e6),
            name="result_rows",
        )(scaled, down)
    )


def down_grad_kernel(count, *refs):
    pieces, (scaled, out, rows) = refs[:count], refs[count:]
    gather_rows(pieces, rows)
    shards, span = out.shape[0], out.shape[3]
    scaled_t = scaled[0].T
    for c in range(shards):
        out[c, 0] = dot_nn(scaled_t, rows[:, c * span : (c + 1) * span]).astype(bf16)


def down_grads(pieces, scaled, shards):
    experts, rows, _ = scaled.shape
    span = MODEL_WIDTH // shards
    return pl.pallas_call(
        functools.partial(down_grad_kernel, len(pieces)),
        out_shape=jax.ShapeDtypeStruct((shards, experts, FF, span), bf16),
        grid=(experts,),
        in_specs=[piece_spec()] * len(pieces) + [pl.BlockSpec((1, rows, FF), lambda e: (e, 0, 0))],
        out_specs=pl.BlockSpec((shards, 1, FF, span), lambda e: (0, e, 0, 0)),
        scratch_shapes=row_scratch(len(pieces)),
        compiler_params=params(56, 1),
        cost_estimate=cost(2 * experts * rows * FF * MODEL_WIDTH, 22e6),
        name="down_grads",
    )(*pieces, scaled)


def in_grad_kernel(count, *refs):
    pieces, (gate_side, up_side, out, rows) = refs[:count], refs[count:]
    gather_rows(pieces, rows)
    shards, span = out.shape[0], out.shape[2]
    rows_t = rows[...].T
    for c in range(shards):
        part = rows_t[c * span : (c + 1) * span]
        out[c, 0, :, :FF] = dot_nn(part, gate_side[0]).astype(bf16)
        out[c, 0, :, FF:] = dot_nn(part, up_side[0]).astype(bf16)


def in_grads(pieces, gate_side, up_side, shards):
    experts, rows, _ = gate_side.shape
    span = MODEL_WIDTH // shards
    whole = pl.BlockSpec((1, rows, FF), lambda e: (e, 0, 0))
    return pl.pallas_call(
        functools.partial(in_grad_kernel, len(pieces)),
        out_shape=jax.ShapeDtypeStruct((shards, experts, span, 2 * FF), bf16),
        grid=(experts,),
        in_specs=[piece_spec()] * len(pieces) + [whole, whole],
        out_specs=pl.BlockSpec((shards, 1, span, 2 * FF), lambda e: (0, e, 0, 0)),
        scratch_shapes=row_scratch(len(pieces)),
        compiler_params=params(56, 1),
        cost_estimate=cost(4 * experts * rows * FF * MODEL_WIDTH, 35e6),
        name="in_grads",
    )(*pieces, gate_side, up_side)


def ring_kernel(wide, *refs):
    picks, pieces = refs[0], refs[1 : 1 + wide]
    arrived, out = refs[1 + wide : -1], refs[-1]
    rows = jnp.concatenate([piece[...] for piece in pieces], axis=0)
    total = dot_tn(picks[0], rows)
    if arrived:
        total = total + arrived[0][...].astype(f32)
    out[...] = total.astype(out.dtype)


def ring_rows(picks, level, pieces, arrived, last):
    _, many, token_rows = picks.shape
    tile = 512
    side = pl.BlockSpec((token_rows, tile), lambda n: (0, n))
    return pl.pallas_call(
        functools.partial(ring_kernel, len(pieces)),
        out_shape=jax.ShapeDtypeStruct((token_rows, MODEL_WIDTH), f32 if last else bf16),
        grid=(MODEL_WIDTH // tile,),
        in_specs=[pl.BlockSpec((1, many, token_rows), lambda n: (level, 0, 0))]
        + [pl.BlockSpec((p.shape[0], tile), lambda n: (0, n)) for p in pieces]
        + [side] * len(arrived),
        out_specs=side,
        compiler_params=params(48, 1),
        cost_estimate=cost(4 * many * token_rows * HALF, 8e6),
        name="ring_rows",
    )(picks, *pieces, *arrived)


def pick_kernel(picks, rows, own, away):
    per = own.shape[0]
    picked = dot_nn(picks[0], rows[...]).astype(bf16)
    own[...] = picked[:per]
    for r in range(away.shape[0]):
        away[r] = picked[(r + 1) * per : (r + 2) * per]


def pick_rows(picks, level, rows, wide):
    _, many, token_rows = picks.shape
    per = many // wide
    tile = 512
    return pl.pallas_call(
        pick_kernel,
        out_shape=(
            jax.ShapeDtypeStruct((per, MODEL_WIDTH), bf16),
            jax.ShapeDtypeStruct((wide - 1, per, MODEL_WIDTH), bf16),
        ),
        grid=(MODEL_WIDTH // tile,),
        in_specs=[
            pl.BlockSpec((1, many, token_rows), lambda n: (level, 0, 0)),
            pl.BlockSpec((token_rows, tile), lambda n: (0, n)),
        ],
        out_specs=(
            pl.BlockSpec((per, tile), lambda n: (0, n)),
            pl.BlockSpec((wide - 1, per, tile), lambda n: (0, 0, n)),
        ),
        compiler_params=params(32, 1),
        cost_estimate=cost(4 * many * token_rows * HALF, 5e6),
        name="pick_rows",
    )(picks, rows)


def weight_grad_kernel(rows, *refs):
    *grads, out = refs
    rows_t = rows[...].T
    at = 0
    for side in grads:
        if side.dtype == f32:
            out[:, at:] = side[...].T.astype(bf16)
        else:
            columns = side.shape[1]
            out[:, at : at + columns] = dot_nn(rows_t, side[...]).astype(bf16)
            at += columns


def weight_grads(rows, grads, extra=None):
    token_rows = rows.shape[0]
    tile = 384
    extras = [] if extra is None else [extra]
    columns = sum(g.shape[1] for g in grads) + sum(e.shape[0] for e in extras)
    return pl.pallas_call(
        weight_grad_kernel,
        out_shape=jax.ShapeDtypeStruct((MODEL_WIDTH, columns), bf16),
        grid=(MODEL_WIDTH // tile,),
        in_specs=[pl.BlockSpec((token_rows, tile), lambda n: (0, n))]
        + [pl.BlockSpec(g.shape, lambda n: (0, 0)) for g in grads]
        + [pl.BlockSpec((e.shape[0], tile), lambda n: (0, n)) for e in extras],
        out_specs=pl.BlockSpec((tile, columns), lambda n: (n, 0)),
        compiler_params=params(56, 1),
        cost_estimate=cost(2 * MODEL_WIDTH * token_rows * columns, 14e6),
        name="weight_grads",
    )(rows, *grads, *extras)


def keep_and_send(core, pair, mine, theirs):
    first, second = (p.astype(bf16) for p in pair)
    mine(jnp.where(core == 0, first, second))
    theirs(jnp.where(core == 0, second, first))


def core_grad_kernel(core, rows, *refs):
    *grads, mine, theirs = refs
    span = mine.shape[1]
    rows_t = rows[...].T
    at = 0
    for side in grads:
        columns = side.shape[1]
        pair = [dot_nn(rows_t[c * span : (c + 1) * span], side[...]) for c in range(2)]
        where = (0, slice(None), slice(at, at + columns))
        keep_and_send(
            core[0],
            pair,
            functools.partial(mine.__setitem__, where),
            functools.partial(theirs.__setitem__, where),
        )
        at += columns


def core_grads(core, rows, grads, shards):
    token_rows = rows.shape[0]
    span = MODEL_WIDTH // shards
    columns = sum(g.shape[1] for g in grads)
    out = jax.ShapeDtypeStruct((shards // 2, span, columns), bf16)
    block = pl.BlockSpec((1, span, columns), lambda n, c: (n, 0, 0))
    return pl.pallas_call(
        core_grad_kernel,
        out_shape=(out, out),
        grid_spec=pltpu.PrefetchScalarGridSpec(
            num_scalar_prefetch=1,
            grid=(shards // 2,),
            in_specs=[pl.BlockSpec((token_rows, 2 * span), lambda n, c: (0, n))]
            + [pl.BlockSpec(g.shape, lambda n, c: (0, 0)) for g in grads],
            out_specs=(block, block),
        ),
        compiler_params=params(56, 1),
        cost_estimate=cost(2 * MODEL_WIDTH * token_rows * columns, 14e6),
        name="core_grads",
    )(core, rows, *grads)


def adamw_update(weight, moment_one, moment_two, gradient, step_rate, decay_rate):
    first_new = BETA_ONE * moment_one + (1.0 - BETA_ONE) * gradient
    second_new = BETA_TWO * moment_two + (1.0 - BETA_TWO) * gradient * gradient
    first_hat = first_new / (1.0 - BETA_ONE**STEP)
    second_hat = second_new / (1.0 - BETA_TWO**STEP)
    weight_new = weight - step_rate * (
        first_hat / (jnp.sqrt(second_hat) + ADAM_EPS) + decay_rate * weight
    )
    return (weight_new, first_new, second_new)


def body(
    tokens,
    cotangent,
    routes,
    gains,
    gains_first,
    gains_second,
    query_weight,
    query_first,
    query_second,
    key_matrix,
    key_moment_first,
    key_moment_second,
    value_matrix,
    value_moment_first,
    value_moment_second,
    output_weight,
    output_first,
    output_second,
    router_weight,
    router_first,
    router_second,
    expert_in,
    in_first,
    in_second,
    expert_out,
    out_first,
    out_second,
):
    token_rows, top_count = routes.shape
    shards = lax.axis_size("fsdp")
    place = lax.axis_index("fsdp")
    groups = lax.axis_size("expert")
    group = lax.axis_index("expert")
    depth = DEPTH
    wide = groups // depth
    level, column = group // wide, group % wide
    experts_local = expert_in.shape[0]
    experts_all = experts_local * groups
    near = wide * experts_local
    shard_rows = query_weight.shape[0]

    def z_shift(value, by):
        return lax.ppermute(
            value,
            "expert",
            [(a * wide + b, (a + by) % depth * wide + b) for a in range(depth) for b in range(wide)],
        )

    def x_shift(value, by):
        return lax.ppermute(
            value,
            "expert",
            [(a * wide + b, a * wide + (b + by) % wide) for a in range(depth) for b in range(wide)],
        )

    def back_shift(value, by):
        pairs = [(a, a + by) for a in range(shards) if 0 <= a + by < shards]
        return lax.ppermute(value, "fsdp", pairs)

    chips = shards // 2
    chip, core = place // 2, place % 2
    core_arg = core.astype(jnp.int32).reshape(1)

    def core_shift(value, by):
        return lax.ppermute(value, "fsdp", [(a, a // 2 * 2 + (a + by) % 2) for a in range(shards)])

    def y_shift(value, by):
        return lax.ppermute(value, "fsdp", [(a, (a + 2 * by) % shards) for a in range(shards)])

    def y_up(value, by):
        return lax.ppermute(value, "fsdp", [(a, a + 2 * by) for a in range(shards - 2 * by)])

    small = jnp.concatenate(
        [
            router_weight.astype(bf16),
            gains.T.astype(bf16),
            jnp.zeros((shard_rows, 128 - experts_all - 2), bf16),
        ],
        axis=1,
    )
    front_low = lax.all_gather(
        jnp.concatenate(
            [query_weight.astype(bf16), key_matrix.astype(bf16), value_matrix.astype(bf16), small], axis=1
        ),
        "fsdp",
        axis=0,
        tiled=True,
    )
    output_low = lax.all_gather(output_weight.astype(bf16), "fsdp", axis=0, tiled=True)
    qkv_low = front_low[:, :QKV]
    router_low = front_low[:, QKV : QKV + experts_all]
    gain_pair = front_low[:, QKV + experts_all : QKV + experts_all + 2].astype(f32).T
    gain_one, gain_two = gain_pair[0], gain_pair[1]

    routes_t = routes.T
    routes_of = jnp.stack([routes_t] + [z_shift(routes_t, i) for i in range(1, depth)])

    def expert_ids(at_level):
        columns = (column + jnp.arange(wide, dtype=jnp.int32)) % wide
        first_ids = (at_level * wide + columns) * experts_local
        return (first_ids[:, None] + jnp.arange(experts_local, dtype=jnp.int32)[None, :]).reshape(near)

    named = (routes_of[:, None] == expert_ids(level)[None, :, None, None]).astype(f32)
    chosen_here = jnp.sum(named, axis=2)
    earlier = (
        jnp.arange(token_rows, dtype=jnp.int32)[:, None] < jnp.arange(token_rows, dtype=jnp.int32)[None, :]
    ).astype(bf16)
    slots = dot_nn(chosen_here.reshape(depth * near, token_rows).astype(bf16), earlier).reshape(
        depth, near, token_rows
    )
    code = jnp.where(chosen_here > 0, slots.astype(jnp.int32), -1)
    picks = code[:, :, None, :] == jnp.arange(CAP, dtype=jnp.int32)[None, None, :, None]
    picks_low = picks.astype(bf16).reshape(depth, near * CAP, token_rows)

    def pick(rows, k):
        return pick_rows(picks_low, k, rows, wide)

    def swap(picked, *before):
        own, away = picked
        pairs = [own]
        for r in range(1, wide):
            pairs.append(x_shift(after(away[r - 1], pairs[1:], before), r))
        return pairs

    def order(swapped):
        return [swapped[k][r] for r in range(wide) for k in range(depth)]

    def swap_back(pieces, *before):
        steps = [None] * depth
        for m in range(depth):
            k = (m + 1) % depth
            steps[k] = [pieces[k]]
            for r in range(1, wide):
                piece = x_shift(after(pieces[r * depth + k], before), -r)
                steps[k].append(piece)
                if m % 2 == 0:
                    before = (piece,)
        return steps

    def chip_sum(mine, mate, chip):
        return lax.dynamic_index_in_dim(mine, chip, 0, keepdims=False).astype(
            f32
        ) + lax.dynamic_index_in_dim(mate, chip, 0, keepdims=False).astype(f32)

    def chip_low(mine, mate):
        return [chip_sum(mine, mate, (chip + s) % chips).astype(bf16) for s in range(1, chips)]

    def chip_send(low):
        return [y_shift(part, s) for s, part in enumerate(low, 1)]

    def chip_total(mine, mate, sent):
        return functools.reduce(lambda total, part: total + part.astype(f32), sent, chip_sum(mine, mate, chip))

    def ring_send(held):
        return [z_shift(held[-1], 1)]

    def ring_step(held, pieces, arrived=()):
        m = len(held)
        out = ring_rows(picks_low, (m + 1) % depth, pieces, arrived, m == depth - 1)
        if m == depth - 1:
            return out
        held.append(out)

    upstream = cotangent.astype(f32)
    level_one = z_shift(cotangent, 1)
    upstream_swapped = [swap(pick(cotangent, 0))]
    level_one = after(level_one, upstream_swapped)
    picked = pick(level_one, 1)
    upstream_swapped.append(swap(picked, upstream_swapped[-1]))

    inputs = tokens.astype(f32)
    scale_one = lax.rsqrt(jnp.mean(inputs * inputs, axis=1, keepdims=True) + NORM_EPS)
    normed_one = inputs * scale_one
    first_hidden = (normed_one * gain_one).astype(bf16)
    inverse = ROPE_BASE ** (-(jnp.arange(HEAD_SIZE // 2, dtype=f32) * 2.0 / HEAD_SIZE))
    places = (place * token_rows + jnp.arange(token_rows, dtype=jnp.int32)).astype(f32)
    angles = places[:, None] * inverse[None, :]
    half_cos, half_sin = jnp.cos(angles), jnp.sin(angles)
    cosine = jnp.concatenate([half_cos, half_cos], axis=1)
    sine = jnp.concatenate([-half_sin, half_sin], axis=1)

    def turn_keys(rows, sign):
        parts = []
        for h in range(KEY_VALUE_HEADS):
            piece = rows[:, h * HEAD_SIZE : (h + 1) * HEAD_SIZE]
            swapped = jnp.concatenate([piece[:, HEAD_SIZE // 2 :], piece[:, : HEAD_SIZE // 2]], axis=1)
            parts.append(piece * cosine + swapped * (sign * sine))
        return jnp.concatenate(parts, axis=1)

    pre = dot_nn(after(first_hidden, picked), qkv_low)
    keys_local = turn_keys(pre[:, MODEL_WIDTH : MODEL_WIDTH + KV], 1.0).astype(bf16)
    kv_local = jnp.concatenate([keys_local, pre[:, MODEL_WIDTH + KV :].astype(bf16)], axis=1)

    same = [kv_local] + [y_up(kv_local, s) for s in range(1, chips)]
    other = [core_shift(v, 1) for v in same]
    blocks = []
    for distance in range(shards):
        s = distance // 2
        if distance % 2 == 0:
            blocks.append(same[s])
        elif s + 1 < chips:
            blocks.append(jnp.where(core == 1, other[s], other[s + 1]))
        else:
            blocks.append(other[s])
    kv_blocks = jnp.stack(blocks)

    down_low = lax.all_gather(after(expert_out, kv_local).astype(bf16), "fsdp", axis=0)
    gate_up_low = lax.all_gather(after(expert_in, kv_local).astype(bf16), "fsdp", axis=0)

    level_two = after(z_shift(level_one, 1), kv_blocks)
    level_three = z_shift(level_two, 1)

    place_arg = place.astype(jnp.int32).reshape(1)
    attended, log_total, query_rows = attend(
        place_arg, pre, cosine, sine, after(kv_blocks, level_two)
    )
    residual = inputs + dot_nn(after(attended, level_three), output_low)
    scale_two = lax.rsqrt(jnp.mean(residual * residual, axis=1, keepdims=True) + NORM_EPS)
    normed_two = residual * scale_two
    hidden_two = (normed_two * gain_two).astype(bf16)

    upstream_swapped[1] = after(upstream_swapped[1], attended)
    upstream_swapped.append(swap(pick(after(level_two, attended), 2), upstream_swapped[1]))
    last_picked = pick(after(level_three, hidden_two), 3)

    levels = [hidden_two, z_shift(hidden_two, 1)]
    logits_t = lax.dot_general(
        router_low, hidden_two, (((0,), (1,)), ((), ())), preferred_element_type=f32
    )
    all_ids = jnp.arange(experts_all, dtype=jnp.int32)
    chosen_t = (routes_t[:, None, :] == all_ids[None, :, None]).astype(f32)
    gate_weights = jax.nn.softmax(jnp.sum(chosen_t * logits_t[None], axis=1), axis=0)
    gates_of = [gate_weights, z_shift(gate_weights, 1)]
    picked = pick(hidden_two, 0)
    hidden_swapped = [swap(picked, upstream_swapped[-1])]
    levels[1] = after(levels[1], picked)
    picked = pick(levels[1], 1)
    hidden_swapped.append(swap(picked, hidden_swapped[-1]))
    upstream_swapped.append(swap(last_picked, hidden_swapped[-1]))
    for k in range(2, depth):
        levels.append(after(z_shift(levels[-1], 1), picked, gates_of[1]))
        if k == depth - 1:
            upstream_pieces = order(after(upstream_swapped, levels[k - 1]))
            inner = inner_rows(upstream_pieces, down_low)
            gates_of[-1] = after(gates_of[-1], inner)
            levels[k] = after(levels[k], gates_of[-1])
        gates_of.append(z_shift(gates_of[-1], 1))
        picked = pick(levels[k], k)
        hidden_swapped.append(swap(picked, hidden_swapped[-1], upstream_swapped[-1]))
    gates_near = jnp.sum(named * jnp.stack(gates_of)[:, None], axis=2)
    row_gates = jnp.sum(jnp.where(picks, gates_near[:, :, None, :], 0.0), axis=3)
    row_gates = row_gates.reshape(depth, wide, experts_local, CAP)
    away_gates = [x_shift(row_gates[:, r], r) for r in range(1, wide)]
    hidden_swapped, away_gates = after((hidden_swapped, away_gates), levels[-1])
    hidden_pieces = order(hidden_swapped)
    row_gates = jnp.stack([row_gates[:, 0]] + away_gates)
    row_gates = row_gates.transpose(2, 0, 1, 3).reshape(experts_local, wide * depth * CAP, 1)

    scaled_hidden, gate_side, up_side, gate_dots, back_pieces = core_rows(
        hidden_pieces, gate_up_low, inner, row_gates
    )
    steps = swap_back(back_pieces)
    gate_dots = gate_dots.reshape(experts_local, wide, depth, CAP)
    away_dots = [x_shift(gate_dots[:, r], -r) for r in range(1, wide)]
    down_term = down_grads(upstream_pieces, scaled_hidden, shards)
    held = []
    ring_step(held, after(steps[1], down_term))
    out_part = lax.psum_scatter(after(down_term, held[0]), "fsdp", scatter_dimension=0)
    arrived = ring_send(held)
    in_term = in_grads(hidden_pieces, *after((gate_side, up_side), held[0]), shards)
    gate_dots = jnp.stack([gate_dots[:, 0]] + after(away_dots, in_term))
    gate_dots = gate_dots.transpose(2, 0, 1, 3).reshape(depth, near, CAP)
    token_dots = jnp.sum(jnp.where(picks, gate_dots[:, :, :, None], 0.0), axis=2)
    choice_dots = jnp.sum(named * token_dots[:, :, None, :], axis=1)
    lane = z_shift(choice_dots[1], 1)
    ring_step(held, after(steps[2], in_term, lane), arrived)
    in_part = lax.psum_scatter(after(in_term, held[1]), "fsdp", scatter_dimension=0)
    lane = z_shift(lane + choice_dots[2], 1)
    arrived = ring_send(held)
    results = result_rows(after(scaled_hidden, held[1]), down_low, len(back_pieces))
    ring_step(held, after(steps[3], results, lane), arrived)
    result_steps = swap_back(results, steps[0])
    lane = z_shift(lane + choice_dots[3], 1)
    arrived = ring_send(held)
    gate_grad = lane + choice_dots[0]
    picked_grad = gate_weights * (
        gate_grad - jnp.sum(gate_weights * gate_grad, axis=0, keepdims=True)
    )
    logit_grad_t = jnp.sum(chosen_t * picked_grad[:, None, :], axis=0).astype(bf16)
    router_term = dot_nn(logit_grad_t, hidden_two)
    hidden_back = ring_step(held, after(steps[0], router_term), arrived)
    hidden_two_grad = hidden_back + lax.dot_general(
        logit_grad_t, router_low, (((0,), (1,)), ((), ())), preferred_element_type=f32
    )

    gain_two_term = jnp.sum(hidden_two_grad * normed_two, axis=0)
    scaled_two = hidden_two_grad * gain_two
    residual_grad = upstream + scale_two * (
        scaled_two - normed_two * jnp.mean(scaled_two * normed_two, axis=1, keepdims=True)
    )
    branch_grad = residual_grad.astype(bf16)
    attended_grad = dot_nt(branch_grad, output_low).astype(bf16)
    result_held = []
    ring_step(result_held, after(result_steps[1], hidden_back))
    attended_grad = after(attended_grad, result_held[0], out_part)
    arrived = ring_send(result_held)
    pre_grad, key_back, value_back = attend_back(
        place_arg, query_rows, kv_blocks, attended, attended_grad, log_total, cosine, sine
    )

    def send_parts(parts, index, shift):
        count = parts.shape[0]
        return [lax.dynamic_index_in_dim(parts, index, 0, keepdims=False)] + [
            shift(lax.dynamic_index_in_dim(parts, (index + s) % count, 0, keepdims=False), s)
            for s in range(1, count)
        ]

    def add_parts(parts):
        return functools.reduce(lambda total, part: total + part.astype(f32), parts[1:], parts[0].astype(f32)).astype(bf16)

    def join(part, index, count, shift):
        whole = jnp.zeros((count,) + part.shape, part.dtype)
        for s in range(count):
            piece = shift(part, s) if s else part
            whole = lax.dynamic_update_index_in_dim(whole, piece, (index - s) % count, 0)
        return whole

    def x_parts(part):
        return send_parts(part.reshape(wide, shard_rows // wide, part.shape[1]), column, x_shift)

    def z_parts(part):
        return send_parts(part.reshape(depth, shard_rows // wide // depth, part.shape[1]), level, z_shift)

    def z_join(part):
        return join(part, level, depth, z_shift).reshape(shard_rows // wide, part.shape[1])

    def x_join(part):
        return join(part, column, wide, x_shift).reshape(shard_rows, part.shape[1]).astype(f32)

    kv_back = jnp.concatenate([key_back, value_back], axis=2)
    none = jnp.zeros_like(kv_back[:1])
    mate = jnp.where(core == 1, kv_back[1::2], jnp.concatenate([none, kv_back[1:-1:2]], axis=0))
    mate = core_shift(mate, 1)
    kv_chip = kv_back[0::2].astype(f32) + mate.astype(f32)
    kv_low = kv_chip.astype(bf16)
    kv_parts = [
        lax.ppermute(kv_low[s], "fsdp", [(a + 2 * s, a) for a in range(shards - 2 * s)]) for s in range(1, chips)
    ]
    back_mine, back_mate = core_grads(core_arg, attended, [after(branch_grad, kv_chip)], shards)
    back_mate = core_shift(back_mate, 1)
    out_state = adamw_update(
        expert_out,
        out_first,
        out_second,
        after(out_part, back_mine).astype(f32),
        0.5 / math.sqrt(FF // 8),
        DECAY,
    )
    ring_step(result_held, after(result_steps[2], out_state), arrived)
    arrived = ring_send(result_held)
    kv_parts = after(kv_parts, result_held[1])
    kv_grad = functools.reduce(lambda total, part: total + part.astype(f32), kv_parts, kv_chip[0])
    key_pre_grad = turn_keys(kv_grad[:, :KV], -1.0)
    kv_pre_grad = jnp.concatenate([key_pre_grad, kv_grad[:, KV:]], axis=1).astype(bf16)

    front_terms = weight_grads(first_hidden, [pre_grad, kv_pre_grad])
    front_part = lax.psum_scatter(front_terms, "fsdp", scatter_dimension=0, tiled=True)
    pre_late, kv_late = after((pre_grad, kv_pre_grad), front_terms)
    hidden_one_grad = dot_nt(pre_late, qkv_low[:, :MODEL_WIDTH]) + dot_nt(kv_late, qkv_low[:, MODEL_WIDTH:])
    gain_one_term = jnp.sum(hidden_one_grad * normed_one, axis=0)
    scaled_one = hidden_one_grad * gain_one
    input_grad = (
        residual_grad
        + scale_one
        * (scaled_one - normed_one * jnp.mean(scaled_one * normed_one, axis=1, keepdims=True))
    ).astype(bf16)
    extra = jnp.concatenate(
        [
            router_term,
            gain_one_term[None],
            gain_two_term[None],
            jnp.zeros((126 - experts_all, MODEL_WIDTH), f32),
        ],
        axis=0,
    )
    extra = extra.T.astype(bf16).reshape(chips, 2, shard_rows, 128)
    extra_mine = jnp.where(core == 0, extra[:, 0], extra[:, 1])
    extra_mate = core_shift(jnp.where(core == 0, extra[:, 1], extra[:, 0]), 1)
    ring_step(result_held, after(result_steps[3], extra_mine), arrived)
    arrived = ring_send(result_held)
    back_mate, extra_mate = after((back_mate, extra_mate), result_held[2])
    back_mine = jnp.concatenate([back_mine, extra_mine], axis=2)
    back_mate = jnp.concatenate([back_mate, extra_mate], axis=2)
    back_low = chip_low(back_mine, back_mate)
    back_sent = chip_send(back_low)
    in_state = adamw_update(
        expert_in,
        in_first,
        in_second,
        after(in_part, back_low).astype(f32),
        0.5 / math.sqrt(MODEL_WIDTH),
        DECAY,
    )
    moe_out = ring_step(result_held, after(result_steps[0], in_state), arrived)
    layer_out = (residual + moe_out).astype(bf16)
    back_sent = after(back_sent, moe_out)
    back_parts = x_parts(chip_total(back_mine, back_mate, back_sent).astype(bf16))
    back_parts = z_parts(add_parts(back_parts))
    back_low = add_parts(back_parts)
    front_low = after(front_part, moe_out)
    front_parts = x_parts(front_low)
    back_low = z_join(after(back_low, front_low))
    front_low = add_parts(front_parts)
    front_low = add_parts(z_parts(front_low))
    back_sum = x_join(after(back_low, front_low))
    front_sum = x_join(z_join(front_low))
    output_sum = back_sum[:, :MODEL_WIDTH]
    router_sum = back_sum[:, MODEL_WIDTH : MODEL_WIDTH + experts_all]
    query_sum = front_sum[:, :MODEL_WIDTH]
    key_sum = front_sum[:, MODEL_WIDTH : MODEL_WIDTH + KV]
    value_sum = front_sum[:, MODEL_WIDTH + KV : QKV]
    at = MODEL_WIDTH + experts_all
    gain_sum = back_sum[:, at : at + 2].T

    rate = 0.5 / math.sqrt(MODEL_WIDTH // 2)
    return (
        layer_out,
        input_grad,
        *adamw_update(gains, gains_first, gains_second, gain_sum, GAIN_RATE, 0.0),
        *adamw_update(query_weight, query_first, query_second, query_sum, rate, DECAY),
        *adamw_update(key_matrix, key_moment_first, key_moment_second, key_sum, rate, DECAY),
        *adamw_update(
            value_matrix,
            value_moment_first,
            value_moment_second,
            value_sum,
            0.5 / math.sqrt(MODEL_WIDTH),
            DECAY,
        ),
        *adamw_update(
            output_weight, output_first, output_second, output_sum, 0.5 / math.sqrt(MODEL_WIDTH // 32), DECAY
        ),
        *adamw_update(
            router_weight, router_first, router_second, router_sum, 0.5 / math.sqrt(4 * MODEL_WIDTH), DECAY
        ),
        *in_state,
        *out_state,
    )


def solution(mesh):
    rows = P(("expert", "fsdp"), None)
    gains = P(None, "fsdp")
    matrix = P("fsdp", None)
    wide = P("expert", "fsdp", None)
    tall = P("expert", None, "fsdp")
    return jax.shard_map(
        body,
        mesh=mesh,
        in_specs=(rows,) * 3 + (gains,) * 3 + (matrix,) * 15 + (wide,) * 3 + (tall,) * 3,
        out_specs=(rows,) * 2 + (gains,) * 3 + (matrix,) * 15 + (wide,) * 3 + (tall,) * 3,
        check_vma=False,
    )
```
